32 devices in a mesh: cube: 8 (over y, x, core), blk: 4 (over z).
Axes of the slice: x: 2, y: 2, z: 4, core: 2. Of those that a mesh axis runs over, the one named last changes fastest.
Arguments:
- inputs: bfloat16 [8, 1728, 768], P('cube', 'blk'), may hold values from -6 to 6
- cotangent: bfloat16 [8, 1728, 768], P('cube', 'blk'), may hold values from -6 to 6
- absent_groups: int32 [8, 12], P('cube'), may hold values from 0 to 1, as said below
- token_group: int32 [8, 1728], P('cube', 'blk'), may hold values from 0 to 11, as said below
- pre_gain: float32 [768], replicated, may hold values from 0.25 to 1.75
- pre_shift: float32 [768], replicated, may hold values from -3 to 3
- input_weight: bfloat16 [768, 2304], replicated, may hold values from -0.3125 to 0.3125
- input_bias: float32 [2, 768], replicated, may hold values from -3 to 3
- output_weight: bfloat16 [768, 768], replicated, may hold values from -1.75 to 1.75
- output_bias: float32 [768], replicated, may hold values from -2 to 2
- mid_gain: float32 [768], replicated, may hold values from 0.25 to 1.75
- mid_shift: float32 [768], replicated, may hold values from -3 to 3
- up_weight: bfloat16 [768, 3072], replicated, may hold values from -0.21875 to 0.21875
- up_bias: float32 [3072], replicated, may hold values from -3 to 3
- down_weight: bfloat16 [3072, 768], replicated, may hold values from -0.109375 to 0.109375
- down_bias: float32 [768], replicated, may hold values from -2 to 2
Outputs:
- layer_out: bfloat16 [8, 1728, 768], P('cube', 'blk')
- input_grad: float32 [8, 1728, 768], P('cube', 'blk')
- grad_pre_gain: float32 [768], replicated
- grad_pre_shift: float32 [768], replicated
- grad_input_weight: float32 [768, 2304], replicated
- grad_input_bias: float32 [2, 768], replicated
- grad_output_weight: float32 [768, 768], replicated
- grad_output_bias: float32 [768], replicated
- grad_mid_gain: float32 [768], replicated
- grad_mid_shift: float32 [768], replicated
- grad_up_weight: float32 [768, 3072], replicated
- grad_up_bias: float32 [3072], replicated
- grad_down_weight: float32 [3072, 768], replicated
- grad_down_bias: float32 [768], replicated
The draws below stay inside these ranges and needn't reach their ends.
Inputs may be any that keep to these rules, and one draw needn't show every extreme that they name: `absent_groups`: each cube lacks between 1 and 3 of its 12 band groups; 1 marks a lacking group. `token_group`: each cube's positions form 12 runs of consecutive positions, position t lying in run t * 12 // 1728; each run belongs to a different group.
All inputs are finite; a program needn't handle non-finite values.
Results may differ from the reference program's by a relative error of at most 0.015.
Values may be sent and summed in bfloat16 or wider, within the bound.
No kernel may reach another device: no remote copies, remote signals or barrier semaphores. Data moves between devices by JAX's collectives and lax.ppermute only.
A program may use at most 192 MiB of HBM per device.

```python
import jax
import jax.numpy as jnp
from jax import lax

D = 768
HEADS = 12
HD = 64
FF = 3072
SEQ = 1728
GROUPS = 12
CUBES = 8


def draw_absent_groups(key, part):
    key = jax.random.fold_in(key, 11)
    count_key, order_key = jax.random.split(key)
    lacking = jax.random.randint(count_key, (CUBES, 1), 1, 4)
    scores = jax.random.randint(order_key, (CUBES, GROUPS), 0, 1 << 20) * GROUPS + jnp.arange(GROUPS, dtype=jnp.int32)[None, :]
    ordering = jnp.argsort(scores, axis=1, stable=True)
    rank_of = jnp.argsort(ordering, axis=1, stable=True)
    return (rank_of < lacking).astype(jnp.int32)


def draw_token_group(key, part):
    key = jax.random.fold_in(key, 23)
    scores = jax.random.randint(key, (CUBES, GROUPS), 0, 1 << 20) * GROUPS + jnp.arange(GROUPS, dtype=jnp.int32)[None, :]
    ordering = jnp.argsort(scores, axis=1, stable=True).astype(jnp.int32)
    run_of = jnp.arange(SEQ, dtype=jnp.int32) * GROUPS // SEQ
    return jnp.take_along_axis(ordering, jnp.broadcast_to(run_of[None, :], (CUBES, SEQ)), axis=1).astype(jnp.int32)


def levels(stream_key, dims, cuts, least, largest):
    loudness = 1.0
    for position, blocks in cuts:
        heights = jax.random.uniform(jax.random.fold_in(jax.random.fold_in(stream_key, 6), position), (blocks,), jnp.float32, least / len(cuts), largest / len(cuts))
        loudness = loudness * jnp.repeat(jnp.exp(heights), dims[position] // blocks).reshape((-1,) + (1,) * (len(dims) - 1 - position))
    return loudness


def noise(key, dims, deviation, reach, shards=(), kind=jnp.bfloat16):
    drawn = jax.random.normal(key, dims, jnp.float32) * deviation
    if len(shards) > 0:
        drawn = levels(key, dims, shards, -0.22, 0.18) * drawn
    return jnp.clip(drawn, min=-reach, max=reach).astype(kind)


def setup_inputs(seed: int = 0) -> dict:
    splits = jax.random.split(jax.random.key(seed), 17)
    return {
        "inputs": noise(splits[0], (CUBES, SEQ, D), 1.0, 6.0, ((0, 8), (1, 4))),
        "cotangent": noise(splits[1], (CUBES, SEQ, D), 1.0, 6.0, ((0, 8), (1, 4))),
        "absent_groups": draw_absent_groups(jax.random.fold_in(splits[16], 71), 0),
        "token_group": draw_token_group(jax.random.fold_in(splits[16], 71), 0),
        "pre_gain": jnp.clip(1.0 + 0.15 * jax.random.normal(splits[4], (D,), jnp.float32), 0.25, 1.75),
        "pre_shift": noise(splits[5], (D,), 0.5, 3.0, (), jnp.float32),
        "input_weight": noise(splits[6], (D, 3 * D), (D // 2) ** -0.5, 0.3125),
        "input_bias": noise(splits[7], (2, D), 0.5, 3.0, (), jnp.float32),
        "output_weight": noise(splits[8], (D, D), (max(D // 64, 2)) ** -0.5, 1.75),
        "output_bias": noise(splits[9], (D,), 0.3, 2.0, (), jnp.float32),
        "mid_gain": jnp.clip(1.0 + 0.15 * jax.random.normal(splits[10], (D,), jnp.float32), 0.25, 1.75),
        "mid_shift": noise(splits[11], (D,), 0.5, 3.0, (), jnp.float32),
        "up_weight": noise(splits[12], (D, FF), D ** -0.5, 0.21875),
        "up_bias": noise(splits[13], (FF,), 0.5, 3.0, (), jnp.float32),
        "down_weight": noise(splits[14], (FF, D), FF ** -0.5, 0.109375),
        "down_bias": noise(splits[15], (D,), 0.3, 2.0, (), jnp.float32),
    }


NEG_FILL = -32768.0
EPSILON = 1e-06

@jax.custom_vjp
def low(v):
    return lax.optimization_barrier(v.astype(jnp.bfloat16)).astype(jnp.float32)

@jax.custom_vjp
def low_back(v):
    return v

def low_keep(v):
    return (low(v), None)

def low_pass(kept, grad):
    return (grad,)

def back_keep(v):
    return (v, None)

def back_low(kept, grad):
    return (low(grad),)
low.defvjp(low_keep, low_pass)
low_back.defvjp(back_keep, back_low)

def layer_norm(values, gain_vec, shift_vec):
    centered = values - lax.optimization_barrier(jnp.mean(values, axis=-1, keepdims=True))
    normed = centered * lax.rsqrt(lax.optimization_barrier(jnp.mean(centered * centered, axis=-1, keepdims=True)) + EPSILON)
    return normed * gain_vec + shift_vec

def matmul_high(left_side, right_side):
    return jnp.dot(left_side, right_side, precision=lax.Precision.HIGHEST, preferred_element_type=jnp.float32)

def forward(params, inputs, valid_rows, key_bias):
    pre_gain, pre_shift, input_weight, input_bias, output_weight, output_bias, mid_gain, mid_shift, up_weight, up_bias, down_weight, down_bias = params
    normed = low(layer_norm(inputs, pre_gain, pre_shift))
    projected = matmul_high(normed, input_weight)
    queries = low(low_back(projected[:, :D] + input_bias[0]))
    key_rows = low(low_back(projected[:, D:2 * D]))
    value_rows = low(low_back(projected[:, 2 * D:] + input_bias[1]))
    query_heads = queries.reshape(SEQ, HEADS, HD)
    key_heads = key_rows.reshape(SEQ, HEADS, HD)
    value_heads = value_rows.reshape(SEQ, HEADS, HD)
    raw_scores = jnp.einsum('qhd,khd->hqk', query_heads, key_heads, precision=lax.Precision.HIGHEST)
    scores = low_back(raw_scores * HD ** (-0.5) + key_bias[None, None, :])
    row_peak = lax.optimization_barrier(jnp.max(scores, axis=2, keepdims=True))
    exp_scores = jnp.exp(scores - row_peak)
    probs_low = low(exp_scores / lax.optimization_barrier(jnp.sum(exp_scores, axis=2, keepdims=True)))
    mixed = jnp.einsum('hqk,khd->qhd', probs_low, value_heads, precision=lax.Precision.HIGHEST)
    attended = low(low_back(mixed.reshape(SEQ, D)))
    hidden = inputs + low_back(matmul_high(attended, output_weight) + output_bias)
    normed_mid = low(layer_norm(hidden, mid_gain, mid_shift))
    gate_pre = low_back(matmul_high(normed_mid, up_weight) + up_bias)
    activated = low(jax.nn.gelu(gate_pre, approximate=False))
    result = hidden + low_back(matmul_high(activated, down_weight) + down_bias)
    return valid_rows[:, None] * result

def reference(inputs, cotangent, absent_groups, token_group, pre_gain, pre_shift, input_weight, input_bias, output_weight, output_bias, mid_gain, mid_shift, up_weight, up_bias, down_weight, down_bias):
    params = tuple((array.astype(jnp.float32) for array in (pre_gain, pre_shift, input_weight, input_bias, output_weight, output_bias, mid_gain, mid_shift, up_weight, up_bias, down_weight, down_bias)))

    def one_cube(totals, pieces):
        cube_in, cube_cot, cube_absent, cube_group = pieces
        group_match = cube_group[:, None] == jnp.arange(GROUPS, dtype=jnp.int32)[None, :]
        lacking = lax.optimization_barrier(jnp.sum(jnp.where(group_match, cube_absent[None, :], 0), axis=1))
        valid_rows = (1 - lacking).astype(jnp.float32)
        key_bias = NEG_FILL * (1.0 - valid_rows)

        def layer_fn(param_set, cube_rows):
            return forward(param_set, cube_rows, valid_rows, key_bias)
        result, pullback = jax.vjp(layer_fn, params, cube_in.astype(jnp.float32))
        grad_set, grad_rows = pullback(cube_cot.astype(jnp.float32))
        totals = jax.tree.map(lambda first, second: first + second, totals, grad_set)
        return (totals, (result.astype(jnp.bfloat16), grad_rows))
    start_totals = jax.tree.map(jnp.zeros_like, params)
    totals, (outputs, grad_inputs) = lax.scan(one_cube, start_totals, (inputs, cotangent, absent_groups, token_group))
    return (outputs, grad_inputs, totals[0], totals[1], totals[2], totals[3], totals[4], totals[5], totals[6], totals[7], totals[8], totals[9], totals[10], totals[11])
```

```python
import jax
import jax.numpy as jnp
from jax import lax
from jax.sharding import PartitionSpec as P

HEADS = 12
HD = 64
GROUPS = 12
MEMBERS = 4
LOCAL_HEADS = HEADS // MEMBERS
WIDTH = LOCAL_HEADS * HD

NEG_FILL = -32768.0
EPSILON = 1e-06
BF16 = jnp.bfloat16
F32 = jnp.float32


def over_cube(value, bit):
    count = lax.axis_size("cube")
    return lax.ppermute(value, "cube", [(i, i ^ (1 << bit)) for i in range(count)])


def over_blk(value, bit):
    return lax.ppermute(value, "blk", [(i, i ^ (1 << bit)) for i in range(MEMBERS)])


def chosen_pairs(is_home, cube_flip, blk_flip):
    pairs = []
    for c in range(lax.axis_size("cube")):
        for b in range(MEMBERS):
            if ((c & 1) == (b >> 1)) == is_home:
                pairs.append((c * MEMBERS + b, (c ^ cube_flip) * MEMBERS + (b ^ blk_flip)))
    return pairs


def sent_between(value, is_home, cube_flip, blk_flip):
    return lax.ppermute(value, ("cube", "blk"), chosen_pairs(is_home, cube_flip, blk_flip))


def exchanged(parts):
    far = over_blk(parts[3], 0)
    near = over_blk(parts[1], 0)
    core = over_cube(parts[2], 0)
    return [parts[0], near, core, over_cube(far, 0)]


def half_of(rows, which, axis=0):
    size = rows.shape[axis] // 2
    return lax.dynamic_slice_in_dim(rows, which * size, size, axis)


def added(first, second):
    return (first.astype(F32) + second.astype(F32)).astype(BF16)


def halved(rows, flag, send, axis=0):
    got = send(half_of(rows, 1 - flag, axis))
    return added(half_of(rows, flag, axis), got)


def joined(own, got, flag, axis=0):
    return jnp.where(
        flag == 0,
        jnp.concatenate([own, got], axis),
        jnp.concatenate([got, own], axis),
    )


def cube_bits():
    return list(range(1, lax.axis_size("cube").bit_length() - 1))


def flag_of(index, bit):
    return (index >> bit) & 1


def reduced_over_planes(first, second, cube):
    bits = cube_bits()
    for one, two in zip(bits, reversed(bits)):
        first = halved(first, flag_of(cube, one), lambda v, s=one: over_cube(v, s))
        second = halved(second, flag_of(cube, two), lambda v, s=two: over_cube(v, s))
    return first, second


def gathered_over_planes(first, second, cube, axis=0):
    bits = cube_bits()
    for one, two in zip(reversed(bits), bits):
        first = joined(first, over_cube(first, one), flag_of(cube, one), axis)
        second = joined(second, over_cube(second, two), flag_of(cube, two), axis)
    return first, second


def summed_everywhere(keep, send, cube, blk):
    half = added(keep, over_cube(send, 0))
    size = half.shape[0] // 2
    first, second = reduced_over_planes(half[:size], half[size:], cube)
    both = jnp.stack([first, second])
    both = halved(both, flag_of(blk, 0), lambda v: over_blk(v, 0), 1)
    both = halved(both, flag_of(blk, 1), lambda v: over_blk(v, 1), 1)
    both = joined(both, over_blk(both, 1), flag_of(blk, 1), 1)
    both = joined(both, over_blk(both, 0), flag_of(blk, 0), 1)
    first, second = gathered_over_planes(both[0], both[1], cube)
    got_first, got_second = over_cube(first, 0), over_cube(second, 0)
    mine = jnp.concatenate([first, second])
    other = jnp.concatenate([got_first, got_second])
    flag = cube & 1
    return jnp.where(flag == 0, mine, other), jnp.where(flag == 0, other, mine)


def layer_norm(values, gain_vec, shift_vec):
    centered = values - jnp.mean(values, axis=-1, keepdims=True)
    normed = centered * lax.rsqrt(jnp.mean(centered * centered, axis=-1, keepdims=True) + EPSILON)
    return normed * gain_vec + shift_vec


def gelu_exact(values):
    return jax.nn.gelu(values, approximate=False)


def matmul_rows(left_side, right_side):
    return jnp.dot(left_side, right_side, preferred_element_type=F32)


def matmul_back(left_side, right_side):
    return jnp.einsum("rf,df->rd", left_side, right_side, preferred_element_type=F32)


def weight_grad(left_side, right_side):
    return jnp.einsum("rd,rf->df", left_side, right_side, preferred_element_type=F32)


def column_sums(low_rows):
    return jnp.sum(low_rows, axis=0, dtype=F32)


def member_columns(matrix, member, axis):
    return lax.dynamic_slice_in_dim(matrix, member * WIDTH, WIDTH, axis)


def body(
    inputs,
    cotangent,
    absent_groups,
    token_group,
    pre_gain,
    pre_shift,
    input_weight,
    input_bias,
    output_weight,
    output_bias,
    mid_gain,
    mid_shift,
    up_weight,
    up_bias,
    down_weight,
    down_bias,
):
    _, rows, model = inputs.shape
    hidden_units = up_weight.shape[1]
    head_scale = HD ** (-0.5)
    cube, blk = lax.axis_index("cube"), lax.axis_index("blk")
    core = cube & 1
    at_home = core == (blk >> 1)
    member = 2 * core + (blk & 1)

    def moved(value):
        return jnp.where(at_home, value, sent_between(value, False, 1, 2))

    def from_group(value):
        value_moved = sent_between(value, False, 1, 2)
        near_home = sent_between(value, True, 0, 1)
        own = jnp.where(at_home, value, value_moved)
        near = jnp.where(at_home, near_home, sent_between(value_moved, False, 0, 1))
        return [own, near, over_cube(own, 0), over_cube(near, 0)]

    group_match = token_group[0][:, None] == jnp.arange(GROUPS, dtype=jnp.int32)[None, :]
    lacking = jnp.sum(jnp.where(group_match, absent_groups, 0), axis=1)
    valid_here = (1 - lacking).astype(BF16)[None, :]
    x_blocks = from_group(inputs[0])
    valid_blocks = from_group(valid_here)
    cot_own = moved(cotangent[0])
    x_all = jnp.concatenate(x_blocks).astype(F32)
    valid_all = jnp.concatenate(valid_blocks, axis=1)[0].astype(F32)
    key_bias = NEG_FILL * (1.0 - valid_all)
    residual_in = x_blocks[0].astype(F32)

    in_columns = jnp.concatenate(
        [member_columns(input_weight[:, s * model : (s + 1) * model], member, 1) for s in range(3)],
        axis=1,
    )
    bias_columns = member_columns(input_bias, member, 1)
    out_rows = [member_columns(output_weight, member ^ e, 0) for e in range(MEMBERS)]

    normed_low = layer_norm(x_all, pre_gain, pre_shift).astype(BF16)
    projected = matmul_rows(normed_low, in_columns)
    total_rows = projected.shape[0]
    heads_shape = (total_rows, LOCAL_HEADS, HD)
    query = (projected[:, :WIDTH] + bias_columns[0]).astype(BF16).reshape(heads_shape)
    key = projected[:, WIDTH : 2 * WIDTH].astype(BF16).reshape(heads_shape)
    value = (projected[:, 2 * WIDTH :] + bias_columns[1]).astype(BF16).reshape(heads_shape)

    def scores():
        raw = jnp.einsum("qhd,khd->hqk", query, key, preferred_element_type=F32)
        return raw * head_scale + key_bias

    peak = jnp.max(scores(), axis=2)
    weights = jnp.exp(scores() - peak[..., None])
    total = jnp.sum(weights, axis=2)
    attended_heads = (
        jnp.einsum("hqk,khd->hqd", weights.astype(BF16), value, preferred_element_type=F32)
        / total[..., None]
    )
    log_total = peak + jnp.log(total)
    attended_own = (
        jnp.transpose(attended_heads, (1, 0, 2)).reshape(MEMBERS, rows, WIDTH).astype(BF16)
    )
    attended = exchanged([attended_own[d] for d in range(MEMBERS)])

    hidden = residual_in + output_bias
    for part, weight_part in zip(attended, out_rows):
        hidden = hidden + matmul_rows(part, weight_part)
    normed_mid, mid_back = jax.vjp(layer_norm, hidden, mid_gain, mid_shift)
    normed_mid_low = normed_mid.astype(BF16)
    gate_pre = matmul_rows(normed_mid_low, up_weight) + up_bias
    activated, gelu_back = jax.vjp(gelu_exact, gate_pre)
    activated_low = activated.astype(BF16)
    result = hidden + matmul_rows(activated_low, down_weight) + down_bias
    valid_own = valid_all[:rows, None]
    layer_out = moved((valid_own * result).astype(BF16))
    grad_out = valid_own * cot_own.astype(F32)
    grad_down_low = grad_out.astype(BF16)
    grad_down_bias = column_sums(grad_down_low)
    (grad_gate,) = gelu_back(matmul_back(grad_down_low, down_weight))
    grad_gate_low = grad_gate.astype(BF16)

    down_halves = [
        weight_grad(half_of(activated_low, side, 1), grad_down_low).astype(BF16)
        for side in (core, 1 - core)
    ]
    grad_up_bias = column_sums(grad_gate_low)
    grad_mid, grad_mid_gain, grad_mid_shift = mid_back(matmul_back(grad_gate_low, up_weight))
    grad_hidden = grad_out + grad_mid
    grad_branch_low = grad_hidden.astype(BF16)
    grad_output_bias = column_sums(grad_branch_low)
    grad_attended = exchanged([matmul_back(grad_branch_low, part).astype(BF16) for part in out_rows])

    blocks = hidden_units // model

    def up_half(side):
        gate_half = half_of(grad_gate_low, side, 1)
        return [
            weight_grad(normed_mid_low, gate_half[:, s * model : (s + 1) * model]).astype(BF16)
            for s in range(blocks // 2)
        ]

    def out_half(side):
        parts = []
        for which in range(MEMBERS // 2):
            away = (2 * side + which) ^ member
            rows_here = lax.dynamic_index_in_dim(jnp.stack(attended), away, 0, keepdims=False)
            parts.append(weight_grad(rows_here, grad_branch_low).astype(BF16))
        return parts

    rest_halves = [jnp.concatenate(up_half(side) + out_half(side)) for side in (core, 1 - core)]
    down_sum = summed_everywhere(down_halves[0], down_halves[1], cube, blk)
    rest_sum = summed_everywhere(rest_halves[0], rest_halves[1], cube, blk)
    grad_down_weight = jnp.concatenate(down_sum).astype(F32)
    up_rows = blocks // 2 * model
    grad_up_weight = jnp.concatenate(
        [
            half[s * model : (s + 1) * model]
            for half in rest_sum
            for s in range(blocks // 2)
        ],
        axis=1,
    ).astype(F32)
    grad_output_weight = jnp.concatenate([half[up_rows:] for half in rest_sum]).astype(F32)

    grad_rows = jnp.concatenate(grad_attended).reshape(heads_shape)
    row_delta = jnp.einsum("qhd,hqd->hq", grad_rows.astype(F32), attended_heads)
    probs = jnp.exp(scores() - log_total[..., None])
    grad_probs = jnp.einsum("qhd,khd->hqk", grad_rows, value, preferred_element_type=F32)
    grad_scores = (probs * (grad_probs - row_delta[..., None])).astype(BF16)
    grad_query = jnp.einsum("hqk,khd->qhd", grad_scores, key, preferred_element_type=F32)
    grad_key = jnp.einsum("hqk,qhd->khd", grad_scores, query, preferred_element_type=F32)
    grad_value = jnp.einsum("hqk,qhd->khd", probs.astype(BF16), grad_rows, preferred_element_type=F32)
    grad_columns = jnp.concatenate(
        [
            (grad_query * head_scale).astype(BF16).reshape(total_rows, WIDTH),
            (grad_key * head_scale).astype(BF16).reshape(total_rows, WIDTH),
            grad_value.astype(BF16).reshape(total_rows, WIDTH),
        ],
        axis=1,
    )
    grad_in = weight_grad(normed_low, grad_columns)
    column_total = column_sums(grad_columns)

    partial = matmul_back(grad_columns, in_columns).astype(BF16).reshape(MEMBERS, rows, model)
    near_sum = added(partial[1], over_cube(partial[3], 0))
    own_sum = partial[0].astype(F32) + over_cube(partial[2], 0).astype(F32)
    grad_normed = own_sum + over_blk(near_sum, 0).astype(F32)
    _, pre_back = jax.vjp(layer_norm, residual_in, pre_gain, pre_shift)
    grad_pre, grad_pre_gain, grad_pre_shift = pre_back(grad_normed)
    grad_here = grad_hidden + grad_pre
    input_grad = jnp.where(
        at_home, grad_here, sent_between(grad_here.astype(BF16), False, 1, 2).astype(F32)
    )

    in_low = grad_in.astype(BF16)
    size = model // 2
    first, second = reduced_over_planes(in_low[:size], in_low[size:], cube)
    both = halved(jnp.stack([first, second]), flag_of(blk, 1), lambda v: over_blk(v, 1), 1)
    both = joined(both, over_blk(both, 1), flag_of(blk, 1), 1)
    both = jnp.stack([both, over_blk(both, 0)], axis=1)
    first, second = gathered_over_planes(both[0], both[1], cube, 1)
    mine = jnp.concatenate([first, second], axis=1)
    other = over_cube(mine, 0)
    pair = [mine[0], mine[1], other[0], other[1]]
    low_flag, high_flag = member & 1, member >> 1
    pair = [jnp.where(low_flag == 0, pair[e], pair[e ^ 1]) for e in range(MEMBERS)]
    pair = [jnp.where(high_flag == 0, pair[e], pair[e ^ 2]) for e in range(MEMBERS)]
    grad_input_weight = jnp.concatenate(
        [
            part[:, s * WIDTH : (s + 1) * WIDTH]
            for s in range(3)
            for part in pair
        ],
        axis=1,
    ).astype(F32)

    here_bias = jnp.stack([column_total[:WIDTH], column_total[2 * WIDTH :]])
    spread_bias = lax.dynamic_update_slice_in_dim(
        jnp.zeros((2, model), F32), here_bias, member * WIDTH, 1
    )
    vectors = jnp.concatenate(
        [
            jnp.stack(
                [
                    grad_pre_gain,
                    grad_pre_shift,
                    grad_output_bias,
                    grad_mid_gain,
                    grad_mid_shift,
                    grad_down_bias,
                ]
            ),
            spread_bias,
            grad_up_bias.reshape(blocks, model),
        ]
    )
    vectors = lax.psum(vectors, ("cube", "blk"))
    return (
        layer_out[None],
        input_grad[None],
        vectors[0],
        vectors[1],
        grad_input_weight,
        vectors[6:8],
        grad_output_weight,
        vectors[2],
        vectors[3],
        vectors[4],
        grad_up_weight,
        vectors[8:].reshape(-1),
        grad_down_weight,
        vectors[5],
    )


def solution(mesh):
    rows_spec = P("cube", "blk", None)
    return jax.shard_map(
        body,
        mesh=mesh,
        in_specs=(rows_spec, rows_spec, P("cube", None), P("cube", "blk")) + (P(),) * 12,
        out_specs=(rows_spec, rows_spec) + (P(),) * 12,
        check_vma=False,
    )
```

```python
import functools
import jax
import jax.numpy as jnp
from jax import lax
from jax.experimental import pallas as pl
from jax.experimental.pallas import tpu as pltpu
from jax.sharding import PartitionSpec as P

HEADS = 12
HD = 64
GROUPS = 12
MEMBERS = 4
LOCAL_HEADS = HEADS // MEMBERS
WIDTH = LOCAL_HEADS * HD
NEG_FILL = -32768.0
EPSILON = 1e-06
BF16 = jnp.bfloat16
F32 = jnp.float32
TILE = 256
LANES = 128
VMEM = pltpu.VMEM


def dot(left, right):
    return jnp.dot(left, right, preferred_element_type=F32)


def dot_nt(left, right):
    return lax.dot_general(left, right, (((1,), (1,)), ((), ())), preferred_element_type=F32)


def dot_tn(left, right):
    return lax.dot_general(left, right, (((0,), (0,)), ((), ())), preferred_element_type=F32)


def params(limit=60 << 20, **more):
    return pltpu.CompilerParams(vmem_limit_bytes=limit, **more)


def whole(*shape):
    return pl.BlockSpec(shape, lambda *_: (0,) * len(shape))


def normalized(values):
    centered = values - jnp.mean(values, axis=-1, keepdims=True)
    inverse = lax.rsqrt(jnp.mean(centered * centered, axis=-1, keepdims=True) + EPSILON)
    return centered * inverse, inverse


def project_kernel(x0, x1, x2, x3, mask, gain, shift, w, wt, bias, bias_col, normed, qa, ka, va, qn, kt, vt):
    rows = x0.shape[0]
    total = MEMBERS * rows
    padded = qa.shape[2]
    step = rows // 3
    for d, x in enumerate((x0, x1, x2, x3)):

        def some(i, carry, d=d, x=x):
            here = x[pl.ds(i * step, step), :].astype(F32)
            unit, _ = normalized(here)
            normed[pl.ds(d * rows + i * step, step), :] = (unit * gain[...] + shift[...]).astype(BF16)
            return carry

        lax.fori_loop(0, 3, some, 0)
    for d in range(MEMBERS):
        here = pl.ds(d * rows, rows)
        natural = dot(normed[here, :], w[...]) + bias[...]
        lane = lax.broadcasted_iota(jnp.int32, (rows, HD), 1)
        low_mask = NEG_FILL * (1.0 - mask[here, :])
        key_tail = jnp.where(lane == 0, low_mask, jnp.where(lane < 4, 1.0, 0.0)).astype(BF16)
        value_tail = jnp.where(lane < 3, 1.0, 0.0).astype(BF16)
        for h in range(LOCAL_HEADS):
            at = h * HD
            qn[h, here, :] = (natural[:, at : at + HD] * HD ** (-0.5)).astype(BF16)
            ka[h, here, :HD] = natural[:, WIDTH + at : WIDTH + at + HD].astype(BF16)
            ka[h, here, HD:] = key_tail
            va[h, here, :HD] = natural[:, 2 * WIDTH + at : 2 * WIDTH + at + HD].astype(BF16)
            va[h, here, HD:] = value_tail
    turned = dot_nt(wt[...], normed[...]) + bias_col[...]
    row = lax.broadcasted_iota(jnp.int32, (HD, padded), 0)
    query_tail = jnp.where(row == 0, 1.0, 0.0).astype(BF16)
    for h in range(LOCAL_HEADS):
        at = h * HD
        qn[h, total:, :] = jnp.zeros((padded - total, HD), BF16)
        qa[h, :HD, :total] = (turned[at : at + HD] * HD ** (-0.5)).astype(BF16)
        qa[h, :HD, total:] = jnp.zeros((HD, padded - total), BF16)
        qa[h, HD:, :] = query_tail
        kt[h] = turned[WIDTH + at : WIDTH + at + HD].astype(BF16)
        vt[h] = turned[2 * WIDTH + at : 2 * WIDTH + at + HD].astype(BF16)


def project(x_blocks, mask, gain, shift, w, bias):
    rows, model = x_blocks[0].shape
    total = MEMBERS * rows
    padded = -(-total // TILE) * TILE
    n = LOCAL_HEADS
    outs = [
        jax.ShapeDtypeStruct((total, model), BF16),
        jax.ShapeDtypeStruct((n, 2 * HD, padded), BF16),
        jax.ShapeDtypeStruct((n, total, 2 * HD), BF16),
        jax.ShapeDtypeStruct((n, total, 2 * HD), BF16),
        jax.ShapeDtypeStruct((n, padded, HD), BF16),
        jax.ShapeDtypeStruct((n, HD, total), BF16),
        jax.ShapeDtypeStruct((n, HD, total), BF16),
    ]
    flops = 4 * total * model * 3 * WIDTH
    return pl.pallas_call(
        project_kernel,
        out_shape=outs,
        in_specs=[pl.BlockSpec(memory_space=VMEM)] * 11,
        out_specs=[pl.BlockSpec(memory_space=VMEM)] * len(outs),
        compiler_params=params(),
        cost_estimate=pl.CostEstimate(flops=flops, bytes_accessed=12 << 20, transcendentals=0),
        name="project",
    )(*x_blocks, mask, gain[None, :], shift[None, :], w, w.T, bias[None, :], bias[:, None])


def forward_kernel(qa, ka, vt, low, turned, logs, held):
    head = pl.program_id(0)
    total = ka.shape[1]
    tiles = qa.shape[2] // TILE

    def some(i, carry):
        here = pl.ds(pl.multiple_of(i * TILE, TILE), TILE)
        scores = dot(ka[0], qa[0, :, here])
        peak = jnp.max(scores, axis=0, keepdims=True)
        weights = jnp.exp(scores - peak)
        sums = jnp.sum(weights, axis=0, keepdims=True)
        mixed = dot(vt[0], weights.astype(BF16)) * (1.0 / sums)
        turned[0, :, here] = mixed
        logs[0, :, here] = peak + jnp.log(sums)
        held[here, :] = mixed.T.astype(BF16)
        return carry

    lax.fori_loop(0, tiles, some, 0)
    for h in range(LOCAL_HEADS):

        @pl.when(head == h)
        def _(h=h):
            low[:, h * HD : (h + 1) * HD] = held[:total, :]


def attend(qa, ka, vt):
    n, total, _ = ka.shape
    padded = qa.shape[2]
    per_head = lambda *shape: pl.BlockSpec((1,) + shape, lambda h: (h, 0, 0))
    return pl.pallas_call(
        forward_kernel,
        grid=(n,),
        out_shape=[
            jax.ShapeDtypeStruct((total, WIDTH), BF16),
            jax.ShapeDtypeStruct((n, HD, padded), F32),
            jax.ShapeDtypeStruct((n, 1, padded), F32),
        ],
        in_specs=[per_head(2 * HD, padded), per_head(total, 2 * HD), per_head(HD, total)],
        out_specs=[whole(total, WIDTH), per_head(HD, padded), per_head(1, padded)],
        scratch_shapes=[VMEM((padded, HD), BF16)],
        compiler_params=params(),
        cost_estimate=pl.CostEstimate(flops=16 * n * total * total * HD, bytes_accessed=8 << 20, transcendentals=n * total * total),
        name="attend",
    )(qa, ka, vt)


def three_parts(row):
    high = row.astype(BF16).astype(F32)
    rest = row - high
    middle = rest.astype(BF16).astype(F32)
    return high, middle, rest - middle


def backward_kernel(qa, ka, va, qn, kt, turned, logs, g0, g1, g2, g3, out, held_g, held_q, sum_k, sum_v):
    head = pl.program_id(0)
    rows = g0.shape[0]
    total = ka.shape[1]
    padded = qa.shape[2]
    tiles = padded // TILE
    for h in range(LOCAL_HEADS):

        @pl.when(head == h)
        def _(h=h):
            for d, part in enumerate((g0, g1, g2, g3)):
                held_g[d * rows : (d + 1) * rows, :] = part[:, h * HD : (h + 1) * HD]

    held_g[total:, :] = jnp.zeros((padded - total, HD), BF16)
    sum_k[...] = jnp.zeros_like(sum_k)
    sum_v[...] = jnp.zeros_like(sum_v)
    row = lax.broadcasted_iota(jnp.int32, (HD, TILE), 0)

    def some(i, carry):
        here = pl.ds(pl.multiple_of(i * TILE, TILE), TILE)
        grad = held_g[here, :]
        grad_turned = grad.astype(F32).T
        delta = jnp.sum(grad_turned * turned[0, :, here], axis=0, keepdims=True)
        high, middle, least = three_parts(-logs[0, :, here])
        tail = jnp.where(row == 0, 1.0, jnp.where(row == 1, high, jnp.where(row == 2, middle, jnp.where(row == 3, least, 0.0))))
        query = jnp.concatenate([qa[0, :HD, here], tail.astype(BF16)], axis=0)
        probs = jnp.exp(dot(ka[0], query))
        high, middle, least = three_parts(-delta)
        tail = jnp.where(row == 0, high, jnp.where(row == 1, middle, jnp.where(row == 2, least, 0.0)))
        grad_tail = jnp.concatenate([grad_turned, tail], axis=0).astype(BF16)
        grad_scores = (probs * dot(va[0], grad_tail)).astype(BF16)
        sum_v[...] += dot(probs.astype(BF16), grad)
        sum_k[...] += dot(grad_scores, qn[0, here, :])
        query_grad = dot(kt[0], grad_scores) * HD ** (-0.5)
        held_q[here, :] = query_grad.T.astype(BF16)
        return carry

    lax.fori_loop(0, tiles, some, 0)
    for h in range(LOCAL_HEADS):

        @pl.when(head == h)
        def _(h=h):
            at = h * HD
            out[:, at : at + HD] = held_q[:total, :]
            out[:, WIDTH + at : WIDTH + at + HD] = sum_k[...].astype(BF16)
            out[:, 2 * WIDTH + at : 2 * WIDTH + at + HD] = sum_v[...].astype(BF16)


def attend_back(qa, ka, va, qn, kt, turned, logs, grads):
    n, total, _ = ka.shape
    padded = qa.shape[2]
    rows = grads[0].shape[0]
    per_head = lambda *shape: pl.BlockSpec((1,) + shape, lambda h: (h, 0, 0))
    return pl.pallas_call(
        backward_kernel,
        grid=(n,),
        out_shape=jax.ShapeDtypeStruct((total, 3 * WIDTH), BF16),
        in_specs=[
            per_head(2 * HD, padded),
            per_head(total, 2 * HD),
            per_head(total, 2 * HD),
            per_head(padded, HD),
            per_head(HD, total),
            per_head(HD, padded),
            per_head(1, padded),
        ]
        + [whole(rows, WIDTH)] * MEMBERS,
        out_specs=whole(total, 3 * WIDTH),
        scratch_shapes=[
            VMEM((padded, HD), BF16),
            VMEM((padded, HD), BF16),
            VMEM((total, HD), F32),
            VMEM((total, HD), F32),
        ],
        compiler_params=params(),
        cost_estimate=pl.CostEstimate(flops=40 * n * total * total * HD, bytes_accessed=12 << 20, transcendentals=n * total * total),
        name="attend_back",
    )(qa, ka, va, qn, kt, turned, logs, *grads)


def middle_kernel(
    side, x, a0, a1, a2, a3, wo, out_bias, gain, shift, cot, valid, down_bias, up, up_bias, down,
    layer, down_send, down_keep, rest_send, rest_keep, grad_up_bias, grad_hidden, g0, g1, g2, g3, vectors,
    hidden, normed, grad_down, total_out, total_grad,
):
    step = pl.program_id(0)
    last = pl.num_programs(0) - 1
    half = pl.num_programs(0) // 2
    model = x.shape[1]

    @pl.when(step == 0)
    def _():
        value = x[...].astype(F32) + out_bias[...]
        for e, part in enumerate((a0, a1, a2, a3)):
            value += dot(part[...], wo[e])
        hidden[...] = value
        unit, _ = normalized(value)
        normed[...] = (unit * gain[...] + shift[...]).astype(BF16)
        low = (valid[...] * cot[...].astype(F32)).astype(BF16)
        grad_down[...] = low
        vectors[3:4, :] = jnp.sum(low.astype(F32), axis=0, keepdims=True)
        total_out[...] = value + down_bias[...]
        total_grad[...] = jnp.zeros_like(total_grad)

    gate = dot(normed[...], up[...]) + up_bias[0]
    below = 0.5 * (1.0 + lax.erf(gate * (0.5**0.5)))
    active = (gate * below).astype(BF16)
    slope = below + gate * (jnp.exp(-0.5 * gate * gate) * (0.5 / jnp.pi) ** 0.5)
    low = grad_down[...]
    grad_gate = (dot_nt(low, down[...]) * slope).astype(BF16)
    total_out[...] += dot(active, down[...])
    total_grad[...] += dot_nt(grad_gate, up[...])
    grad_up_bias[0] = jnp.sum(grad_gate.astype(F32), axis=0, keepdims=True)
    of_down = dot_tn(active, low).astype(BF16)
    of_up = dot_tn(normed[...], grad_gate).astype(BF16)
    for i in range(2 * half):

        @pl.when(step == i)
        def _(i=i):
            if i < half:
                down_send[...] = of_down
                rest_send[i * model : (i + 1) * model, :] = of_up
            else:
                down_keep[...] = of_down
                rest_keep[(i - half) * model : (i - half + 1) * model, :] = of_up

    @pl.when(step == last)
    def _():
        unit, inverse = normalized(hidden[...])
        layer[...] = (valid[...] * total_out[...]).astype(BF16)
        grad = total_grad[...]
        vectors[0:1, :] = jnp.sum(grad * unit, axis=0, keepdims=True)
        vectors[1:2, :] = jnp.sum(grad, axis=0, keepdims=True)
        scaled = grad * gain[...]
        inner = scaled - jnp.mean(scaled, axis=-1, keepdims=True)
        inner = inner - unit * jnp.mean(scaled * unit, axis=-1, keepdims=True)
        grad = grad_down[...].astype(F32) + inverse * inner
        grad_hidden[...] = grad
        branch = grad.astype(BF16)
        vectors[2:3, :] = jnp.sum(branch.astype(F32), axis=0, keepdims=True)
        parts = (a0, a1, a2, a3)
        for e, given in enumerate((g0, g1, g2, g3)):
            given[...] = dot_nt(branch, wo[e]).astype(BF16)
            place = half * model + (side[1] ^ (e & 1)) * WIDTH
            held = rest_keep if e < 2 else rest_send
            held[pl.ds(pl.multiple_of(place, WIDTH), WIDTH), :] = dot_tn(parts[e][...], branch).astype(BF16)


def middle(core, near, x, attended, wo, out_bias, gain, shift, cot, valid, down_bias, up, up_bias, down):
    rows, model = x.shape
    blocks = up.shape[1] // model
    half = blocks // 2

    def block_of(i, side):
        return lax.rem(i, half) + half * jnp.where(i < half, 1 - side[0], side[0])

    whole_s = lambda *shape: pl.BlockSpec(shape, lambda i, side: (0,) * len(shape))
    rest_rows = half * model + 2 * WIDTH
    shaped = jax.ShapeDtypeStruct
    outs = [
        (shaped((rows, model), BF16), whole_s(rows, model)),
        (shaped((half * model, model), BF16), pl.BlockSpec((model, model), lambda i, side: (jnp.minimum(i, half - 1), 0))),
        (shaped((half * model, model), BF16), pl.BlockSpec((model, model), lambda i, side: (jnp.maximum(i - half, 0), 0))),
        (shaped((rest_rows, model), BF16), whole_s(rest_rows, model)),
        (shaped((rest_rows, model), BF16), whole_s(rest_rows, model)),
        (shaped((blocks, 1, model), F32), pl.BlockSpec((1, 1, model), lambda i, side: (block_of(i, side), 0, 0))),
        (shaped((rows, model), F32), whole_s(rows, model)),
    ]
    outs += [(shaped((rows, WIDTH), BF16), whole_s(rows, WIDTH))] * MEMBERS
    outs += [(shaped((4, model), F32), whole_s(4, model))]
    return pl.pallas_call(
        middle_kernel,
        out_shape=[o[0] for o in outs],
        grid_spec=pltpu.PrefetchScalarGridSpec(
            num_scalar_prefetch=1,
            grid=(blocks,),
            in_specs=[whole_s(rows, model)]
            + [whole_s(rows, WIDTH)] * MEMBERS
            + [whole_s(MEMBERS, WIDTH, model)]
            + [whole_s(1, model)] * 3
            + [whole_s(rows, model), whole_s(rows, 1), whole_s(1, model)]
            + [
                pl.BlockSpec((model, model), lambda i, side: (0, block_of(i, side))),
                pl.BlockSpec((1, 1, model), lambda i, side: (block_of(i, side), 0, 0)),
                pl.BlockSpec((model, model), lambda i, side: (block_of(i, side), 0)),
            ],
            out_specs=[o[1] for o in outs],
            scratch_shapes=[
                VMEM((rows, model), F32),
                VMEM((rows, model), BF16),
                VMEM((rows, model), BF16),
                VMEM((rows, model), F32),
                VMEM((rows, model), F32),
            ],
        ),
        compiler_params=params(),
        cost_estimate=pl.CostEstimate(flops=12 * rows * model * model * blocks, bytes_accessed=25 << 20, transcendentals=2 * rows * model * blocks),
        name="middle",
    )(
        jnp.stack([core, near]).astype(jnp.int32),
        x, *attended, wo, out_bias[None], gain[None], shift[None], cot, valid, down_bias[None],
        up, up_bias.reshape(blocks, 1, model), down,
    )


def over_cube(value, bit):
    count = lax.axis_size("cube")
    return lax.ppermute(value, "cube", [(i, i ^ (1 << bit)) for i in range(count)])


def over_blk(value, bit):
    return lax.ppermute(value, "blk", [(i, i ^ (1 << bit)) for i in range(MEMBERS)])


def chosen_pairs(is_home, cube_flip, blk_flip):
    pairs = []
    for c in range(lax.axis_size("cube")):
        for b in range(MEMBERS):
            if ((c & 1) == (b >> 1)) == is_home:
                pairs.append((c * MEMBERS + b, (c ^ cube_flip) * MEMBERS + (b ^ blk_flip)))
    return pairs


def sent_between(value, is_home, cube_flip, blk_flip):
    return lax.ppermute(value, ("cube", "blk"), chosen_pairs(is_home, cube_flip, blk_flip))


def exchanged(parts):
    far = over_blk(parts[3], 0)
    near = over_blk(parts[1], 0)
    core = over_cube(parts[2], 0)
    return [parts[0], near, core, over_cube(far, 0)]


def half_of(rows, which, axis=0):
    size = rows.shape[axis] // 2
    return lax.dynamic_slice_in_dim(rows, which * size, size, axis)


def added(first, second):
    return (first.astype(F32) + second.astype(F32)).astype(BF16)


def halved(rows, flag, send, axis=0):
    got = send(half_of(rows, 1 - flag, axis))
    return added(half_of(rows, flag, axis), got)


def joined(own, got, flag, axis=0):
    return jnp.where(
        flag == 0,
        jnp.concatenate([own, got], axis),
        jnp.concatenate([got, own], axis),
    )


def cube_bits():
    return list(range(1, lax.axis_size("cube").bit_length() - 1))


def flag_of(index, bit):
    return (index >> bit) & 1


def reduced_over_planes(first, second, cube):
    bits = cube_bits()
    for one, two in zip(bits, reversed(bits)):
        first = halved(first, flag_of(cube, one), lambda v, s=one: over_cube(v, s))
        second = halved(second, flag_of(cube, two), lambda v, s=two: over_cube(v, s))
    return first, second


def gathered_over_planes(first, second, cube, axis=0):
    bits = cube_bits()
    for one, two in zip(reversed(bits), bits):
        first = joined(first, over_cube(first, one), flag_of(cube, one), axis)
        second = joined(second, over_cube(second, two), flag_of(cube, two), axis)
    return first, second


def summed_everywhere(keep, send, cube, blk):
    half = added(keep, over_cube(send, 0))
    size = half.shape[0] // 2
    first, second = reduced_over_planes(half[:size], half[size:], cube)
    both = jnp.stack([first, second])
    both = halved(both, flag_of(blk, 0), lambda v: over_blk(v, 0), 1)
    both = halved(both, flag_of(blk, 1), lambda v: over_blk(v, 1), 1)
    both = joined(both, over_blk(both, 1), flag_of(blk, 1), 1)
    both = joined(both, over_blk(both, 0), flag_of(blk, 0), 1)
    first, second = gathered_over_planes(both[0], both[1], cube)
    got_first, got_second = over_cube(first, 0), over_cube(second, 0)
    mine = jnp.concatenate([first, second])
    other = jnp.concatenate([got_first, got_second])
    flag = cube & 1
    return jnp.where(flag == 0, mine, other), jnp.where(flag == 0, other, mine)


def layer_norm(values, gain_vec, shift_vec):
    centered = values - jnp.mean(values, axis=-1, keepdims=True)
    normed = centered * lax.rsqrt(jnp.mean(centered * centered, axis=-1, keepdims=True) + EPSILON)
    return normed * gain_vec + shift_vec


def matmul_back(left_side, right_side):
    return jnp.einsum("rf,df->rd", left_side, right_side, preferred_element_type=F32)


def weight_grad(left_side, right_side):
    return jnp.einsum("rd,rf->df", left_side, right_side, preferred_element_type=F32)


def column_sums(low_rows):
    return jnp.sum(low_rows, axis=0, dtype=F32)


def member_columns(matrix, member, axis):
    return lax.dynamic_slice_in_dim(matrix, member * WIDTH, WIDTH, axis)


def body(
    inputs,
    cotangent,
    absent_groups,
    token_group,
    pre_gain,
    pre_shift,
    input_weight,
    input_bias,
    output_weight,
    output_bias,
    mid_gain,
    mid_shift,
    up_weight,
    up_bias,
    down_weight,
    down_bias,
):
    _, rows, model = inputs.shape
    hidden_units = up_weight.shape[1]
    cube, blk = lax.axis_index("cube"), lax.axis_index("blk")
    core = cube & 1
    at_home = core == (blk >> 1)
    member = 2 * core + (blk & 1)

    def moved(value):
        return jnp.where(at_home, value, sent_between(value, False, 1, 2))

    def from_group(value):
        value_moved = sent_between(value, False, 1, 2)
        near_home = sent_between(value, True, 0, 1)
        own = jnp.where(at_home, value, value_moved)
        near = jnp.where(at_home, near_home, sent_between(value_moved, False, 0, 1))
        return [own, near, over_cube(own, 0), over_cube(near, 0)]

    group_match = token_group[0][:, None] == jnp.arange(GROUPS, dtype=jnp.int32)[None, :]
    lacking = jnp.sum(jnp.where(group_match, absent_groups, 0), axis=1)
    valid_here = (1 - lacking).astype(BF16)[None, :]
    x_blocks = from_group(inputs[0])
    valid_blocks = from_group(valid_here)
    cot_own = moved(cotangent[0])
    valid_all = jnp.concatenate(valid_blocks, axis=1).astype(F32).reshape(-1, 1)

    in_columns = jnp.concatenate(
        [member_columns(input_weight[:, s * model : (s + 1) * model], member, 1) for s in range(3)],
        axis=1,
    )
    bias_columns = member_columns(input_bias, member, 1)
    bias_columns = jnp.concatenate([bias_columns[0], jnp.zeros((WIDTH,), F32), bias_columns[1]])
    out_rows = jnp.stack([member_columns(output_weight, member ^ e, 0) for e in range(MEMBERS)])

    normed_low, qa, ka, va, qn, kt, vt = project(
        x_blocks, valid_all, pre_gain, pre_shift, in_columns, bias_columns
    )
    attended_own, turned, logs = attend(qa, ka, vt)
    attended = exchanged([attended_own[d * rows : (d + 1) * rows] for d in range(MEMBERS)])
    (
        layer_here,
        down_send,
        down_keep,
        rest_send,
        rest_keep,
        grad_up_bias,
        grad_hidden,
        *grad_attended,
        middle_vectors,
    ) = middle(
        core,
        blk & 1,
        x_blocks[0],
        attended,
        out_rows,
        output_bias,
        mid_gain,
        mid_shift,
        cot_own,
        valid_all[:rows],
        down_bias,
        up_weight,
        up_bias,
        down_weight,
    )
    layer_out = moved(layer_here)
    blocks = hidden_units // model
    down_sum = summed_everywhere(down_keep, down_send, cube, blk)
    rest_sum = summed_everywhere(rest_keep, rest_send, cube, blk)
    grad_down_weight = jnp.concatenate(down_sum).astype(F32)
    up_rows = blocks // 2 * model
    grad_up_weight = jnp.concatenate(
        [
            half[s * model : (s + 1) * model]
            for half in rest_sum
            for s in range(blocks // 2)
        ],
        axis=1,
    ).astype(F32)
    grad_output_weight = jnp.concatenate([half[up_rows:] for half in rest_sum]).astype(F32)

    grad_columns = attend_back(qa, ka, va, qn, kt, turned, logs, exchanged(grad_attended))
    grad_in = weight_grad(normed_low, grad_columns)
    column_total = column_sums(grad_columns)

    partial = matmul_back(grad_columns, in_columns).astype(BF16).reshape(MEMBERS, rows, model)
    near_sum = added(partial[1], over_cube(partial[3], 0))
    own_sum = partial[0].astype(F32) + over_cube(partial[2], 0).astype(F32)
    grad_normed = own_sum + over_blk(near_sum, 0).astype(F32)
    _, pre_back = jax.vjp(layer_norm, x_blocks[0].astype(F32), pre_gain, pre_shift)
    grad_pre, grad_pre_gain, grad_pre_shift = pre_back(grad_normed)
    grad_here = grad_hidden + grad_pre
    input_grad = jnp.where(
        at_home, grad_here, sent_between(grad_here.astype(BF16), False, 1, 2).astype(F32)
    )

    in_low = grad_in.astype(BF16)
    size = model // 2
    first, second = reduced_over_planes(in_low[:size], in_low[size:], cube)
    both = halved(jnp.stack([first, second]), flag_of(blk, 1), lambda v: over_blk(v, 1), 1)
    both = joined(both, over_blk(both, 1), flag_of(blk, 1), 1)
    both = jnp.stack([both, over_blk(both, 0)], axis=1)
    first, second = gathered_over_planes(both[0], both[1], cube, 1)
    mine = jnp.concatenate([first, second], axis=1)
    other = over_cube(mine, 0)
    pair = [mine[0], mine[1], other[0], other[1]]
    low_flag, high_flag = member & 1, member >> 1
    pair = [jnp.where(low_flag == 0, pair[e], pair[e ^ 1]) for e in range(MEMBERS)]
    pair = [jnp.where(high_flag == 0, pair[e], pair[e ^ 2]) for e in range(MEMBERS)]
    grad_input_weight = jnp.concatenate(
        [
            part[:, s * WIDTH : (s + 1) * WIDTH]
            for s in range(3)
            for part in pair
        ],
        axis=1,
    ).astype(F32)

    here_bias = jnp.stack([column_total[:WIDTH], column_total[2 * WIDTH :]])
    spread_bias = lax.dynamic_update_slice_in_dim(
        jnp.zeros((2, model), F32), here_bias, member * WIDTH, 1
    )
    vectors = jnp.concatenate(
        [
            jnp.stack([grad_pre_gain, grad_pre_shift]),
            middle_vectors,
            spread_bias,
            grad_up_bias.reshape(blocks, model),
        ]
    )
    vectors = lax.psum(vectors, ("cube", "blk"))
    return (
        layer_out[None],
        input_grad[None],
        vectors[0],
        vectors[1],
        grad_input_weight,
        vectors[6:8],
        grad_output_weight,
        vectors[4],
        vectors[2],
        vectors[3],
        grad_up_weight,
        vectors[8:].reshape(-1),
        grad_down_weight,
        vectors[5],
    )


def solution(mesh):
    rows_spec = P("cube", "blk", None)
    return jax.shard_map(
        body,
        mesh=mesh,
        in_specs=(rows_spec, rows_spec, P("cube", None), P("cube", "blk")) + (P(),) * 12,
        out_specs=(rows_spec, rows_spec) + (P(),) * 12,
        check_vma=False,
    )
```

```python
import functools
import jax
import jax.numpy as jnp
from jax import lax
from jax.experimental import pallas as pl
from jax.experimental.pallas import tpu as pltpu
from jax.sharding import PartitionSpec as P

HEADS = 12
HD = 64
GROUPS = 12
MEMBERS = 4
LOCAL_HEADS = HEADS // MEMBERS
WIDTH = LOCAL_HEADS * HD
NEG_FILL = -32768.0
EPSILON = 1e-06
BF16 = jnp.bfloat16
F32 = jnp.float32
TILE = 256
LANES = 128
VMEM = pltpu.VMEM
QUICK = pl.CostEstimate(flops=1, bytes_accessed=1, transcendentals=0)


def dot(left, right):
    return jnp.dot(left, right, preferred_element_type=F32)


def dot_nt(left, right):
    return lax.dot_general(left, right, (((1,), (1,)), ((), ())), preferred_element_type=F32)


def dot_tn(left, right):
    return lax.dot_general(left, right, (((0,), (0,)), ((), ())), preferred_element_type=F32)


def params(limit=60 << 20, **more):
    return pltpu.CompilerParams(vmem_limit_bytes=limit, **more)


def whole(*shape):
    return pl.BlockSpec(shape, lambda *_: (0,) * len(shape))


def normalized(values):
    centered = values - jnp.mean(values, axis=-1, keepdims=True)
    inverse = lax.rsqrt(jnp.mean(centered * centered, axis=-1, keepdims=True) + EPSILON)
    return centered * inverse, inverse


def mask_column(x, rows):
    return x[rows:, :rows].astype(F32).T[:, :1]


def project_kernel(x0, x1, x2, x3, gain, shift, w, wt, bias, bias_col, normed, qa, ka, va, qn, kt, vt):
    rows = normed.shape[0] // MEMBERS
    total = MEMBERS * rows
    padded = qa.shape[2]
    step = rows // 3
    for d, x in enumerate((x0, x1, x2, x3)):

        def some(i, carry, d=d, x=x):
            here = x[pl.ds(i * step, step), :].astype(F32)
            unit, _ = normalized(here)
            normed[pl.ds(d * rows + i * step, step), :] = (unit * gain[...][None] + shift[...][None]).astype(BF16)
            return carry

        lax.fori_loop(0, 3, some, 0)
    for d, x in enumerate((x0, x1, x2, x3)):
        here = pl.ds(d * rows, rows)
        natural = dot(normed[here, :], w[...]) + bias[...][None]
        lane = lax.broadcasted_iota(jnp.int32, (rows, HD), 1)
        low_mask = NEG_FILL * (1.0 - mask_column(x, rows))
        key_tail = jnp.where(lane == 0, low_mask, jnp.where(lane < 4, 1.0, 0.0)).astype(BF16)
        value_tail = jnp.where(lane < 3, 1.0, 0.0).astype(BF16)
        for h in range(LOCAL_HEADS):
            at = h * HD
            qn[h, here, :] = (natural[:, at : at + HD] * HD ** (-0.5)).astype(BF16)
            ka[h, here, :HD] = natural[:, WIDTH + at : WIDTH + at + HD].astype(BF16)
            ka[h, here, HD:] = key_tail
            va[h, here, :HD] = natural[:, 2 * WIDTH + at : 2 * WIDTH + at + HD].astype(BF16)
            va[h, here, HD:] = value_tail
    turned = dot_nt(wt[...], normed[...]) + bias_col[...]
    row = lax.broadcasted_iota(jnp.int32, (HD, padded), 0)
    query_tail = jnp.where(row == 0, 1.0, 0.0).astype(BF16)
    for h in range(LOCAL_HEADS):
        at = h * HD
        qn[h, total:, :] = jnp.zeros((padded - total, HD), BF16)
        qa[h, :HD, :total] = (turned[at : at + HD] * HD ** (-0.5)).astype(BF16)
        qa[h, :HD, total:] = jnp.zeros((HD, padded - total), BF16)
        qa[h, HD:, :] = query_tail
        kt[h] = turned[WIDTH + at : WIDTH + at + HD].astype(BF16)
        vt[h] = turned[2 * WIDTH + at : 2 * WIDTH + at + HD].astype(BF16)


def project(x_blocks, rows, gain, shift, w, wt, bias, bias_col):
    model = x_blocks[0].shape[1]
    total = MEMBERS * rows
    padded = -(-total // TILE) * TILE
    n = LOCAL_HEADS
    outs = [
        jax.ShapeDtypeStruct((total, model), BF16),
        jax.ShapeDtypeStruct((n, 2 * HD, padded), BF16),
        jax.ShapeDtypeStruct((n, total, 2 * HD), BF16),
        jax.ShapeDtypeStruct((n, total, 2 * HD), BF16),
        jax.ShapeDtypeStruct((n, padded, HD), BF16),
        jax.ShapeDtypeStruct((n, HD, total), BF16),
        jax.ShapeDtypeStruct((n, HD, total), BF16),
    ]
    flops = 4 * total * model * 3 * WIDTH
    return pl.pallas_call(
        project_kernel,
        out_shape=outs,
        in_specs=[pl.BlockSpec(memory_space=VMEM)] * 10,
        out_specs=[pl.BlockSpec(memory_space=VMEM)] * len(outs),
        compiler_params=params(),
        cost_estimate=QUICK,
        name="project",
    )(*x_blocks, gain, shift, w, wt, bias, bias_col)


def forward_kernel(qa, ka, vt, l0, l1, l2, l3, turned, logs, held, even, odd):
    head = pl.program_id(0)
    rows = l0.shape[0]
    tiles = qa.shape[2] // TILE

    def scored(i, out):
        here = pl.ds(pl.multiple_of(i * TILE, TILE), TILE)
        out[...] = dot(ka[0], qa[0, :, here])

    def mixed_of(i, scores):
        here = pl.ds(pl.multiple_of(i * TILE, TILE), TILE)
        peak = jnp.max(scores[...], axis=0, keepdims=True)
        weights = jnp.exp(scores[...] - peak)
        sums = jnp.sum(weights, axis=0, keepdims=True)
        mixed = dot(vt[0], weights.astype(BF16)) * (1.0 / sums)
        turned[0, :, here] = mixed
        logs[0, :, here] = peak + jnp.log(sums)
        held[here, :] = mixed.T.astype(BF16)

    scored(0, even)

    def pair(i, carry):
        scored(2 * i + 1, odd)
        mixed_of(2 * i, even)
        scored(jnp.minimum(2 * i + 2, tiles - 1), even)
        mixed_of(2 * i + 1, odd)
        return carry

    lax.fori_loop(0, tiles // 2, pair, 0)
    if tiles % 2:
        mixed_of(tiles - 1, even)
    for h in range(LOCAL_HEADS):

        @pl.when(head == h)
        def _(h=h):
            for d, low in enumerate((l0, l1, l2, l3)):
                low[:, h * HD : (h + 1) * HD] = held[d * rows : (d + 1) * rows, :]


def attend(qa, ka, vt):
    n, total, _ = ka.shape
    padded = qa.shape[2]
    rows = total // MEMBERS
    per_head = lambda *shape: pl.BlockSpec((1,) + shape, lambda h: (h, 0, 0))
    *low, turned, logs = pl.pallas_call(
        forward_kernel,
        grid=(n,),
        out_shape=[jax.ShapeDtypeStruct((rows, WIDTH), BF16)] * MEMBERS
        + [
            jax.ShapeDtypeStruct((n, HD, padded), F32),
            jax.ShapeDtypeStruct((n, 1, padded), F32),
        ],
        in_specs=[per_head(2 * HD, padded), per_head(total, 2 * HD), per_head(HD, total)],
        out_specs=[whole(rows, WIDTH)] * MEMBERS + [per_head(HD, padded), per_head(1, padded)],
        scratch_shapes=[VMEM((padded, HD), BF16), VMEM((total, TILE), F32), VMEM((total, TILE), F32)],
        compiler_params=params(),
        cost_estimate=QUICK,
        name="attend",
    )(qa, ka, vt)
    return low, turned, logs


def three_parts(row):
    high = row.astype(BF16).astype(F32)
    rest = row - high
    middle = rest.astype(BF16).astype(F32)
    return high, middle, rest - middle


def backward_kernel(head, qa, ka, va, qn, kt, turned, logs, g0, g1, g2, g3, out_q, out_k, out_v, held_g, sum_k, sum_v):
    rows = g0.shape[0]
    total = ka.shape[1]
    padded = qa.shape[2]
    tiles = padded // TILE
    for d, part in enumerate((g0, g1, g2, g3)):
        held_g[d * rows : (d + 1) * rows, :] = part[:, head * HD : (head + 1) * HD]
    held_g[total:, :] = jnp.zeros((padded - total, HD), BF16)
    sum_k[...] = jnp.zeros_like(sum_k)
    sum_v[...] = jnp.zeros_like(sum_v)
    row = lax.broadcasted_iota(jnp.int32, (HD, TILE), 0)

    def some(i, width):
        here = pl.ds(pl.multiple_of(i * TILE, TILE), TILE)
        grad = held_g[here, :]
        grad_turned = grad.astype(F32).T
        delta = jnp.sum(grad_turned * turned[0, :, here], axis=0, keepdims=True)
        high, middle, least = three_parts(-logs[0, :, here])
        tail = jnp.where(row == 0, 1.0, jnp.where(row == 1, high, jnp.where(row == 2, middle, jnp.where(row == 3, least, 0.0))))
        query = jnp.concatenate([qa[0, :HD, here], tail.astype(BF16)], axis=0)
        probs = jnp.exp(dot(ka[0], query))
        high, middle, least = three_parts(-delta)
        tail = jnp.where(row == 0, high, jnp.where(row == 1, middle, jnp.where(row == 2, least, 0.0)))
        grad_tail = jnp.concatenate([grad_turned, tail], axis=0).astype(BF16)
        grad_scores = (probs * dot(va[0], grad_tail)).astype(BF16)
        sum_v[...] += dot(probs.astype(BF16), grad)
        sum_k[...] += dot(grad_scores, qn[0, here, :])
        query_grad = dot(kt[0], grad_scores) * HD ** (-0.5)
        out_q[pl.ds(pl.multiple_of(i * TILE, TILE), width), :] = query_grad.T.astype(BF16)[:width]

    def full(i, carry):
        some(i, TILE)
        return carry

    lax.fori_loop(0, tiles - 1, full, 0)
    some(tiles - 1, total - (tiles - 1) * TILE)
    out_k[...] = sum_k[...].astype(BF16)
    out_v[...] = sum_v[...].astype(BF16)


def attend_back(head, qa, ka, va, qn, kt, turned, logs, grads):
    n, total, _ = ka.shape
    padded = qa.shape[2]
    rows = grads[0].shape[0]
    per_head = lambda *shape: pl.BlockSpec((1,) + shape, lambda i: (head, 0, 0))
    return pl.pallas_call(
        functools.partial(backward_kernel, head),
        grid=(1,),
        out_shape=[jax.ShapeDtypeStruct((total, HD), BF16)] * 3,
        in_specs=[
            per_head(2 * HD, padded),
            per_head(total, 2 * HD),
            per_head(total, 2 * HD),
            per_head(padded, HD),
            per_head(HD, total),
            per_head(HD, padded),
            per_head(1, padded),
        ]
        + [whole(rows, WIDTH)] * MEMBERS,
        out_specs=[whole(total, HD)] * 3,
        scratch_shapes=[
            VMEM((padded, HD), BF16),
            VMEM((total, HD), F32),
            VMEM((total, HD), F32),
        ],
        compiler_params=params(),
        cost_estimate=QUICK,
        name="attend_back",
    )(qa, ka, va, qn, kt, turned, logs, *grads)


def unproject_kernel(*refs):
    columns, normed, w = refs[:9], refs[9], refs[10]
    n0, n1, n2, n3, first, second, sums, joint = refs[11:]
    rows = n0.shape[0]
    for s in range(3):
        for h in range(LOCAL_HEADS):
            at = s * WIDTH + h * HD
            joint[:, at : at + HD] = columns[3 * h + s][...]
    for d, out in enumerate((n0, n1, n2, n3)):
        out[...] = dot_nt(joint[d * rows : (d + 1) * rows, :], w[...]).astype(BF16)
    grad = dot_tn(normed[...], joint[...]).astype(BF16)
    pieces, each, _ = first.shape
    for i in range(pieces):
        first[i] = grad[2 * i * each : (2 * i + 1) * each]
        second[i] = grad[(2 * i + 1) * each : (2 * i + 2) * each]
    sums[...] = jnp.sum(joint[...].astype(F32), axis=0, keepdims=True)


def unproject(columns, normed, w, pieces):
    total, model = normed.shape
    rows = total // MEMBERS
    width = 3 * WIDTH
    shaped = jax.ShapeDtypeStruct
    outs = [shaped((rows, model), BF16)] * MEMBERS
    outs += [shaped((pieces, model // pieces // 2, width), BF16)] * 2 + [shaped((1, width), F32)]
    return pl.pallas_call(
        unproject_kernel,
        out_shape=outs,
        in_specs=[pl.BlockSpec(memory_space=VMEM)] * 11,
        out_specs=[pl.BlockSpec(memory_space=VMEM)] * len(outs),
        scratch_shapes=[VMEM((total, width), BF16)],
        compiler_params=params(),
        cost_estimate=QUICK,
        name="unproject",
    )(*columns, normed, w)


def close_kernel(x, p0, p1, gain, hidden, grad, low, vectors):
    rows = hidden.shape[0]
    unit, inverse = normalized(x[:rows, :].astype(F32))
    given = p0[...].astype(F32) + p1[...].astype(F32)
    vectors[0:1, :] = jnp.sum(given * unit, axis=0, keepdims=True)
    vectors[1:2, :] = jnp.sum(given, axis=0, keepdims=True)
    scaled = given * gain[...][None]
    inner = scaled - jnp.mean(scaled, axis=-1, keepdims=True)
    inner = inner - unit * jnp.mean(scaled * unit, axis=-1, keepdims=True)
    total = hidden[...] + inverse * inner
    grad[...] = total
    low[...] = total.astype(BF16)


def close(x, parts, gain, hidden):
    rows, model = hidden.shape
    shaped = jax.ShapeDtypeStruct
    return pl.pallas_call(
        close_kernel,
        out_shape=[shaped((rows, model), F32), shaped((rows, model), BF16), shaped((2, model), F32)],
        in_specs=[pl.BlockSpec(memory_space=VMEM)] * 5,
        out_specs=[pl.BlockSpec(memory_space=VMEM)] * 3,
        compiler_params=params(),
        cost_estimate=QUICK,
        name="close",
    )(x, *parts, gain, hidden)


def middle_kernel(
    side, x, a0, a1, a2, a3, wo, out_bias, gain, shift, cot, down_bias, up, up_bias, down,
    layer, down_send, down_keep, rest_send, rest_keep, grad_up_bias, grad_hidden, g0, g1, g2, g3, vectors,
    hidden, normed, grad_down, total_out, total_grad, valid,
):
    step = pl.program_id(0)
    last = pl.num_programs(0) - 1
    half = pl.num_programs(0) // 2
    rows, model = cot.shape
    pieces = down_keep.shape[0]
    each = half * model // pieces
    share = model // each

    @pl.when(step == 0)
    def _():
        valid[...] = mask_column(x, rows)
        value = x[:rows, :].astype(F32) + out_bias[...][None]
        for e, part in enumerate((a0, a1, a2, a3)):
            value += dot(part[...], wo[e])
        hidden[...] = value
        unit, _ = normalized(value)
        normed[...] = (unit * gain[...][None] + shift[...][None]).astype(BF16)
        low = (valid[...] * cot[...].astype(F32)).astype(BF16)
        grad_down[...] = low
        vectors[3:4, :] = jnp.sum(low.astype(F32), axis=0, keepdims=True)
        total_out[...] = value + down_bias[...][None]
        total_grad[...] = jnp.zeros_like(total_grad)

    gate = dot(normed[...], up[...]) + up_bias[0]
    below = 0.5 * (1.0 + lax.erf(gate * (0.5**0.5)))
    active = (gate * below).astype(BF16)
    slope = below + gate * (jnp.exp(-0.5 * gate * gate) * (0.5 / jnp.pi) ** 0.5)
    low = grad_down[...]
    grad_gate = (dot_nt(low, down[...]) * slope).astype(BF16)
    total_out[...] += dot(active, down[...])
    total_grad[...] += dot_nt(grad_gate, up[...])
    grad_up_bias[0] = jnp.sum(grad_gate.astype(F32), axis=0, keepdims=True)
    of_down = dot_tn(active, low).astype(BF16)
    of_up = dot_tn(normed[...], grad_gate).astype(BF16)
    for i in range(2 * half):

        @pl.when(step == i)
        def _(i=i):
            down_held, rest_held = (down_send, rest_send) if i < half else (down_keep, rest_keep)
            for j in range(share):
                at = (i % half) * share + j
                down_held[at] = of_down[j * each : (j + 1) * each]
                rest_held[at, :each, :] = of_up[j * each : (j + 1) * each]

    @pl.when(step == last)
    def _():
        unit, inverse = normalized(hidden[...])
        layer[...] = (valid[...] * total_out[...]).astype(BF16)
        grad = total_grad[...]
        vectors[0:1, :] = jnp.sum(grad * unit, axis=0, keepdims=True)
        vectors[1:2, :] = jnp.sum(grad, axis=0, keepdims=True)
        scaled = grad * gain[...][None]
        inner = scaled - jnp.mean(scaled, axis=-1, keepdims=True)
        inner = inner - unit * jnp.mean(scaled * unit, axis=-1, keepdims=True)
        grad = grad_down[...].astype(F32) + inverse * inner
        grad_hidden[...] = grad
        branch = grad.astype(BF16)
        vectors[2:3, :] = jnp.sum(branch.astype(F32), axis=0, keepdims=True)
        parts = (a0, a1, a2, a3)
        count = pieces // 2
        few = WIDTH // count
        for e, given in enumerate((g0, g1, g2, g3)):
            given[...] = dot_nt(branch, wo[e]).astype(BF16)
            held = rest_keep if e < 2 else rest_send
            place = (side[1] ^ (e & 1)) * count
            of_out = dot_tn(parts[e][...], branch).astype(BF16)
            for j in range(count):
                held[place + j, each:, :] = of_out[j * few : (j + 1) * few]


def middle(core, near, pieces, x, attended, wo, out_bias, gain, shift, cot, down_bias, up, up_bias, down):
    rows, model = cot.shape
    blocks = up.shape[1] // model
    half = blocks // 2

    def block_of(i, side):
        return lax.rem(i, half) + half * jnp.where(i < half, 1 - side[0], side[0])

    whole_s = lambda *shape: pl.BlockSpec(shape, lambda i, side: (0,) * len(shape))
    each = half * model // pieces
    held = (pieces, each, model)
    rest = (pieces, each + 2 * WIDTH // pieces, model)
    shaped = jax.ShapeDtypeStruct
    outs = [
        (shaped((rows, model), BF16), whole_s(rows, model)),
        (shaped(held, BF16), whole_s(*held)),
        (shaped(held, BF16), whole_s(*held)),
        (shaped(rest, BF16), whole_s(*rest)),
        (shaped(rest, BF16), whole_s(*rest)),
        (shaped((blocks, 1, model), F32), pl.BlockSpec((1, 1, model), lambda i, side: (block_of(i, side), 0, 0))),
        (shaped((rows, model), F32), whole_s(rows, model)),
    ]
    outs += [(shaped((rows, WIDTH), BF16), whole_s(rows, WIDTH))] * MEMBERS
    outs += [(shaped((4, model), F32), whole_s(4, model))]
    return pl.pallas_call(
        middle_kernel,
        out_shape=[o[0] for o in outs],
        grid_spec=pltpu.PrefetchScalarGridSpec(
            num_scalar_prefetch=1,
            grid=(blocks,),
            in_specs=[whole_s(*x.shape)]
            + [whole_s(rows, WIDTH)] * MEMBERS
            + [whole_s(MEMBERS, WIDTH, model)]
            + [whole_s(model)] * 3
            + [whole_s(rows, model), whole_s(model)]
            + [
                pl.BlockSpec((model, model), lambda i, side: (0, block_of(i, side))),
                pl.BlockSpec((1, 1, model), lambda i, side: (block_of(i, side), 0, 0)),
                pl.BlockSpec((model, model), lambda i, side: (block_of(i, side), 0)),
            ],
            out_specs=[o[1] for o in outs],
            scratch_shapes=[
                VMEM((rows, model), F32),
                VMEM((rows, model), BF16),
                VMEM((rows, model), BF16),
                VMEM((rows, model), F32),
                VMEM((rows, model), F32),
                VMEM((rows, 1), F32),
            ],
        ),
        compiler_params=params(),
        cost_estimate=QUICK,
        name="middle",
    )(
        jnp.stack([core, near]).astype(jnp.int32),
        x, *attended, wo, out_bias, gain, shift, cot, down_bias,
        up, up_bias.reshape(blocks, 1, model), down,
    )


def place_down_kernel(side, a0, b0, a1, b1, out):
    lanes = a0.shape[2]

    @pl.when(pl.program_id(0) == 0)
    def _():
        out[:, :lanes] = a0[0].astype(F32)
        out[:, lanes:] = b0[0].astype(F32)

    @pl.when(pl.program_id(0) == 1)
    def _():
        out[:, :lanes] = a1[0].astype(F32)
        out[:, lanes:] = b1[0].astype(F32)


def place_rest_kernel(side, a0, b0, a1, b1, up, out):
    lanes = a0.shape[2]
    each = up.shape[0]

    @pl.when(pl.program_id(0) == 0)
    def _():
        for at, part in ((0, a0), (lanes, b0)):
            up[:, at : at + lanes] = part[0, :each, :].astype(F32)
            out[:, at : at + lanes] = part[0, each:, :].astype(F32)

    @pl.when(pl.program_id(0) == 1)
    def _():
        for at, part in ((0, a1), (lanes, b1)):
            up[:, at : at + lanes] = part[0, :each, :].astype(F32)
            out[:, at : at + lanes] = part[0, each:, :].astype(F32)


def placed(kernel, core, parts, outs):
    pieces, rows, lanes = parts[0].shape
    first = pl.BlockSpec((1, rows, lanes), lambda n, i, side: (jnp.where(n == 0, i, pieces - 1), 0, 0))
    second = pl.BlockSpec((1, rows, lanes), lambda n, i, side: (jnp.where(n == 0, 0, i), 0, 0))
    return pl.pallas_call(
        kernel,
        out_shape=[jax.ShapeDtypeStruct(shape, F32) for shape, _, _ in outs],
        grid_spec=pltpu.PrefetchScalarGridSpec(
            num_scalar_prefetch=1,
            grid=(2, pieces),
            in_specs=[first, first, second, second],
            out_specs=[
                pl.BlockSpec(block, lambda n, i, side, place=place: place(lax.rem(n + side[0], 2), i))
                for _, block, place in outs
            ],
        ),
        compiler_params=params(),
        cost_estimate=QUICK,
        name="placed",
    )(core, *parts)


def placed_down(core, parts, hidden_units):
    pieces, each, lanes = parts[0].shape
    (down,) = placed(
        place_down_kernel,
        core,
        parts,
        [((hidden_units, 2 * lanes), (each, 2 * lanes), lambda k, i: (k * pieces + i, 0))],
    )
    return down


def placed_rest(core, parts, hidden_units):
    pieces, rows, lanes = parts[0].shape
    model = 2 * lanes
    each = hidden_units // 2 // pieces
    few = rows - each
    share = model // each
    half = hidden_units // model // 2
    return placed(
        place_rest_kernel,
        core,
        parts,
        [
            ((model, hidden_units), (each, model), lambda k, i: (lax.rem(i, share), k * half + i // share)),
            ((2 * pieces * few, model), (few, model), lambda k, i: (k * pieces + i, 0)),
        ],
    )


def place_in_kernel(gathered, out):
    model = out.shape[1] // 3
    rows = gathered.shape[5]
    for n in range(2):
        for p in range(2):
            here = pl.ds((2 * n + p) * rows, rows)
            for s in range(3):
                parts = [
                    gathered[0, k, p, q, n, :, s * WIDTH : (s + 1) * WIDTH]
                    for k in range(2)
                    for q in range(2)
                ]
                out[here, s * model : (s + 1) * model] = jnp.concatenate(parts, axis=1).astype(F32)


def placed_in(gathered):
    pieces, *rest = gathered.shape
    rows, width = rest[-2:]
    model = width * MEMBERS // 3
    return pl.pallas_call(
        place_in_kernel,
        grid=(pieces,),
        out_shape=jax.ShapeDtypeStruct((pieces * 4 * rows, 3 * model), F32),
        in_specs=[pl.BlockSpec((1, *rest), lambda i: (i, 0, 0, 0, 0, 0, 0))],
        out_specs=pl.BlockSpec((4 * rows, 3 * model), lambda i: (i, 0)),
        compiler_params=params(),
        cost_estimate=QUICK,
        name="placed_in",
    )(gathered)


def over_cube(value, bit):
    count = lax.axis_size("cube")
    return lax.ppermute(value, "cube", [(i, i ^ (1 << bit)) for i in range(count)])


def over_blk(value, bit):
    return lax.ppermute(value, "blk", [(i, i ^ (1 << bit)) for i in range(MEMBERS)])


def chosen_pairs(is_home, cube_flip, blk_flip):
    pairs = []
    for c in range(lax.axis_size("cube")):
        for b in range(MEMBERS):
            if ((c & 1) == (b >> 1)) == is_home:
                pairs.append((c * MEMBERS + b, (c ^ cube_flip) * MEMBERS + (b ^ blk_flip)))
    return pairs


def sent_between(value, is_home, cube_flip, blk_flip):
    return lax.ppermute(value, ("cube", "blk"), chosen_pairs(is_home, cube_flip, blk_flip))


def exchanged(parts):
    far = over_blk(parts[3], 0)
    near = over_blk(parts[1], 0)
    core = over_cube(parts[2], 0)
    return [parts[0], near, core, over_cube(far, 0)]


def half_of(rows, which, axis=0):
    size = rows.shape[axis] // 2
    return lax.dynamic_slice_in_dim(rows, which * size, size, axis)


def added(first, second):
    return (first.astype(F32) + second.astype(F32)).astype(BF16)


def halved(rows, flag, send, axis=0):
    got = send(half_of(rows, 1 - flag, axis))
    return added(half_of(rows, flag, axis), got)


def joined(own, got, flag, axis=0):
    return jnp.where(
        flag == 0,
        jnp.concatenate([own, got], axis),
        jnp.concatenate([got, own], axis),
    )


def cube_bits():
    return list(range(1, lax.axis_size("cube").bit_length() - 1))


def flag_of(index, bit):
    return (index >> bit) & 1


def summing(keep, send, cube, blk):
    (got,) = yield [(send, lambda v: over_cube(v, 0))]
    bits = cube_bits()
    pieces, rows, lanes = keep.shape
    total = added(keep, got).reshape((2,) * len(bits) + (rows, lanes))
    parts = [total[..., : lanes // 2], total[..., lanes // 2 :]]
    parts = yield from scattered(parts, cube)
    total = jnp.concatenate([p.reshape(2, 2, rows // MEMBERS, lanes // 2) for p in parts], axis=3)
    for bit in range(2):
        flag = flag_of(blk, bit)
        (got,) = yield [(half_of(total, 1 - flag, 1 - bit), functools.partial(over_blk, bit=bit))]
        total = added(half_of(total, flag, 1 - bit), got)
    for bit in (1, 0):
        (got,) = yield [(total, functools.partial(over_blk, bit=bit))]
        total = joined(total, got, flag_of(blk, bit), 1 - bit)
    total = total.reshape((1,) * len(bits) + (rows, lanes))
    parts = [total[..., : lanes // 2], total[..., lanes // 2 :]]
    for steps in zip(bits[::-1], bits):
        got = yield [(part, functools.partial(over_cube, bit=bit)) for part, bit in zip(parts, steps)]
        parts = [
            joined(part, other, flag_of(cube, bit), len(bits) - bit)
            for part, other, bit in zip(parts, got, steps)
        ]
    parts = [part.reshape(pieces, rows, lanes // 2) for part in parts]
    got = yield [(part, lambda v: over_cube(v, 0)) for part in parts]
    return parts + list(got)


def scattered(parts, cube):
    bits = cube_bits()
    for steps in zip(bits, bits[::-1]):
        flags = [flag_of(cube, bit) for bit in steps]
        axes = [len(bits) - bit for bit in steps]
        got = yield [
            (half_of(part, 1 - flag, axis), functools.partial(over_cube, bit=bit))
            for part, flag, axis, bit in zip(parts, flags, axes, steps)
        ]
        parts = [
            added(half_of(part, flag, axis), other)
            for part, flag, axis, other in zip(parts, flags, axes, got)
        ]
    return parts


def summing_columns(parts, cube, blk):
    bits = cube_bits()
    _, rows, lanes = parts[0].shape
    parts = yield from scattered([p.reshape((2,) * len(bits) + (rows, lanes)) for p in parts], cube)
    total = jnp.concatenate([p.reshape(1, 2, rows // 2, lanes) for p in parts])
    flag = flag_of(blk, 1)
    (got,) = yield [(half_of(total, 1 - flag, 1), functools.partial(over_blk, bit=1))]
    return added(half_of(total, flag, 1), got).reshape(2, rows // 2, lanes)


class Order:
    def __init__(self, token):
        self.token = token

    def __call__(self, values):
        values, self.token = lax.optimization_barrier((values, self.token))
        return values


class Running:
    def __init__(self, steps, order):
        self.steps = steps
        self.order = order
        self.result = None
        self.sent(next(steps))

    def sent(self, ready):
        values = self.order([v for v, _ in ready])
        self.arrived = [move(v) for v, (_, move) in zip(values, ready)]

    def step(self):
        arrived = self.order(self.arrived)
        try:
            ready = self.steps.send(arrived)
        except StopIteration as stop:
            self.result = stop.value
        else:
            self.sent(ready)

    def finish(self):
        while self.result is None:
            self.step()
        return self.result


def summing_vectors(rows):
    for bit in range(2):
        (got,) = yield [(rows, functools.partial(over_blk, bit=bit))]
        rows = rows + got
    for bit in range(lax.axis_size("cube").bit_length() - 1):
        (got,) = yield [(rows, functools.partial(over_cube, bit=bit))]
        rows = rows + got
    return rows


def member_columns(matrix, member, axis):
    return lax.dynamic_slice_in_dim(matrix, member * WIDTH, WIDTH, axis)


def body(
    inputs,
    cotangent,
    absent_groups,
    token_group,
    pre_gain,
    pre_shift,
    input_weight,
    input_bias,
    output_weight,
    output_bias,
    mid_gain,
    mid_shift,
    up_weight,
    up_bias,
    down_weight,
    down_bias,
):
    _, rows, model = inputs.shape
    hidden_units = up_weight.shape[1]
    cube, blk = lax.axis_index("cube"), lax.axis_index("blk")
    core = cube & 1
    pieces = lax.axis_size("cube") // 2
    at_home = core == (blk >> 1)
    member = 2 * core + (blk & 1)

    def moved(value):
        return jnp.where(at_home, value, sent_between(value, False, 1, 2))

    group_match = token_group[0][None, :] == jnp.arange(GROUPS, dtype=jnp.int32)[:, None]
    lacking = jnp.sum(jnp.where(group_match, absent_groups.reshape(GROUPS, 1), 0), axis=0)
    valid_here = (1 - lacking).astype(BF16)
    carried = jnp.concatenate(
        [inputs[0], jnp.broadcast_to(jnp.pad(valid_here, (0, model - rows)), (16, model))]
    )
    arriving = sent_between(carried, False, 1, 2)
    near_home = sent_between(carried, True, 0, 1)

    in_columns = jnp.concatenate(
        [member_columns(input_weight[:, s * model : (s + 1) * model], member, 1) for s in range(3)],
        axis=1,
    )
    bias_columns = member_columns(input_bias, member, 1)
    bias_columns = jnp.concatenate([bias_columns[0], jnp.zeros((WIDTH,), F32), bias_columns[1]])
    out_rows = jnp.stack([member_columns(output_weight, member ^ e, 0) for e in range(MEMBERS)])
    prepared = (in_columns, in_columns.T, bias_columns, bias_columns[:, None], out_rows)
    prepared, arriving = lax.optimization_barrier((prepared, arriving))
    in_columns, in_columns_turned, bias_columns, bias_turned, out_rows = prepared

    own = jnp.where(at_home, carried, arriving)
    near = jnp.where(at_home, near_home, sent_between(arriving, False, 0, 1))
    x_blocks = [own, near, over_cube(own, 0), over_cube(near, 0)]

    normed_low, qa, ka, va, qn, kt, vt = project(
        x_blocks, rows, pre_gain, pre_shift, in_columns, in_columns_turned, bias_columns, bias_turned
    )
    qa, cot_here = lax.optimization_barrier((qa, cotangent[0]))
    cot_own = moved(cot_here)
    attended_own, turned, logs = attend(qa, ka, vt)
    attended = exchanged(attended_own)
    (
        layer_here,
        down_send,
        down_keep,
        rest_send,
        rest_keep,
        grad_up_bias,
        grad_hidden,
        *grad_attended,
        middle_vectors,
    ) = middle(
        core,
        blk & 1,
        pieces,
        own,
        attended,
        out_rows,
        output_bias,
        mid_gain,
        mid_shift,
        cot_own,
        down_bias,
        up_weight,
        up_bias,
        down_weight,
    )
    blocks = hidden_units // model
    order = Order(core.astype(jnp.int32)[None])
    down_run = Running(summing(down_keep, down_send, cube, blk), order)
    rest_run = Running(summing(rest_keep, rest_send, cube, blk), order)
    grads_here = exchanged(grad_attended)
    down_run.step()
    rest_run.step()
    columns = []

    def back(head):
        grads = order(grads_here)
        columns.extend(order(attend_back(head, qa, ka, va, qn, kt, turned, logs, grads)))

    back(0)
    down_run.step()
    layer_out = moved(order(layer_here))
    back(1)
    down_run.step()
    rest_run.step()
    back(2)
    down_run.step()
    rest_run.step()
    p0, p1, p2, p3, in_first, in_second, column_total = order(
        unproject(order(columns), normed_low, in_columns, pieces)
    )
    core_far, core_near = over_cube(p3, 0), over_cube(p2, 0)
    in_run = Running(summing_columns([in_first, in_second], cube, blk), order)
    down_run.step()
    core_far, core_near = order((core_far, core_near))
    near_sum, own_sum = order((added(p1, core_far), added(p0, core_near)))
    near_got = over_blk(near_sum, 0)
    in_run.step()
    rest_run.step()
    down_run.step()
    in_run.step()
    rest_run.step()
    down_run.step()
    grad_here, grad_low, grad_pre = order(
        close(own, order([own_sum, near_got]), pre_gain, grad_hidden)
    )
    grad_moved = sent_between(grad_low, False, 1, 2)
    column_total = column_total[0]
    here_bias = jnp.stack([column_total[:WIDTH], column_total[2 * WIDTH :]])
    spread_bias = lax.dynamic_update_slice_in_dim(
        jnp.zeros((2, model), F32), here_bias, member * WIDTH, 1
    )
    vectors = jnp.concatenate(
        [grad_pre, middle_vectors, spread_bias, grad_up_bias.reshape(blocks, model)]
    )
    vector_run = Running(summing_vectors(vectors), order)
    gathered = lax.all_gather(in_run.finish(), ("cube", "blk"))
    rest_run.step()
    vector_run.step()
    down_run.step()
    rest_run.step()
    vector_run.step()
    down_run.step()
    rest_run.step()
    vector_run.step()
    down_run.step()
    (grad_down_weight,) = order([placed_down(order.token, down_run.finish(), hidden_units)])
    rest_run.step()
    vectors = vector_run.finish()
    grad_moved = order(grad_moved)
    input_grad = order(jnp.where(at_home, grad_here, grad_moved.astype(F32)))
    gathered = order(gathered)
    gathered = gathered.reshape((pieces, 2, 2, 2) + in_run.result.shape)
    grad_input_weight = order(placed_in(gathered))
    rest_sum = rest_run.finish()
    grad_up_weight, grad_output_weight = placed_rest(order.token, rest_sum, hidden_units)
    return (
        layer_out[None],
        input_grad[None],
        vectors[0],
        vectors[1],
        grad_input_weight,
        vectors[6:8],
        grad_output_weight,
        vectors[4],
        vectors[2],
        vectors[3],
        grad_up_weight,
        vectors[8:].reshape(-1),
        grad_down_weight,
        vectors[5],
    )


def solution(mesh):
    rows_spec = P("cube", "blk", None)
    return jax.shard_map(
        body,
        mesh=mesh,
        in_specs=(rows_spec, rows_spec, P("cube", None), P("cube", "blk")) + (P(),) * 12,
        out_specs=(rows_spec, rows_spec) + (P(),) * 12,
        check_vma=False,
    )
```

```python
import functools
import jax
import jax.numpy as jnp
from jax import lax
from jax.experimental import pallas as pl
from jax.experimental.pallas import tpu as pltpu
from jax.sharding import PartitionSpec as P

HEADS = 12
HD = 64
GROUPS = 12
MEMBERS = 4
LOCAL_HEADS = HEADS // MEMBERS
WIDTH = LOCAL_HEADS * HD
NEG_FILL = -32768.0
EPSILON = 1e-06
BF16 = jnp.bfloat16
F32 = jnp.float32
TILE = 256
LANES = 128
VMEM = pltpu.VMEM
QUICK = pl.CostEstimate(flops=1, bytes_accessed=1, transcendentals=0)
LONG = pl.CostEstimate(flops=20_000_000_000, bytes_accessed=60_000_000, transcendentals=0)


def dot(left, right):
    return jnp.dot(left, right, preferred_element_type=F32)


def dot_nt(left, right):
    return lax.dot_general(left, right, (((1,), (1,)), ((), ())), preferred_element_type=F32)


def dot_tn(left, right):
    return lax.dot_general(left, right, (((0,), (0,)), ((), ())), preferred_element_type=F32)


def params(limit=60 << 20, **more):
    return pltpu.CompilerParams(vmem_limit_bytes=limit, **more)


def whole(*shape):
    return pl.BlockSpec(shape, lambda *_: (0,) * len(shape))


def normalized(values):
    centered = values - jnp.mean(values, axis=-1, keepdims=True)
    inverse = lax.rsqrt(jnp.mean(centered * centered, axis=-1, keepdims=True) + EPSILON)
    return centered * inverse, inverse


def mask_column(x, rows):
    return x[rows:, :rows].astype(F32).T[:, :1]


def project_kernel(x0, x1, x2, x3, gain, shift, w, wt, bias, bias_col, normed, qa, ka, va, qn, kt, vt):
    rows = normed.shape[0] // MEMBERS
    total = MEMBERS * rows
    padded = qa.shape[2]
    step = rows // 3
    for d, x in enumerate((x0, x1, x2, x3)):

        def some(i, carry, d=d, x=x):
            here = x[pl.ds(i * step, step), :].astype(F32)
            unit, _ = normalized(here)
            normed[pl.ds(d * rows + i * step, step), :] = (unit * gain[...][None] + shift[...][None]).astype(BF16)
            return carry

        lax.fori_loop(0, 3, some, 0)
    for d, x in enumerate((x0, x1, x2, x3)):
        here = pl.ds(d * rows, rows)
        natural = dot(normed[here, :], w[...]) + bias[...][None]
        lane = lax.broadcasted_iota(jnp.int32, (rows, HD), 1)
        low_mask = NEG_FILL * (1.0 - mask_column(x, rows))
        key_tail = jnp.where(lane == 0, low_mask, jnp.where(lane < 4, 1.0, 0.0)).astype(BF16)
        value_tail = jnp.where(lane < 3, 1.0, 0.0).astype(BF16)
        for h in range(LOCAL_HEADS):
            at = h * HD
            qn[h, here, :] = (natural[:, at : at + HD] * HD ** (-0.5)).astype(BF16)
            ka[h, here, :HD] = natural[:, WIDTH + at : WIDTH + at + HD].astype(BF16)
            ka[h, here, HD:] = key_tail
            va[h, here, :HD] = natural[:, 2 * WIDTH + at : 2 * WIDTH + at + HD].astype(BF16)
            va[h, here, HD:] = value_tail
    turned = dot_nt(wt[...], normed[...]) + bias_col[...]
    row = lax.broadcasted_iota(jnp.int32, (HD, padded), 0)
    query_tail = jnp.where(row == 0, 1.0, 0.0).astype(BF16)
    for h in range(LOCAL_HEADS):
        at = h * HD
        qn[h, total:, :] = jnp.zeros((padded - total, HD), BF16)
        qa[h, :HD, :total] = (turned[at : at + HD] * HD ** (-0.5)).astype(BF16)
        qa[h, :HD, total:] = jnp.zeros((HD, padded - total), BF16)
        qa[h, HD:, :] = query_tail
        kt[h] = turned[WIDTH + at : WIDTH + at + HD].astype(BF16)
        vt[h] = turned[2 * WIDTH + at : 2 * WIDTH + at + HD].astype(BF16)


def project(x_blocks, rows, gain, shift, w, wt, bias, bias_col):
    model = x_blocks[0].shape[1]
    total = MEMBERS * rows
    padded = -(-total // TILE) * TILE
    n = LOCAL_HEADS
    outs = [
        jax.ShapeDtypeStruct((total, model), BF16),
        jax.ShapeDtypeStruct((n, 2 * HD, padded), BF16),
        jax.ShapeDtypeStruct((n, total, 2 * HD), BF16),
        jax.ShapeDtypeStruct((n, total, 2 * HD), BF16),
        jax.ShapeDtypeStruct((n, padded, HD), BF16),
        jax.ShapeDtypeStruct((n, HD, total), BF16),
        jax.ShapeDtypeStruct((n, HD, total), BF16),
    ]
    flops = 4 * total * model * 3 * WIDTH
    return pl.pallas_call(
        project_kernel,
        out_shape=outs,
        in_specs=[pl.BlockSpec(memory_space=VMEM)] * 10,
        out_specs=[pl.BlockSpec(memory_space=VMEM)] * len(outs),
        compiler_params=params(),
        cost_estimate=LONG,
        name="project",
    )(*x_blocks, gain, shift, w, wt, bias, bias_col)


def forward_kernel(qa, ka, vt, l0, l1, l2, l3, turned, logs, held, even, odd):
    head = pl.program_id(0)
    rows = l0.shape[0]
    tiles = qa.shape[2] // TILE

    def scored(i, out):
        here = pl.ds(pl.multiple_of(i * TILE, TILE), TILE)
        out[...] = dot(ka[0], qa[0, :, here])

    def mixed_of(i, scores):
        here = pl.ds(pl.multiple_of(i * TILE, TILE), TILE)
        peak = jnp.max(scores[...], axis=0, keepdims=True)
        weights = jnp.exp(scores[...] - peak)
        sums = jnp.sum(weights, axis=0, keepdims=True)
        mixed = dot(vt[0], weights.astype(BF16)) * (1.0 / sums)
        turned[0, :, here] = mixed
        logs[0, :, here] = peak + jnp.log(sums)
        held[here, :] = mixed.T.astype(BF16)

    scored(0, even)

    def pair(i, carry):
        scored(2 * i + 1, odd)
        mixed_of(2 * i, even)
        scored(jnp.minimum(2 * i + 2, tiles - 1), even)
        mixed_of(2 * i + 1, odd)
        return carry

    lax.fori_loop(0, tiles // 2, pair, 0)
    if tiles % 2:
        mixed_of(tiles - 1, even)
    for h in range(LOCAL_HEADS):

        @pl.when(head == h)
        def _(h=h):
            for d, low in enumerate((l0, l1, l2, l3)):
                low[:, h * HD : (h + 1) * HD] = held[d * rows : (d + 1) * rows, :]


def attend(qa, ka, vt):
    n, total, _ = ka.shape
    padded = qa.shape[2]
    rows = total // MEMBERS
    per_head = lambda *shape: pl.BlockSpec((1,) + shape, lambda h: (h, 0, 0))
    *low, turned, logs = pl.pallas_call(
        forward_kernel,
        grid=(n,),
        out_shape=[jax.ShapeDtypeStruct((rows, WIDTH), BF16)] * MEMBERS
        + [
            jax.ShapeDtypeStruct((n, HD, padded), F32),
            jax.ShapeDtypeStruct((n, 1, padded), F32),
        ],
        in_specs=[per_head(2 * HD, padded), per_head(total, 2 * HD), per_head(HD, total)],
        out_specs=[whole(rows, WIDTH)] * MEMBERS + [per_head(HD, padded), per_head(1, padded)],
        scratch_shapes=[VMEM((padded, HD), BF16), VMEM((total, TILE), F32), VMEM((total, TILE), F32)],
        compiler_params=params(),
        cost_estimate=LONG,
        name="attend",
    )(qa, ka, vt)
    return low, turned, logs


def three_parts(row):
    high = row.astype(BF16).astype(F32)
    rest = row - high
    middle = rest.astype(BF16).astype(F32)
    return high, middle, rest - middle


def backward_kernel(head, qa, ka, va, qn, kt, turned, logs, g0, g1, g2, g3, out_q, out_k, out_v, held_g, sum_k, sum_v):
    rows = g0.shape[0]
    total = ka.shape[1]
    padded = qa.shape[2]
    tiles = padded // TILE
    for d, part in enumerate((g0, g1, g2, g3)):
        held_g[d * rows : (d + 1) * rows, :] = part[:, head * HD : (head + 1) * HD]
    held_g[total:, :] = jnp.zeros((padded - total, HD), BF16)
    sum_k[...] = jnp.zeros_like(sum_k)
    sum_v[...] = jnp.zeros_like(sum_v)
    row = lax.broadcasted_iota(jnp.int32, (HD, TILE), 0)

    def some(i, width):
        here = pl.ds(pl.multiple_of(i * TILE, TILE), TILE)
        grad = held_g[here, :]
        grad_turned = grad.astype(F32).T
        delta = jnp.sum(grad_turned * turned[0, :, here], axis=0, keepdims=True)
        high, middle, least = three_parts(-logs[0, :, here])
        tail = jnp.where(row == 0, 1.0, jnp.where(row == 1, high, jnp.where(row == 2, middle, jnp.where(row == 3, least, 0.0))))
        query = jnp.concatenate([qa[0, :HD, here], tail.astype(BF16)], axis=0)
        probs = jnp.exp(dot(ka[0], query))
        high, middle, least = three_parts(-delta)
        tail = jnp.where(row == 0, high, jnp.where(row == 1, middle, jnp.where(row == 2, least, 0.0)))
        grad_tail = jnp.concatenate([grad_turned, tail], axis=0).astype(BF16)
        grad_scores = (probs * dot(va[0], grad_tail)).astype(BF16)
        sum_v[...] += dot(probs.astype(BF16), grad)
        sum_k[...] += dot(grad_scores, qn[0, here, :])
        query_grad = dot(kt[0], grad_scores) * HD ** (-0.5)
        out_q[pl.ds(pl.multiple_of(i * TILE, TILE), width), :] = query_grad.T.astype(BF16)[:width]

    def full(i, carry):
        some(i, TILE)
        return carry

    lax.fori_loop(0, tiles - 1, full, 0)
    some(tiles - 1, total - (tiles - 1) * TILE)
    out_k[...] = sum_k[...].astype(BF16)
    out_v[...] = sum_v[...].astype(BF16)


def attend_back(head, qa, ka, va, qn, kt, turned, logs, grads):
    n, total, _ = ka.shape
    padded = qa.shape[2]
    rows = grads[0].shape[0]
    per_head = lambda *shape: pl.BlockSpec((1,) + shape, lambda i: (head, 0, 0))
    return pl.pallas_call(
        functools.partial(backward_kernel, head),
        grid=(1,),
        out_shape=[jax.ShapeDtypeStruct((total, HD), BF16)] * 3,
        in_specs=[
            per_head(2 * HD, padded),
            per_head(total, 2 * HD),
            per_head(total, 2 * HD),
            per_head(padded, HD),
            per_head(HD, total),
            per_head(HD, padded),
            per_head(1, padded),
        ]
        + [whole(rows, WIDTH)] * MEMBERS,
        out_specs=[whole(total, HD)] * 3,
        scratch_shapes=[
            VMEM((padded, HD), BF16),
            VMEM((total, HD), F32),
            VMEM((total, HD), F32),
        ],
        compiler_params=params(),
        cost_estimate=LONG,
        name="attend_back",
    )(qa, ka, va, qn, kt, turned, logs, *grads)


def unproject_kernel(where, *refs):
    columns, normed, w = refs[:9], refs[9], refs[10]
    n0, n1, n2, n3, a_send, a_keep, b_send, b_keep, sums, joint, grad = refs[11:]
    rows = n0.shape[0]
    for s in range(3):
        for h in range(LOCAL_HEADS):
            at = s * WIDTH + h * HD
            joint[:, at : at + HD] = columns[3 * h + s][...]
    for d, out in enumerate((n0, n1, n2, n3)):
        out[...] = dot_nt(joint[d * rows : (d + 1) * rows, :], w[...]).astype(BF16)
    whole_grad = dot_tn(joint[...], normed[...])
    count, each, model = grad.shape
    for i in range(count):
        grad[i] = whole_grad[i * each : (i + 1) * each]
    pieces = count // 2
    for r in range(pieces):
        for p in range(2):
            part = grad[(r ^ where[1]) * 2 + (p ^ (where[2] // 2))].astype(BF16)
            out = (a_keep, a_send)[r % 2]
            out[r // 2, p] = part[:, : model // 2]
            out = (b_keep, b_send)[2 * r // pieces]
            out[r % (pieces // 2), p] = part[:, model // 2 :]
    total = jnp.sum(joint[...].astype(F32), axis=0, keepdims=True)
    sums[...] = jnp.zeros_like(sums)
    for m in range(MEMBERS):

        @pl.when(2 * where[0] + where[2] % 2 == m)
        def _(m=m):
            sums[0:1, m * WIDTH : (m + 1) * WIDTH] = total[:, :WIDTH]
            sums[1:2, m * WIDTH : (m + 1) * WIDTH] = total[:, 2 * WIDTH :]


def unproject(where, columns, normed, w, pieces):
    total, model = normed.shape
    rows = total // MEMBERS
    width = 3 * WIDTH
    each = width // pieces // 2
    shaped = jax.ShapeDtypeStruct
    outs = [shaped((rows, model), BF16)] * MEMBERS
    outs += [shaped((pieces // 2, 2, each, model // 2), BF16)] * 4 + [shaped((2, model), F32)]
    return pl.pallas_call(
        unproject_kernel,
        out_shape=outs,
        in_specs=[pl.BlockSpec(memory_space=pltpu.SMEM)] + [pl.BlockSpec(memory_space=VMEM)] * 11,
        out_specs=[pl.BlockSpec(memory_space=VMEM)] * len(outs),
        scratch_shapes=[VMEM((total, width), BF16), VMEM((2 * pieces, each, model), F32)],
        compiler_params=params(),
        cost_estimate=LONG,
        name="unproject",
    )(where, *columns, normed, w)


def close_kernel(x, p0, p1, gain, hidden, grad, low, vectors):
    rows = hidden.shape[0]
    unit, inverse = normalized(x[:rows, :].astype(F32))
    given = p0[...].astype(F32) + p1[...].astype(F32)
    vectors[0:1, :] = jnp.sum(given * unit, axis=0, keepdims=True)
    vectors[1:2, :] = jnp.sum(given, axis=0, keepdims=True)
    scaled = given * gain[...][None]
    inner = scaled - jnp.mean(scaled, axis=-1, keepdims=True)
    inner = inner - unit * jnp.mean(scaled * unit, axis=-1, keepdims=True)
    total = hidden[...] + inverse * inner
    grad[...] = total
    low[...] = total.astype(BF16)


def close(x, parts, gain, hidden):
    rows, model = hidden.shape
    shaped = jax.ShapeDtypeStruct
    return pl.pallas_call(
        close_kernel,
        out_shape=[shaped((rows, model), F32), shaped((rows, model), BF16), shaped((2, model), F32)],
        in_specs=[pl.BlockSpec(memory_space=VMEM)] * 5,
        out_specs=[pl.BlockSpec(memory_space=VMEM)] * 3,
        compiler_params=params(),
        cost_estimate=LONG,
        name="close",
    )(x, *parts, gain, hidden)


def middle_kernel(
    side, x, a0, a1, a2, a3, wo, out_bias, gain, shift, cot, down_bias, up, up_bias, down,
    layer, down_send, down_keep, rest_send, rest_keep, grad_up_bias, grad_hidden, g0, g1, g2, g3, vectors,
    hidden, normed, grad_down, total_out, total_grad, valid,
):
    step = pl.program_id(0)
    last = pl.num_programs(0) - 1
    half = pl.num_programs(0) // 2
    rows, model = cot.shape
    pieces = down_keep.shape[0]
    each = half * model // pieces
    share = model // each

    @pl.when(step == 0)
    def _():
        valid[...] = mask_column(x, rows)
        value = x[:rows, :].astype(F32) + out_bias[...][None]
        for e, part in enumerate((a0, a1, a2, a3)):
            value += dot(part[...], wo[e])
        hidden[...] = value
        unit, _ = normalized(value)
        normed[...] = (unit * gain[...][None] + shift[...][None]).astype(BF16)
        low = (valid[...] * cot[...].astype(F32)).astype(BF16)
        grad_down[...] = low
        vectors[3:4, :] = jnp.sum(low.astype(F32), axis=0, keepdims=True)
        total_out[...] = value + down_bias[...][None]
        total_grad[...] = jnp.zeros_like(total_grad)

    gate = dot(normed[...], up[...]) + up_bias[0]
    below = 0.5 * (1.0 + lax.erf(gate * (0.5**0.5)))
    active = (gate * below).astype(BF16)
    slope = below + gate * (jnp.exp(-0.5 * gate * gate) * (0.5 / jnp.pi) ** 0.5)
    low = grad_down[...]
    grad_gate = (dot_nt(low, down[...]) * slope).astype(BF16)
    total_out[...] += dot(active, down[...])
    total_grad[...] += dot_nt(grad_gate, up[...])
    grad_up_bias[0] = jnp.sum(grad_gate.astype(F32), axis=0, keepdims=True)
    of_down = dot_tn(active, low).astype(BF16)
    of_up = dot_tn(normed[...], grad_gate).astype(BF16)
    few = each // MEMBERS
    for i in range(2 * half):

        @pl.when(step == i)
        def _(i=i):
            down_held, rest_held = (down_send, rest_send) if i < half else (down_keep, rest_keep)
            for j in range(share):
                piece = ((i % half) * share + j) ^ side[1]
                for z in range(MEMBERS):
                    at = j * each + z * few
                    down_held[piece, z ^ side[2]] = of_down[at : at + few]
                    rest_held[piece, z ^ side[2], :few, :] = of_up[at : at + few]

    @pl.when(step == last)
    def _():
        unit, inverse = normalized(hidden[...])
        layer[...] = (valid[...] * total_out[...]).astype(BF16)
        grad = total_grad[...]
        vectors[0:1, :] = jnp.sum(grad * unit, axis=0, keepdims=True)
        vectors[1:2, :] = jnp.sum(grad, axis=0, keepdims=True)
        scaled = grad * gain[...][None]
        inner = scaled - jnp.mean(scaled, axis=-1, keepdims=True)
        inner = inner - unit * jnp.mean(scaled * unit, axis=-1, keepdims=True)
        grad = grad_down[...].astype(F32) + inverse * inner
        grad_hidden[...] = grad
        branch = grad.astype(BF16)
        vectors[2:3, :] = jnp.sum(branch.astype(F32), axis=0, keepdims=True)
        parts = (a0, a1, a2, a3)
        count = pieces // 2
        some = WIDTH // count // MEMBERS
        for e, given in enumerate((g0, g1, g2, g3)):
            given[...] = dot_nt(branch, wo[e]).astype(BF16)
            held = rest_keep if e < 2 else rest_send
            place = ((side[2] % 2) ^ (e & 1)) * count
            of_out = dot_tn(parts[e][...], branch).astype(BF16)
            for j in range(count):
                for z in range(MEMBERS):
                    at = (j * MEMBERS + z) * some
                    held[(place + j) ^ side[1], z ^ side[2], few:, :] = of_out[at : at + some]


def middle(where, pieces, x, attended, wo, out_bias, gain, shift, cot, down_bias, up, up_bias, down):
    rows, model = cot.shape
    blocks = up.shape[1] // model
    half = blocks // 2

    def block_of(i, side):
        return lax.rem(i, half) + half * jnp.where(i < half, 1 - side[0], side[0])

    whole_s = lambda *shape: pl.BlockSpec(shape, lambda i, side: (0,) * len(shape))
    each = half * model // pieces // MEMBERS
    held = (pieces, MEMBERS, each, model)
    rest = (pieces, MEMBERS, each + 2 * WIDTH // pieces // MEMBERS, model)
    shaped = jax.ShapeDtypeStruct
    outs = [
        (shaped((rows, model), BF16), whole_s(rows, model)),
        (shaped(held, BF16), whole_s(*held)),
        (shaped(held, BF16), whole_s(*held)),
        (shaped(rest, BF16), whole_s(*rest)),
        (shaped(rest, BF16), whole_s(*rest)),
        (shaped((blocks, 1, model), F32), pl.BlockSpec((1, 1, model), lambda i, side: (block_of(i, side), 0, 0))),
        (shaped((rows, model), F32), whole_s(rows, model)),
    ]
    outs += [(shaped((rows, WIDTH), BF16), whole_s(rows, WIDTH))] * MEMBERS
    outs += [(shaped((4, model), F32), whole_s(4, model))]
    return pl.pallas_call(
        middle_kernel,
        out_shape=[o[0] for o in outs],
        grid_spec=pltpu.PrefetchScalarGridSpec(
            num_scalar_prefetch=1,
            grid=(blocks,),
            in_specs=[whole_s(*x.shape)]
            + [whole_s(rows, WIDTH)] * MEMBERS
            + [whole_s(MEMBERS, WIDTH, model)]
            + [whole_s(model)] * 3
            + [whole_s(rows, model), whole_s(model)]
            + [
                pl.BlockSpec((model, model), lambda i, side: (0, block_of(i, side))),
                pl.BlockSpec((1, 1, model), lambda i, side: (block_of(i, side), 0, 0)),
                pl.BlockSpec((model, model), lambda i, side: (block_of(i, side), 0)),
            ],
            out_specs=[o[1] for o in outs],
            scratch_shapes=[
                VMEM((rows, model), F32),
                VMEM((rows, model), BF16),
                VMEM((rows, model), BF16),
                VMEM((rows, model), F32),
                VMEM((rows, model), F32),
                VMEM((rows, 1), F32),
            ],
        ),
        compiler_params=params(),
        cost_estimate=LONG,
        name="middle",
    )(
        where,
        x, *attended, wo, out_bias, gain, shift, cot, down_bias,
        up, up_bias.reshape(blocks, 1, model), down,
    )


def reversed_bits(index, count):
    bits = count.bit_length() - 1
    total = 0
    for bit in range(bits):
        total = total | (((index >> bit) & 1) << (bits - 1 - bit))
    return total


def streamed(steps):
    for ins, _, _ in steps:
        for copy in ins:
            copy.start()
    for ins, compute, outs in steps:
        for copy in ins:
            copy.wait()
        compute()
        for copy in outs:
            copy.start()
    for _, _, outs in steps:
        for copy in outs:
            copy.wait()


def place_kernel(where, a0, b0, a1, b1, *refs):
    pieces, _, few, lanes = a0.shape
    count = (len(refs) - 2) // 2
    outs, held_in, held, (sem_in, sem_out) = refs[:count], refs[count], refs[count + 1 : -2], refs[-2:]
    model = 2 * lanes
    if count == 1:
        each = few * MEMBERS
        cuts = [(0, few)]
    else:
        each = outs[1].shape[0] // 2 // pieces
        cuts = [(0, few - each // MEMBERS), (few - each // MEMBERS, each // MEMBERS)]
    steps = []
    for n, parts in enumerate(((a0, b0), (a1, b1))):
        half = n ^ where[0]
        for r in range(pieces):
            slot = n * pieces + r
            piece = r ^ where[1]
            ins = [
                pltpu.make_async_copy(part.at[at], held_in.at[slot, i], sem_in.at[slot, i])
                for i, (part, at) in enumerate(zip(parts, (reversed_bits(r, pieces), r)))
            ]

            def compute(slot=slot):
                for z in range(MEMBERS):
                    given = reversed_bits(z ^ where[2], MEMBERS)
                    for i in range(2):
                        for out, (start, size) in zip(held, cuts):
                            value = held_in[slot, i, given, start : start + size, :]
                            out[slot, z * size : (z + 1) * size, i * lanes : (i + 1) * lanes] = value.astype(F32)

            places = []
            for out, (_, size) in zip(outs, cuts):
                rows = size * MEMBERS
                if out.shape[1] == model:
                    places.append(out.at[pl.ds((half * pieces + piece) * rows, rows)])
                else:
                    share = model // rows
                    column = half * (out.shape[1] // model // 2) + piece // share
                    places.append(
                        out.at[
                            pl.ds(lax.rem(piece, share) * rows, rows),
                            pl.ds(pl.multiple_of(column * model, model), model),
                        ]
                    )
            sends = [
                pltpu.make_async_copy(given.at[slot], place, sem_out.at[slot, i])
                for i, (given, place) in enumerate(zip(held, places))
            ]
            steps.append((ins, compute, sends))
    streamed(steps)


def placed(where, parts, shapes):
    pieces, _, few, lanes = parts[0].shape
    count = len(shapes)
    sizes = [shape[0] * shape[1] // (2 * lanes) // 2 // pieces for shape in shapes]
    return pl.pallas_call(
        place_kernel,
        out_shape=[jax.ShapeDtypeStruct(shape, F32) for shape in shapes],
        in_specs=[pl.BlockSpec(memory_space=pltpu.SMEM)] + [pl.BlockSpec(memory_space=pl.ANY)] * 4,
        out_specs=[pl.BlockSpec(memory_space=pl.ANY)] * count,
        scratch_shapes=[VMEM((2 * pieces, 2, MEMBERS, few, lanes), BF16)]
        + [VMEM((2 * pieces, size, 2 * lanes), F32) for size in sizes]
        + [pltpu.SemaphoreType.DMA((2 * pieces, 2)), pltpu.SemaphoreType.DMA((2 * pieces, count))],
        compiler_params=params(),
        cost_estimate=LONG,
        name="placed",
    )(where, *parts)


def placed_down(where, parts, hidden_units):
    return placed(where, parts, [(hidden_units, 2 * parts[0].shape[3])])


def placed_rest(where, parts, hidden_units):
    model = 2 * parts[0].shape[3]
    return placed(where, parts, [(model, hidden_units), (model, model)])


def place_in_kernel(where, a0, b0, a1, b1, out, held):
    pieces, _, each, lanes = a0.shape
    model = 2 * lanes
    for half, (first, second) in enumerate(((a0, b0), (a1, b1))):
        for r in range(pieces):
            for z in range(MEMBERS):
                at = reversed_bits(z, MEMBERS)
                piece, side = r ^ where[1], z ^ where[2]
                member = 2 * (half ^ where[0]) + side % 2
                place = piece * 2 + side // 2
                held[member, place, :, :lanes] = first[reversed_bits(r, pieces), at].astype(F32)
                held[member, place, :, lanes:] = second[r, at].astype(F32)
    for m in range(MEMBERS):
        columns = held[m].reshape(3 * WIDTH, model)
        for s in range(3):
            at = s * model + m * WIDTH
            out[:, at : at + WIDTH] = columns[s * WIDTH : (s + 1) * WIDTH].T


def placed_in(where, parts):
    pieces, _, rows, lanes = parts[0].shape
    model = 2 * lanes
    return pl.pallas_call(
        place_in_kernel,
        out_shape=jax.ShapeDtypeStruct((model, 3 * model), F32),
        in_specs=[pl.BlockSpec(memory_space=pltpu.SMEM)] + [pl.BlockSpec(memory_space=VMEM)] * 4,
        out_specs=pl.BlockSpec(memory_space=VMEM),
        scratch_shapes=[VMEM((MEMBERS, 2 * pieces, rows, model), F32)],
        compiler_params=params(),
        cost_estimate=LONG,
        name="placed_in",
    )(where, *parts)


def plus(first, second):
    return (first.astype(F32) + second.astype(F32)).astype(BF16)


def fold_core_kernel(keep, got, a_send, a_keep, b_send, b_keep, held, held_got, held_out, sem_in, sem_out):
    pieces, _, _, lanes = keep.shape
    steps = []
    for p in range(pieces):
        ins = [
            pltpu.make_async_copy(keep.at[p], held.at[p], sem_in.at[p, 0]),
            pltpu.make_async_copy(got.at[p], held_got.at[p], sem_in.at[p, 1]),
        ]

        def compute(p=p):
            total = plus(held[p], held_got[p])
            held_out[p, 0] = total[:, :, : lanes // 2]
            held_out[p, 1] = total[:, :, lanes // 2 :]

        first = (a_keep, a_send)[p % 2].at[p // 2]
        second = (b_keep, b_send)[2 * p // pieces].at[p % (pieces // 2)]
        outs = [
            pltpu.make_async_copy(held_out.at[p, i], place, sem_out.at[p, i])
            for i, place in enumerate((first, second))
        ]
        steps.append((ins, compute, outs))
    streamed(steps)


def fold_core(keep, got):
    pieces, quarters, rows, lanes = keep.shape
    half = (quarters, rows, lanes // 2)
    return pl.pallas_call(
        fold_core_kernel,
        out_shape=[jax.ShapeDtypeStruct((pieces // 2, *half), BF16)] * 4,
        in_specs=[pl.BlockSpec(memory_space=pl.ANY)] * 2,
        out_specs=[pl.BlockSpec(memory_space=pl.ANY)] * 4,
        scratch_shapes=[
            VMEM(keep.shape, BF16),
            VMEM(keep.shape, BF16),
            VMEM((pieces, 2, *half), BF16),
            pltpu.SemaphoreType.DMA((pieces, 2)),
            pltpu.SemaphoreType.DMA((pieces, 2)),
        ],
        compiler_params=params(),
        cost_estimate=QUICK,
        name="fold_core",
    )(keep, got)


def in_vmem(kernel, outs, *values, name):
    return pl.pallas_call(
        kernel,
        out_shape=outs,
        in_specs=[pl.BlockSpec(memory_space=VMEM)] * len(values),
        out_specs=[pl.BlockSpec(memory_space=VMEM)] * len(outs),
        compiler_params=params(),
        cost_estimate=QUICK,
        name=name,
    )(*values)


def fold_planes_kernel(ak, ag, bk, bg, a_send, a_keep, b_send, b_keep):
    count = ak.shape[0]
    for r in range(count):
        out = (a_keep, a_send)[r % 2]
        out[r // 2] = plus(ak[r], ag[r])
        out = (b_keep, b_send)[2 * r // count]
        out[r % (count // 2)] = plus(bk[r], bg[r])


def fold_last_kernel(ak, ag, bk, bg, send, keep):
    quarters = ak.shape[1]
    lanes = ak.shape[3]
    for z in range(quarters):
        out = (keep, send)[z % 2]
        out[z // 2, :, :lanes] = plus(ak[0, z], ag[0, z])
        out[z // 2, :, lanes:] = plus(bk[0, z], bg[0, z])


def fold_planes(ak, ag, bk, bg):
    count, quarters, rows, lanes = ak.shape
    if count > 1:
        outs = [jax.ShapeDtypeStruct((count // 2, quarters, rows, lanes), BF16)] * 4
        return in_vmem(fold_planes_kernel, outs, ak, ag, bk, bg, name="fold_planes")
    outs = [jax.ShapeDtypeStruct((quarters // 2, rows, 2 * lanes), BF16)] * 2
    return in_vmem(fold_last_kernel, outs, ak, ag, bk, bg, name="fold_last")


def fold_quarters_kernel(keep, got, *outs):
    for z in range(keep.shape[0]):
        out = outs[len(outs) - 1 - z]
        out[...] = plus(keep[z], got[z])


def fold_quarters(keep, got):
    count, rows, lanes = keep.shape
    outs = [jax.ShapeDtypeStruct((rows, lanes), BF16)] * count
    return in_vmem(fold_quarters_kernel, outs, keep, got, name="fold_quarters")


def over_cube(value, bit):
    count = lax.axis_size("cube")
    return lax.ppermute(value, "cube", [(i, i ^ (1 << bit)) for i in range(count)])


def over_blk(value, bit):
    return lax.ppermute(value, "blk", [(i, i ^ (1 << bit)) for i in range(MEMBERS)])


def chosen_pairs(is_home, cube_flip, blk_flip):
    pairs = []
    for c in range(lax.axis_size("cube")):
        for b in range(MEMBERS):
            if ((c & 1) == (b >> 1)) == is_home:
                pairs.append((c * MEMBERS + b, (c ^ cube_flip) * MEMBERS + (b ^ blk_flip)))
    return pairs


def sent_between(value, is_home, cube_flip, blk_flip):
    return lax.ppermute(value, ("cube", "blk"), chosen_pairs(is_home, cube_flip, blk_flip))


def exchanged(parts):
    far = over_blk(parts[3], 0)
    near = over_blk(parts[1], 0)
    core = over_cube(parts[2], 0)
    return [parts[0], near, core, over_cube(far, 0)]


def cube_bits():
    return list(range(1, lax.axis_size("cube").bit_length() - 1))


def by_cube(bit):
    return functools.partial(over_cube, bit=bit)


def by_blk(bit):
    return functools.partial(over_blk, bit=bit)


def scattering(a_send, a_keep, b_send, b_keep):
    for low, high in zip(cube_bits(), cube_bits()[::-1]):
        a_got, b_got = yield [(a_send, by_cube(low)), (b_send, by_cube(high))]
        *folded, = fold_planes(a_keep, a_got, b_keep, b_got)
        if len(folded) == 2:
            return folded
        a_send, a_keep, b_send, b_keep = folded


def spreading(shard):
    (got,) = yield [(shard, by_blk(1))]
    both = jnp.stack([shard, got])
    (got,) = yield [(both, by_blk(0))]
    both = jnp.concatenate([both, got])[None]
    lanes = both.shape[3] // 2
    a_part, b_part = both[..., :lanes], both[..., lanes:]
    for low, high in zip(cube_bits(), cube_bits()[::-1]):
        a_got, b_got = yield [(a_part, by_cube(high)), (b_part, by_cube(low))]
        a_part, b_part = jnp.concatenate([a_part, a_got]), jnp.concatenate([b_part, b_got])
    got = yield [(a_part, by_cube(0)), (b_part, by_cube(0))]
    return [a_part, b_part, *got]


def summing(keep, send):
    (got,) = yield [(send, by_cube(0))]
    send, keep = yield from scattering(*fold_core(keep, got))
    (got,) = yield [(send, by_blk(0))]
    send, keep = fold_quarters(keep, got)
    (got,) = yield [(send, by_blk(1))]
    return (yield from spreading(plus(keep, got)))


def summing_columns(parts):
    send, keep = yield from scattering(*parts)
    (got,) = yield [(send, by_blk(1))]
    return (yield from spreading(plus(keep[0], got[0])))


def summing_vectors(rows):
    for bit in range(2):
        (got,) = yield [(rows, by_blk(bit))]
        rows = rows + got
    for bit in range(lax.axis_size("cube").bit_length() - 1):
        (got,) = yield [(rows, by_cube(bit))]
        rows = rows + got
    return rows


class Order:
    def __init__(self, token):
        self.token = token

    def __call__(self, values):
        values, self.token = lax.optimization_barrier((values, self.token))
        return values


class Running:
    def __init__(self, steps, order):
        self.steps = steps
        self.order = order
        self.result = None
        self.sent(next(steps))

    def sent(self, ready):
        values = self.order([v for v, _ in ready])
        self.arrived = [move(v) for v, (_, move) in zip(values, ready)]

    def step(self):
        arrived = self.order(self.arrived)
        try:
            ready = self.steps.send(arrived)
        except StopIteration as stop:
            self.result = stop.value
        else:
            self.sent(ready)

    def finish(self):
        while self.result is None:
            self.step()
        return self.result


def member_columns(matrix, member, axis):
    return lax.dynamic_slice_in_dim(matrix, member * WIDTH, WIDTH, axis)


def body(
    inputs,
    cotangent,
    absent_groups,
    token_group,
    pre_gain,
    pre_shift,
    input_weight,
    input_bias,
    output_weight,
    output_bias,
    mid_gain,
    mid_shift,
    up_weight,
    up_bias,
    down_weight,
    down_bias,
):
    _, rows, model = inputs.shape
    hidden_units = up_weight.shape[1]
    cube, blk = lax.axis_index("cube"), lax.axis_index("blk")
    core = cube & 1
    pieces = lax.axis_size("cube") // 2
    where = jnp.stack([core, cube >> 1, blk]).astype(jnp.int32)
    at_home = core == (blk >> 1)
    member = 2 * core + (blk & 1)

    def moved(value):
        return jnp.where(at_home, value, sent_between(value, False, 1, 2))

    group_match = token_group[0][None, :] == jnp.arange(GROUPS, dtype=jnp.int32)[:, None]
    lacking = jnp.sum(jnp.where(group_match, absent_groups.reshape(GROUPS, 1), 0), axis=0)
    valid_here = (1 - lacking).astype(BF16)
    carried = jnp.concatenate(
        [inputs[0], jnp.broadcast_to(jnp.pad(valid_here, (0, model - rows)), (16, model))]
    )
    arriving = sent_between(carried, False, 1, 2)
    near_home = sent_between(carried, True, 0, 1)

    in_columns = jnp.concatenate(
        [member_columns(input_weight[:, s * model : (s + 1) * model], member, 1) for s in range(3)],
        axis=1,
    )
    bias_columns = member_columns(input_bias, member, 1)
    bias_columns = jnp.concatenate([bias_columns[0], jnp.zeros((WIDTH,), F32), bias_columns[1]])
    out_rows = jnp.stack([member_columns(output_weight, member ^ e, 0) for e in range(MEMBERS)])
    prepared = (in_columns, in_columns.T, bias_columns, bias_columns[:, None], out_rows)
    prepared, arriving = lax.optimization_barrier((prepared, arriving))
    in_columns, in_columns_turned, bias_columns, bias_turned, out_rows = prepared

    own = jnp.where(at_home, carried, arriving)
    near = jnp.where(at_home, near_home, sent_between(arriving, False, 0, 1))
    x_blocks = [own, near, over_cube(own, 0), over_cube(near, 0)]

    normed_low, qa, ka, va, qn, kt, vt = project(
        x_blocks, rows, pre_gain, pre_shift, in_columns, in_columns_turned, bias_columns, bias_turned
    )
    qa, cot_here = lax.optimization_barrier((qa, cotangent[0]))
    cot_own = moved(cot_here)
    attended_own, turned, logs = attend(qa, ka, vt)
    attended = exchanged(attended_own)
    (
        layer_here,
        down_send,
        down_keep,
        rest_send,
        rest_keep,
        grad_up_bias,
        grad_hidden,
        *grad_attended,
        middle_vectors,
    ) = middle(
        where,
        pieces,
        own,
        attended,
        out_rows,
        output_bias,
        mid_gain,
        mid_shift,
        cot_own,
        down_bias,
        up_weight,
        up_bias,
        down_weight,
    )
    blocks = hidden_units // model
    order = Order(where)
    down_run = Running(summing(down_keep, down_send), order)
    rest_run = Running(summing(rest_keep, rest_send), order)
    far, near = order((over_blk(grad_attended[3], 0), over_blk(grad_attended[1], 0)))
    core_parts = (over_cube(grad_attended[2], 0), over_cube(far, 0))
    down_run.step()
    rest_run.step()
    grads_here = [grad_attended[0], near, *order(core_parts)]
    columns = []

    def back(head):
        grads = order(grads_here)
        columns.extend(order(attend_back(head, qa, ka, va, qn, kt, turned, logs, grads)))

    back(0)
    down_run.step()
    layer_moved = sent_between(order(layer_here), False, 1, 2)
    back(1)
    down_run.step()
    rest_run.step()
    back(2)
    layer_out = jnp.where(at_home, layer_here, order(layer_moved))
    down_run.step()
    rest_run.step()
    p0, p1, p2, p3, *in_parts, biases = order(
        unproject(where, order(columns), normed_low, in_columns, pieces)
    )
    in_run = Running(summing_columns(in_parts), order)
    core_far, core_near = over_cube(p3, 0), over_cube(p2, 0)
    down_run.step()
    rest_run.step()
    in_run.step()
    near_sum, own_sum = order((plus(p1, order(core_far)), plus(p0, core_near)))
    down_run.step()
    in_run.step()
    rest_run.step()
    near_got = over_blk(near_sum, 0)
    down_run.step()
    in_run.step()
    rest_run.step()
    down_run.step()
    in_run.step()
    rest_run.step()
    down_run.step()
    grad_here, grad_low, grad_pre = order(
        close(own, order([own_sum, near_got]), pre_gain, grad_hidden)
    )
    grad_moved = sent_between(grad_low, False, 1, 2)
    vector_run = Running(
        summing_vectors(
            jnp.concatenate([grad_pre, middle_vectors, biases, grad_up_bias.reshape(blocks, model)])
        ),
        order,
    )
    in_run.step()
    rest_run.step()
    vector_run.step()
    (grad_down_weight,) = order(placed_down(order.token, down_run.finish(), hidden_units))
    vector_run.step()
    rest_run.step()
    in_run.step()
    vector_run.step()
    input_grad = order(jnp.where(at_home, grad_here, order(grad_moved).astype(F32)))
    rest_sum = rest_run.finish()
    vector_run.step()
    in_run.step()
    vectors = vector_run.finish()
    grad_up_weight, grad_output_weight = order(placed_rest(order.token, rest_sum, hidden_units))
    grad_input_weight = placed_in(order.token, in_run.finish())
    return (
        layer_out[None],
        input_grad[None],
        vectors[0],
        vectors[1],
        grad_input_weight,
        vectors[6:8],
        grad_output_weight,
        vectors[4],
        vectors[2],
        vectors[3],
        grad_up_weight,
        vectors[8:].reshape(-1),
        grad_down_weight,
        vectors[5],
    )


def solution(mesh):
    rows_spec = P("cube", "blk", None)
    return jax.shard_map(
        body,
        mesh=mesh,
        in_specs=(rows_spec, rows_spec, P("cube", None), P("cube", "blk")) + (P(),) * 12,
        out_specs=(rows_spec, rows_spec) + (P(),) * 12,
        check_vma=False,
    )
```

```python
import functools
import jax
import jax.numpy as jnp
from jax import lax
from jax.experimental import pallas as pl
from jax.experimental.pallas import tpu as pltpu
from jax.sharding import PartitionSpec as P

HEADS = 12
HD = 64
GROUPS = 12
MEMBERS = 4
LOCAL_HEADS = HEADS // MEMBERS
WIDTH = LOCAL_HEADS * HD
NEG_FILL = -32768.0
EPSILON = 1e-06
BF16 = jnp.bfloat16
F32 = jnp.float32
TILE = 256
LANES = 128
VMEM = pltpu.VMEM
QUICK = pl.CostEstimate(flops=1, bytes_accessed=1, transcendentals=0)
LONG = pl.CostEstimate(flops=20_000_000_000, bytes_accessed=60_000_000, transcendentals=0)


def dot(left, right):
    return jnp.dot(left, right, preferred_element_type=F32)


def dot_nt(left, right):
    return lax.dot_general(left, right, (((1,), (1,)), ((), ())), preferred_element_type=F32)


def dot_tn(left, right):
    return lax.dot_general(left, right, (((0,), (0,)), ((), ())), preferred_element_type=F32)


def params(limit=60 << 20, **more):
    return pltpu.CompilerParams(vmem_limit_bytes=limit, **more)


def whole(*shape):
    return pl.BlockSpec(shape, lambda *_: (0,) * len(shape))


def normalized(values):
    centered = values - jnp.mean(values, axis=-1, keepdims=True)
    inverse = lax.rsqrt(jnp.mean(centered * centered, axis=-1, keepdims=True) + EPSILON)
    return centered * inverse, inverse


def streamed(steps):
    for ins, _, _ in steps:
        for copy in ins:
            copy.start()
    for ins, compute, outs in steps:
        for copy in ins:
            copy.wait()
        compute()
        for copy in outs:
            copy.start()
    for _, _, outs in steps:
        for copy in outs:
            copy.wait()


def mask_column(x, rows):
    return x[rows:, :rows].astype(F32).T[:, :1]


def project_kernel(x0, x1, x2, x3, gain, shift, w, wt, bias, bias_col, *refs):
    results, held, (x_held, w_held, sem_in, sem_out) = refs[:6], refs[6:12], refs[12:]
    normed, qa, ka, va, kt, vt = held
    rows = normed.shape[0] // MEMBERS
    total = MEMBERS * rows
    padded = qa.shape[2]
    step = rows // 3
    low_w = pltpu.make_async_copy(w, w_held.at[0], sem_in.at[MEMBERS])
    steps = []
    for d, x in enumerate((x0, x1, x2, x3)):
        here = pl.ds(d * rows, rows)

        def compute(d=d, here=here):
            part = x_held.at[d]

            def some(i, carry):
                unit, _ = normalized(part[pl.ds(i * step, step), :].astype(F32))
                place = pl.ds(d * rows + i * step, step)
                normed[place, :] = (unit * gain[...][None] + shift[...][None]).astype(BF16)
                return carry

            for i in range(3):
                some(i, 0)
            natural = dot(normed[here, :], w_held[0, :, WIDTH:]) + bias[...][None, WIDTH:]
            lane = lax.broadcasted_iota(jnp.int32, (rows, HD), 1)
            low_mask = NEG_FILL * (1.0 - mask_column(part, rows))
            key_tail = jnp.where(lane == 0, low_mask, jnp.where(lane < 4, 1.0, 0.0)).astype(BF16)
            value_tail = jnp.where(lane < 3, 1.0, 0.0).astype(BF16)
            for h in range(LOCAL_HEADS):
                at = h * HD
                ka[h, here, :HD] = natural[:, at : at + HD].astype(BF16)
                ka[h, here, HD:] = key_tail
                va[h, here, :HD] = natural[:, WIDTH + at : WIDTH + at + HD].astype(BF16)
                va[h, here, HD:] = value_tail

        ins = [pltpu.make_async_copy(x, x_held.at[d], sem_in.at[d])] + ([low_w] if d == 0 else [])
        outs = [pltpu.make_async_copy(normed.at[here], results[0].at[here], sem_out.at[d, 0])]
        for i, at in enumerate((2, 3)):
            outs.append(
                pltpu.make_async_copy(held[at].at[:, here], results[at].at[:, here], sem_out.at[d, i + 1])
            )
        steps.append((ins, compute, outs))

    def turn():
        turned = dot_nt(wt[...], normed[...]) + bias_col[...]
        row = lax.broadcasted_iota(jnp.int32, (HD, padded), 0)
        query_tail = jnp.where(row == 0, 1.0, 0.0).astype(BF16)
        for h in range(LOCAL_HEADS):
            at = h * HD
            qa[h, :HD, :total] = (turned[at : at + HD] * HD ** (-0.5)).astype(BF16)
            qa[h, :HD, total:] = jnp.zeros((HD, padded - total), BF16)
            qa[h, HD:, :] = query_tail
            kt[h] = turned[WIDTH + at : WIDTH + at + HD].astype(BF16)
            vt[h] = turned[2 * WIDTH + at : 2 * WIDTH + at + HD].astype(BF16)

    outs = [
        pltpu.make_async_copy(held[at], results[at], sem_out.at[MEMBERS, i])
        for i, at in enumerate((1, 4, 5))
    ]
    steps.append(([], turn, outs))
    streamed(steps)


def project(x_blocks, rows, gain, shift, w, wt, bias, bias_col):
    model = x_blocks[0].shape[1]
    total = MEMBERS * rows
    padded = -(-total // TILE) * TILE
    n = LOCAL_HEADS
    outs = [
        jax.ShapeDtypeStruct((total, model), BF16),
        jax.ShapeDtypeStruct((n, 2 * HD, padded), BF16),
        jax.ShapeDtypeStruct((n, total, 2 * HD), BF16),
        jax.ShapeDtypeStruct((n, total, 2 * HD), BF16),
        jax.ShapeDtypeStruct((n, HD, total), BF16),
        jax.ShapeDtypeStruct((n, HD, total), BF16),
    ]
    anywhere, near = pl.BlockSpec(memory_space=pl.ANY), pl.BlockSpec(memory_space=VMEM)
    return pl.pallas_call(
        project_kernel,
        out_shape=outs,
        in_specs=[anywhere] * MEMBERS + [near] * 2 + [anywhere] + [near] * 3,
        out_specs=[anywhere] * len(outs),
        scratch_shapes=[VMEM(o.shape, o.dtype) for o in outs]
        + [
            VMEM((MEMBERS, *x_blocks[0].shape), BF16),
            VMEM((1, *w.shape), BF16),
            pltpu.SemaphoreType.DMA((MEMBERS + 1,)),
            pltpu.SemaphoreType.DMA((MEMBERS + 1, 3)),
        ],
        compiler_params=params(),
        cost_estimate=LONG,
        name="project",
    )(*x_blocks, gain, shift, w, wt, bias, bias_col)


def packing(rows):
    top = packed_rows(rows)
    return [(0, top, 0), (top, rows - top, WIDTH)]


def packed_rows(rows):
    return -(-rows // 32) * 16


def forward_kernel(qa, ka, vt, l0, l1, l2, l3, turned, logs, held, even, odd, top_even, top_odd):
    head = pl.program_id(0)
    rows = ka.shape[1] // MEMBERS
    tiles = qa.shape[2] // TILE

    def scored(i, out, top):
        here = pl.ds(pl.multiple_of(i * TILE, TILE), TILE)
        scores = dot(ka[0], qa[0, :, here])
        out[...] = scores
        top[...] = jnp.max(scores, axis=0, keepdims=True)

    def mixed_of(i, scores, top):
        here = pl.ds(pl.multiple_of(i * TILE, TILE), TILE)
        peak = top[...]
        weights = jnp.exp(scores[...] - peak)
        sums = jnp.sum(weights, axis=0, keepdims=True)
        mixed = dot(vt[0], weights.astype(BF16)) * (1.0 / sums)
        turned[0, :, here] = mixed
        logs[0, :, here] = peak + jnp.log(sums)
        held[here, :] = mixed.T.astype(BF16)

    scored(0, even, top_even)

    def pair(i, carry):
        scored(2 * i + 1, odd, top_odd)
        mixed_of(2 * i, even, top_even)
        scored(jnp.minimum(2 * i + 2, tiles - 1), even, top_even)
        mixed_of(2 * i + 1, odd, top_odd)
        return carry

    lax.fori_loop(0, tiles // 2, pair, 0)
    if tiles % 2:
        mixed_of(tiles - 1, even, top_even)
    for h in range(LOCAL_HEADS):

        @pl.when(head == h)
        def _(h=h):
            for d, low in enumerate((l0, l1, l2, l3)):
                for rows_at, size, lane in packing(rows):
                    at = d * rows + rows_at
                    low[:size, lane + h * HD : lane + (h + 1) * HD] = held[at : at + size, :]


def attend(qa, ka, vt):
    n, total, _ = ka.shape
    padded = qa.shape[2]
    rows = total // MEMBERS
    per_head = lambda *shape: pl.BlockSpec((1,) + shape, lambda h: (h, 0, 0))
    *low, turned, logs = pl.pallas_call(
        forward_kernel,
        grid=(n,),
        out_shape=[jax.ShapeDtypeStruct((packed_rows(rows), 2 * WIDTH), BF16)] * MEMBERS
        + [
            jax.ShapeDtypeStruct((n, HD, padded), F32),
            jax.ShapeDtypeStruct((n, 1, padded), F32),
        ],
        in_specs=[per_head(2 * HD, padded), per_head(total, 2 * HD), per_head(HD, total)],
        out_specs=[whole(packed_rows(rows), 2 * WIDTH)] * MEMBERS + [per_head(HD, padded), per_head(1, padded)],
        scratch_shapes=[VMEM((padded, HD), BF16), VMEM((total, TILE), F32), VMEM((total, TILE), F32)]
        + [VMEM((1, TILE), F32)] * 2,
        compiler_params=params(),
        cost_estimate=LONG,
        name="attend",
    )(qa, ka, vt)
    return low, turned, logs


def three_parts(row):
    high = row.astype(BF16).astype(F32)
    rest = row - high
    middle = rest.astype(BF16).astype(F32)
    return high, middle, rest - middle


def backward_kernel(
    head, qa, ka, va, kt, turned, logs, g0, g1, g2, g3, out_q, out_k, out_v, held_g, sum_k, sum_v, s0, s1, d0, d1
):
    total = ka.shape[1]
    rows = total // MEMBERS
    padded = qa.shape[2]
    tiles = padded // TILE
    for d, part in enumerate((g0, g1, g2, g3)):
        for rows_at, size, lane in packing(rows):
            at = d * rows + rows_at
            held_g[at : at + size, :] = part[:size, lane + head * HD : lane + (head + 1) * HD]
    held_g[total:, :] = jnp.zeros((padded - total, HD), BF16)
    sum_k[...] = jnp.zeros_like(sum_k)
    sum_v[...] = jnp.zeros_like(sum_v)
    row = lax.broadcasted_iota(jnp.int32, (HD, TILE), 0)

    def scored(i, probs_out, grads_out):
        here = pl.ds(pl.multiple_of(i * TILE, TILE), TILE)
        grad_turned = held_g[here, :].astype(F32).T
        delta = jnp.sum(grad_turned * turned[0, :, here], axis=0, keepdims=True)
        high, middle, least = three_parts(-logs[0, :, here])
        tail = jnp.where(row == 0, 1.0, jnp.where(row == 1, high, jnp.where(row == 2, middle, jnp.where(row == 3, least, 0.0))))
        query = jnp.concatenate([qa[0, :HD, here], tail.astype(BF16)], axis=0)
        probs_out[...] = dot(ka[0], query)
        high, middle, least = three_parts(-delta)
        tail = jnp.where(row == 0, high, jnp.where(row == 1, middle, jnp.where(row == 2, least, 0.0)))
        grad_tail = jnp.concatenate([grad_turned, tail], axis=0).astype(BF16)
        grads_out[...] = dot(va[0], grad_tail)

    def some(i, width, probs_in, grads_in):
        here = pl.ds(pl.multiple_of(i * TILE, TILE), TILE)
        probs = jnp.exp(probs_in[...])
        grad_scores = (probs * grads_in[...]).astype(BF16)
        grad_turned = held_g[here, :].astype(F32).T.astype(BF16)
        sum_v[...] += dot_nt(grad_turned, probs.astype(BF16))
        sum_k[...] += dot_nt(qa[0, :HD, here], grad_scores)
        query_grad = dot(kt[0], grad_scores) * HD ** (-0.5)
        out_q[pl.ds(pl.multiple_of(i * TILE, TILE), width), :] = query_grad.T.astype(BF16)[:width]

    def pair(i, carry):
        scored(2 * i + 1, s1, d1)
        some(2 * i, TILE, s0, d0)
        scored(2 * i + 2, s0, d0)
        some(2 * i + 1, TILE, s1, d1)
        return carry

    least = total - (tiles - 1) * TILE
    scored(0, s0, d0)
    lax.fori_loop(0, (tiles - 1) // 2, pair, 0)
    if tiles % 2 == 0:
        scored(tiles - 1, s1, d1)
        some(tiles - 2, TILE, s0, d0)
        some(tiles - 1, least, s1, d1)
    else:
        some(tiles - 1, least, s0, d0)
    out_k[...] = sum_k[...].T.astype(BF16)
    out_v[...] = sum_v[...].T.astype(BF16)


def attend_back(head, qa, ka, va, kt, turned, logs, grads):
    n, total, _ = ka.shape
    padded = qa.shape[2]
    per_head = lambda *shape: pl.BlockSpec((1,) + shape, lambda i: (head, 0, 0))
    return pl.pallas_call(
        functools.partial(backward_kernel, head),
        grid=(1,),
        out_shape=[jax.ShapeDtypeStruct((total, HD), BF16)] * 3,
        in_specs=[
            per_head(2 * HD, padded),
            per_head(total, 2 * HD),
            per_head(total, 2 * HD),
            per_head(HD, total),
            per_head(HD, padded),
            per_head(1, padded),
        ]
        + [whole(*grads[0].shape)] * MEMBERS,
        out_specs=[whole(total, HD)] * 3,
        scratch_shapes=[
            VMEM((padded, HD), BF16),
            VMEM((HD, total), F32),
            VMEM((HD, total), F32),
        ]
        + [VMEM((total, TILE), F32)] * 4,
        compiler_params=params(),
        cost_estimate=LONG,
        name="attend_back",
    )(qa, ka, va, kt, turned, logs, *grads)


def unproject_kernel(where, *refs):
    columns, normed, w = refs[:9], refs[9], refs[10]
    n0, n1, n23, a_send, a_keep, b_send, b_keep, sums = refs[11:19]
    held, held_normed, held_n, joint, grad, sem_in, sem_out = refs[19:]
    rows = n0.shape[0]
    here = [pl.ds(d * rows, rows) for d in range(MEMBERS)]
    steps = []
    for s in range(3):
        for h in range(LOCAL_HEADS):
            at = s * WIDTH + h * HD
            slot = 3 * h + s

            def put(at=at, slot=slot):
                joint[:, at : at + HD] = held[slot]

            steps.append(([pltpu.make_async_copy(columns[slot], held.at[slot], sem_in.at[slot])], put, []))
    for d in (2, 3, 1, 0):

        def back(d=d):
            held_n[d] = dot_nt(joint[here[d], :], w[...]).astype(BF16)

        place = (n0, n1, n23.at[0], n23.at[1])[d]
        ins = [pltpu.make_async_copy(normed, held_normed, sem_in.at[9])] if d == 0 else []
        steps.append((ins, back, [pltpu.make_async_copy(held_n.at[d], place, sem_out.at[d])]))

    def weights():
        whole_grad = dot_tn(joint[...], held_normed[...])
        count, each, model = grad.shape
        for i in range(count):
            grad[i] = whole_grad[i * each : (i + 1) * each]
        pieces = count // 2
        for r in range(pieces):
            for p in range(2):
                part = grad[(r ^ where[1]) * 2 + (p ^ (where[2] // 2))].astype(BF16)
                out = (a_keep, a_send)[r % 2]
                out[r // 2, p] = part[:, : model // 2]
                out = (b_keep, b_send)[2 * r // pieces]
                out[r % (pieces // 2), p] = part[:, model // 2 :]
        total = jnp.sum(joint[...].astype(F32), axis=0, keepdims=True)
        sums[...] = jnp.zeros_like(sums)
        for m in range(MEMBERS):

            @pl.when(2 * where[0] + where[2] % 2 == m)
            def _(m=m):
                sums[0:1, m * WIDTH : (m + 1) * WIDTH] = total[:, :WIDTH]
                sums[1:2, m * WIDTH : (m + 1) * WIDTH] = total[:, 2 * WIDTH :]

    steps.append(([], weights, []))
    streamed(steps)


def unproject(where, columns, normed, w, pieces):
    total, model = normed.shape
    rows = total // MEMBERS
    width = 3 * WIDTH
    each = width // pieces // 2
    shaped = jax.ShapeDtypeStruct
    outs = [shaped((rows, model), BF16)] * 2 + [shaped((2, rows, model), BF16)]
    outs += [shaped((pieces // 2, 2, each, model // 2), BF16)] * 4 + [shaped((2, model), F32)]
    anywhere, near = pl.BlockSpec(memory_space=pl.ANY), pl.BlockSpec(memory_space=VMEM)
    return pl.pallas_call(
        unproject_kernel,
        out_shape=outs,
        in_specs=[pl.BlockSpec(memory_space=pltpu.SMEM)] + [anywhere] * 10 + [near],
        out_specs=[anywhere] * 3 + [near] * 5,
        scratch_shapes=[
            VMEM((9, total, HD), BF16),
            VMEM((total, model), BF16),
            VMEM((MEMBERS, rows, model), BF16),
            VMEM((total, width), BF16),
            VMEM((2 * pieces, each, model), F32),
            pltpu.SemaphoreType.DMA((10,)),
            pltpu.SemaphoreType.DMA((MEMBERS,)),
        ],
        compiler_params=params(),
        cost_estimate=LONG,
        name="unproject",
    )(where, *columns, normed, w)


def pre_sums_kernel(x0, x1, x2, x3, n0, n1, n23, out):
    rows = n0.shape[0]
    out[...] = jnp.zeros_like(out)
    for x, given in ((x0, n0), (x1, n1), (x2, n23.at[0]), (x3, n23.at[1])):
        unit, _ = normalized(x[:rows, :].astype(F32))
        grad = given[...].astype(F32)
        out[0:1, :] += jnp.sum(grad * unit, axis=0, keepdims=True)
        out[1:2, :] += jnp.sum(grad, axis=0, keepdims=True)


def close_kernel(x, p0, p1, gain, hidden, grad, low):
    rows = hidden.shape[0]
    unit, inverse = normalized(x[:rows, :].astype(F32))
    given = p0[...].astype(F32) + p1[...].astype(F32)
    scaled = given * gain[...][None]
    inner = scaled - jnp.mean(scaled, axis=-1, keepdims=True)
    inner = inner - unit * jnp.mean(scaled * unit, axis=-1, keepdims=True)
    total = hidden[...] + inverse * inner
    grad[...] = total
    low[...] = total.astype(BF16)


def close(x, parts, gain, hidden):
    rows, model = hidden.shape
    shaped = jax.ShapeDtypeStruct
    return pl.pallas_call(
        close_kernel,
        out_shape=[shaped((rows, model), F32), shaped((rows, model), BF16)],
        in_specs=[pl.BlockSpec(memory_space=VMEM)] * 5,
        out_specs=[pl.BlockSpec(memory_space=VMEM)] * 2,
        compiler_params=params(),
        cost_estimate=LONG,
        name="close",
    )(x, *parts, gain, hidden)


def middle_kernel(
    side, x, a0, a1, a2, a3, wo, out_bias, gain, shift, cot, down_bias, up, up_bias, down,
    layer, down_send, down_keep, rest_send, rest_keep, grad_up_bias, grad_hidden, g0, g1, g2, g3, vectors,
    hidden, normed, grad_down, total_out, total_grad, valid,
):
    step = pl.program_id(0)
    last = pl.num_programs(0) - 1
    half = pl.num_programs(0) // 2
    rows, model = cot.shape
    pieces = down_keep.shape[0]
    each = half * model // pieces
    share = model // each

    @pl.when(step == 0)
    def _():
        valid[...] = mask_column(x, rows)
        value = x[:rows, :].astype(F32) + out_bias[...][None]
        cuts = packing(rows)
        value += jnp.concatenate(
            [
                sum(dot(part[:size, lane : lane + WIDTH], wo[e]) for e, part in enumerate((a0, a1, a2, a3)))
                for _, size, lane in cuts
            ]
        )
        hidden[...] = value
        unit, _ = normalized(value)
        normed[...] = (unit * gain[...][None] + shift[...][None]).astype(BF16)
        low = (valid[...] * cot[...].astype(F32)).astype(BF16)
        grad_down[...] = low
        vectors[3:4, :] = jnp.sum(low.astype(F32), axis=0, keepdims=True)
        total_out[...] = value + down_bias[...][None]
        total_grad[...] = jnp.zeros_like(total_grad)

    gate = dot(normed[...], up[...]) + up_bias[0]
    below = 0.5 * (1.0 + lax.erf(gate * (0.5**0.5)))
    active = (gate * below).astype(BF16)
    slope = below + gate * (jnp.exp(-0.5 * gate * gate) * (0.5 / jnp.pi) ** 0.5)
    low = grad_down[...]
    grad_gate = (dot_nt(low, down[...]) * slope).astype(BF16)
    total_out[...] += dot(active, down[...])
    total_grad[...] += dot_nt(grad_gate, up[...])
    grad_up_bias[0] = jnp.sum(grad_gate.astype(F32), axis=0, keepdims=True)
    of_down = dot_tn(active, low).astype(BF16)
    of_up = dot_tn(normed[...], grad_gate).astype(BF16)
    few = each // MEMBERS
    for i in range(2 * half):

        @pl.when(step == i)
        def _(i=i):
            down_held, rest_held = (down_send, rest_send) if i < half else (down_keep, rest_keep)
            for j in range(share):
                piece = ((i % half) * share + j) ^ side[1]
                for z in range(MEMBERS):
                    at = j * each + z * few
                    down_held[piece, z ^ side[2]] = of_down[at : at + few]
                    rest_held[piece, z ^ side[2], :few, :] = of_up[at : at + few]

    @pl.when(step == last)
    def _():
        unit, inverse = normalized(hidden[...])
        layer[...] = (valid[...] * total_out[...]).astype(BF16)
        grad = total_grad[...]
        vectors[0:1, :] = jnp.sum(grad * unit, axis=0, keepdims=True)
        vectors[1:2, :] = jnp.sum(grad, axis=0, keepdims=True)
        scaled = grad * gain[...][None]
        inner = scaled - jnp.mean(scaled, axis=-1, keepdims=True)
        inner = inner - unit * jnp.mean(scaled * unit, axis=-1, keepdims=True)
        grad = grad_down[...].astype(F32) + inverse * inner
        grad_hidden[...] = grad
        branch = grad.astype(BF16)
        vectors[2:3, :] = jnp.sum(branch.astype(F32), axis=0, keepdims=True)
        parts = (a0, a1, a2, a3)
        count = pieces // 2
        some = WIDTH // count // MEMBERS
        for e, given in enumerate((g0, g1, g2, g3)):
            back = dot_nt(branch, wo[e]).astype(BF16)
            given[...] = jnp.zeros_like(given)
            for at, size, lane in packing(rows):
                given[:size, lane : lane + WIDTH] = back[at : at + size]
            held = rest_keep if e < 2 else rest_send
            place = ((side[2] % 2) ^ (e & 1)) * count
            of_out = sum(
                dot_tn(parts[e][:size, lane : lane + WIDTH], branch[at : at + size])
                for at, size, lane in packing(rows)
            ).astype(BF16)
            for j in range(count):
                for z in range(MEMBERS):
                    at = (j * MEMBERS + z) * some
                    held[(place + j) ^ side[1], z ^ side[2], few:, :] = of_out[at : at + some]


def middle(where, pieces, x, attended, wo, out_bias, gain, shift, cot, down_bias, up, up_bias, down):
    rows, model = cot.shape
    blocks = up.shape[1] // model
    half = blocks // 2

    def block_of(i, side):
        return lax.rem(i, half) + half * jnp.where(i < half, 1 - side[0], side[0])

    whole_s = lambda *shape: pl.BlockSpec(shape, lambda i, side: (0,) * len(shape))
    each = half * model // pieces // MEMBERS
    held = (pieces, MEMBERS, each, model)
    rest = (pieces, MEMBERS, each + 2 * WIDTH // pieces // MEMBERS, model)
    shaped = jax.ShapeDtypeStruct
    outs = [
        (shaped((rows, model), BF16), whole_s(rows, model)),
        (shaped(held, BF16), whole_s(*held)),
        (shaped(held, BF16), whole_s(*held)),
        (shaped(rest, BF16), whole_s(*rest)),
        (shaped(rest, BF16), whole_s(*rest)),
        (shaped((blocks, 1, model), F32), pl.BlockSpec((1, 1, model), lambda i, side: (block_of(i, side), 0, 0))),
        (shaped((rows, model), F32), whole_s(rows, model)),
    ]
    outs += [(shaped(attended[0].shape, BF16), whole_s(*attended[0].shape))] * MEMBERS
    outs += [(shaped((4, model), F32), whole_s(4, model))]
    return pl.pallas_call(
        middle_kernel,
        out_shape=[o[0] for o in outs],
        grid_spec=pltpu.PrefetchScalarGridSpec(
            num_scalar_prefetch=1,
            grid=(blocks,),
            in_specs=[whole_s(*x.shape)]
            + [whole_s(*attended[0].shape)] * MEMBERS
            + [whole_s(MEMBERS, WIDTH, model)]
            + [whole_s(model)] * 3
            + [whole_s(rows, model), whole_s(model)]
            + [
                pl.BlockSpec((model, model), lambda i, side: (0, block_of(i, side))),
                pl.BlockSpec((1, 1, model), lambda i, side: (block_of(i, side), 0, 0)),
                pl.BlockSpec((model, model), lambda i, side: (block_of(i, side), 0)),
            ],
            out_specs=[o[1] for o in outs],
            scratch_shapes=[
                VMEM((rows, model), F32),
                VMEM((rows, model), BF16),
                VMEM((rows, model), BF16),
                VMEM((rows, model), F32),
                VMEM((rows, model), F32),
                VMEM((rows, 1), F32),
            ],
        ),
        compiler_params=params(),
        cost_estimate=LONG,
        name="middle",
    )(
        where,
        x, *attended, wo, out_bias, gain, shift, cot, down_bias,
        up, up_bias.reshape(blocks, 1, model), down,
    )


def reversed_bits(index, count):
    bits = count.bit_length() - 1
    total = 0
    for bit in range(bits):
        total = total | (((index >> bit) & 1) << (bits - 1 - bit))
    return total


def place_steps(where, other, parts, cuts, outs, held_in, held, sem_in, sem_out):
    _, pieces, _, _, lanes = parts.shape
    model = 2 * lanes
    half = where[0] ^ other
    steps = []
    for r in range(pieces):
        piece = r ^ where[1]
        ins = [
            pltpu.make_async_copy(parts.at[i, at], held_in.at[other, r, i], sem_in.at[other, r, i])
            for i, at in enumerate((reversed_bits(r, pieces), r))
        ]

        def compute(r=r):
            for z in range(MEMBERS):
                given = reversed_bits(z ^ where[2], MEMBERS)
                for i in range(2):
                    for out, (start, size) in zip(held, cuts):
                        value = held_in[other, r, i, given, start : start + size, :]
                        out[other, r, z * size : (z + 1) * size, i * lanes : (i + 1) * lanes] = value.astype(F32)

        places = []
        for out, (_, size) in zip(outs, cuts):
            rows = size * MEMBERS
            if out.shape[1] == model:
                places.append(out.at[pl.ds((half * pieces + piece) * rows, rows)])
            else:
                share = model // rows
                column = half * (out.shape[1] // model // 2) + piece // share
                places.append(
                    out.at[
                        pl.ds(lax.rem(piece, share) * rows, rows),
                        pl.ds(pl.multiple_of(column * model, model), model),
                    ]
                )
        sends = [
            pltpu.make_async_copy(given.at[other, r], place, sem_out.at[other, r, i])
            for i, (given, place) in enumerate(zip(held, places))
        ]
        steps.append((ins, compute, sends))
    return steps


def cuts_of(parts, shapes):
    _, pieces, _, rows, lanes = parts.shape
    sizes = [shape[0] * shape[1] // (2 * lanes) // 2 // pieces // MEMBERS for shape in shapes]
    return [(sum(sizes[:i]), size) for i, size in enumerate(sizes)]


def place_scratch(parts, cuts):
    _, pieces, _, rows, lanes = parts.shape
    scratch = [VMEM((2, pieces, 2, MEMBERS, rows, lanes), BF16)]
    scratch += [VMEM((2, pieces, MEMBERS * size, 2 * lanes), F32) for _, size in cuts]
    return scratch + [
        pltpu.SemaphoreType.DMA((2, pieces, 2)),
        pltpu.SemaphoreType.DMA((2, pieces, len(cuts))),
    ]


def place_kernel(cuts, where, own, got, *refs):
    count = len(cuts)
    outs, held_in, held, sems = refs[:count], refs[count], refs[count + 1 : -2], refs[-2:]
    streamed(
        place_steps(where, 0, own, cuts, outs, held_in, held, *sems)
        + place_steps(where, 1, got, cuts, outs, held_in, held, *sems)
    )


def placed(where, own, got, shapes):
    cuts = cuts_of(own, shapes)
    anywhere = pl.BlockSpec(memory_space=pl.ANY)
    return pl.pallas_call(
        functools.partial(place_kernel, cuts),
        out_shape=[jax.ShapeDtypeStruct(shape, F32) for shape in shapes],
        in_specs=[pl.BlockSpec(memory_space=pltpu.SMEM)] + [anywhere] * 2,
        out_specs=[anywhere] * len(cuts),
        scratch_shapes=place_scratch(own, cuts),
        compiler_params=params(),
        cost_estimate=LONG,
        name="placed",
    )(where, own, got)


def place_last_kernel(cuts, where, own, got, in_own, in_got, *refs):
    count = len(cuts)
    outs, (out, *vectors), scratch = refs[:count], refs[count : count + 9], refs[count + 9 :]
    held_in, held, sems = scratch[0], scratch[1 : 1 + count], scratch[1 + count : 3 + count]
    in_held, columns, out_held, sem_in, sem_out = scratch[3 + count :]
    steps = place_steps(where, 0, own, cuts, outs, held_in, held, *sems)
    steps += place_steps(where, 1, got, cuts, outs, held_in, held, *sems)
    _, pieces, _, _, lanes = in_own.shape
    model = 2 * lanes
    each = columns.shape[2]
    totals = []

    def gather(other):
        total = 0.0
        for piece in range(pieces):
            for side in range(MEMBERS):
                r, z = piece ^ where[1], side ^ where[2]
                at = reversed_bits(z, MEMBERS)
                both = (in_held[other, 0, reversed_bits(r, pieces), at], in_held[other, 1, r, at])
                both = jnp.concatenate([v.astype(F32) for v in both], axis=1)
                columns[2 * other + side % 2, piece * 2 + side // 2] = both[:each]
                total = total + both[each:]
        totals.append(total)

    def turn(other, s):
        for m in range(2):
            given = columns[2 * other + m].reshape(3 * WIDTH, model)[s * WIDTH : (s + 1) * WIDTH]
            out_held[other, s, :, m * WIDTH : (m + 1) * WIDTH] = given.T

    for other, given in enumerate((in_own, in_got)):
        copy = pltpu.make_async_copy(given, in_held.at[other], sem_in.at[other])
        steps.append(([copy], functools.partial(gather, other), []))
        for s in range(3):
            at = s * model + (where[0] ^ other) * lanes
            place = out.at[:, pl.ds(pl.multiple_of(at, lanes), lanes)]
            copy = pltpu.make_async_copy(out_held.at[other, s], place, sem_out.at[other, s])
            steps.append(([], functools.partial(turn, other, s), [copy]))
    streamed(steps)
    total = totals[0] + totals[1]
    for i in range(6):
        vectors[i][...] = total[i]
    vectors[6][...] = total[6:8]
    for i in range(vectors[7].shape[0] // model):
        vectors[7][i * model : (i + 1) * model] = total[8 + i]


def placed_last(where, own, got, in_own, in_got, extra, hidden_units):
    _, pieces, _, rows, lanes = in_own.shape
    model = 2 * lanes
    shapes = [(model, hidden_units), (model, model)]
    cuts = cuts_of(own, shapes)
    vectors = [(model,)] * 6 + [(2, model), (hidden_units,)]
    anywhere, near = pl.BlockSpec(memory_space=pl.ANY), pl.BlockSpec(memory_space=VMEM)
    return pl.pallas_call(
        functools.partial(place_last_kernel, cuts),
        out_shape=[jax.ShapeDtypeStruct(shape, F32) for shape in shapes + [(model, 3 * model)] + vectors],
        in_specs=[pl.BlockSpec(memory_space=pltpu.SMEM)] + [anywhere] * 4,
        out_specs=[anywhere] * 3 + [near] * 8,
        scratch_shapes=place_scratch(own, cuts)
        + [
            VMEM((2, *in_own.shape), BF16),
            VMEM((MEMBERS, 2 * pieces, rows - extra, model), F32),
            VMEM((2, 3, model, lanes), F32),
            pltpu.SemaphoreType.DMA((2,)),
            pltpu.SemaphoreType.DMA((2, 3)),
        ],
        compiler_params=params(),
        cost_estimate=LONG,
        name="placed_last",
    )(where, own, got, in_own, in_got)


def plus(first, second):
    return (first.astype(F32) + second.astype(F32)).astype(BF16)


def fold_core_kernel(keep, got, a_send, a_keep, b_send, b_keep, held, held_got, held_out, sem_in, sem_out):
    pieces, _, _, lanes = keep.shape
    steps = []
    for p in range(pieces):
        ins = [
            pltpu.make_async_copy(keep.at[p], held.at[p], sem_in.at[p, 0]),
            pltpu.make_async_copy(got.at[p], held_got.at[p], sem_in.at[p, 1]),
        ]

        def compute(p=p):
            total = plus(held[p], held_got[p])
            held_out[p, 0] = total[:, :, : lanes // 2]
            held_out[p, 1] = total[:, :, lanes // 2 :]

        first = (a_keep, a_send)[p % 2].at[p // 2]
        second = (b_keep, b_send)[2 * p // pieces].at[p % (pieces // 2)]
        outs = [
            pltpu.make_async_copy(held_out.at[p, i], place, sem_out.at[p, i])
            for i, place in enumerate((first, second))
        ]
        steps.append((ins, compute, outs))
    streamed(steps)


def fold_core(keep, got):
    pieces, quarters, rows, lanes = keep.shape
    half = (quarters, rows, lanes // 2)
    return pl.pallas_call(
        fold_core_kernel,
        out_shape=[jax.ShapeDtypeStruct((pieces // 2, *half), BF16)] * 4,
        in_specs=[pl.BlockSpec(memory_space=pl.ANY)] * 2,
        out_specs=[pl.BlockSpec(memory_space=pl.ANY)] * 4,
        scratch_shapes=[
            VMEM(keep.shape, BF16),
            VMEM(keep.shape, BF16),
            VMEM((pieces, 2, *half), BF16),
            pltpu.SemaphoreType.DMA((pieces, 2)),
            pltpu.SemaphoreType.DMA((pieces, 2)),
        ],
        compiler_params=params(),
        cost_estimate=QUICK,
        name="fold_core",
    )(keep, got)


def fold_core_quarters_kernel(keep, got, send, kept, held, held_got, held_out, sem_in, sem_out):
    pieces, quarters = keep.shape[:2]
    steps = []
    for p in range(pieces):
        ins = [
            pltpu.make_async_copy(keep.at[p], held.at[p], sem_in.at[p, 0]),
            pltpu.make_async_copy(got.at[p], held_got.at[p], sem_in.at[p, 1]),
        ]

        def compute(p=p):
            for z in range(quarters):
                held_out[p, z % 2, z // 2] = plus(held[p, z], held_got[p, z])

        outs = [
            pltpu.make_async_copy(held_out.at[p, i], place.at[p], sem_out.at[p, i])
            for i, place in enumerate((kept, send))
        ]
        steps.append((ins, compute, outs))
    streamed(steps)


def fold_core_quarters(keep, got):
    pieces, quarters, rows, lanes = keep.shape
    half = (quarters // 2, rows, lanes)
    return pl.pallas_call(
        fold_core_quarters_kernel,
        out_shape=[jax.ShapeDtypeStruct((pieces, *half), BF16)] * 2,
        in_specs=[pl.BlockSpec(memory_space=pl.ANY)] * 2,
        out_specs=[pl.BlockSpec(memory_space=pl.ANY)] * 2,
        scratch_shapes=[
            VMEM(keep.shape, BF16),
            VMEM(keep.shape, BF16),
            VMEM((pieces, 2, *half), BF16),
            pltpu.SemaphoreType.DMA((pieces, 2)),
            pltpu.SemaphoreType.DMA((pieces, 2)),
        ],
        compiler_params=params(),
        cost_estimate=QUICK,
        name="fold_core_quarters",
    )(keep, got)


def fold_halves_kernel(keep, got, send, kept):
    for p in range(keep.shape[0]):
        kept[p] = plus(keep[p, 0], got[p, 0])
        send[p] = plus(keep[p, 1], got[p, 1])


def fold_halves(keep, got):
    pieces, _, rows, lanes = keep.shape
    outs = [jax.ShapeDtypeStruct((pieces, rows, lanes), BF16)] * 2
    return in_vmem(fold_halves_kernel, outs, keep, got, name="fold_halves")


def fold_pieces_kernel(keep, got, a_send, a_keep, b_send, b_keep):
    pieces, _, model = keep.shape
    for r in range(pieces):
        total = plus(keep[r], got[r])
        out = (a_keep, a_send)[r % 2]
        out[r // 2, 0] = total[:, : model // 2]
        out = (b_keep, b_send)[2 * r // pieces]
        out[r % (pieces // 2), 0] = total[:, model // 2 :]


def fold_pieces(keep, got):
    pieces, rows, model = keep.shape
    outs = [jax.ShapeDtypeStruct((pieces // 2, 1, rows, model // 2), BF16)] * 4
    return in_vmem(fold_pieces_kernel, outs, keep, got, name="fold_pieces")


def join_planes_kernel(ak, ag, bk, bg, out):
    count = ak.shape[0]
    for r in range(count):
        out[0, r], out[0, count + r] = ak[r], ag[r]
        out[1, r], out[1, count + r] = bk[r], bg[r]


def join_planes(ak, ag, bk, bg):
    count, *rest = ak.shape
    outs = [jax.ShapeDtypeStruct((2, 2 * count, *rest), BF16)]
    return in_vmem(join_planes_kernel, outs, ak, ag, bk, bg, name="join_planes")[0]


def fold_in_kernel(keep, got, pre, mid, biases, up_bias, out):
    rows = keep.shape[1]
    out[:rows, :] = plus(keep[0], got[0])
    vectors = [pre[...], mid[...], biases[...]] + [up_bias[i] for i in range(up_bias.shape[0])]
    count = sum(v.shape[0] for v in vectors)
    filled = vectors + [jnp.zeros((out.shape[0] - rows - count, out.shape[1]), F32)]
    out[rows:, :] = jnp.concatenate(filled).astype(BF16)


def fold_in(keep, got, vectors, extra):
    _, rows, lanes = keep.shape
    outs = [jax.ShapeDtypeStruct((rows + extra, lanes), BF16)]
    return in_vmem(fold_in_kernel, outs, keep, got, *vectors, name="fold_in")[0]


def in_vmem(kernel, outs, *values, name):
    return pl.pallas_call(
        kernel,
        out_shape=outs,
        in_specs=[pl.BlockSpec(memory_space=VMEM)] * len(values),
        out_specs=[pl.BlockSpec(memory_space=VMEM)] * len(outs),
        compiler_params=params(),
        cost_estimate=QUICK,
        name=name,
    )(*values)


def fold_planes_kernel(ak, ag, bk, bg, a_send, a_keep, b_send, b_keep):
    count = ak.shape[0]
    for r in range(count):
        out = (a_keep, a_send)[r % 2]
        out[r // 2] = plus(ak[r], ag[r])
        out = (b_keep, b_send)[2 * r // count]
        out[r % (count // 2)] = plus(bk[r], bg[r])


def fold_last_kernel(ak, ag, bk, bg, send, keep=None):
    quarters = ak.shape[1]
    lanes = ak.shape[3]
    keep = send if keep is None else keep
    for z in range(quarters):
        out = (keep, send)[z % 2]
        out[z // 2, :, :lanes] = plus(ak[0, z], ag[0, z])
        out[z // 2, :, lanes:] = plus(bk[0, z], bg[0, z])


def fold_planes(ak, ag, bk, bg):
    count, quarters, rows, lanes = ak.shape
    if count > 1:
        outs = [jax.ShapeDtypeStruct((count // 2, quarters, rows, lanes), BF16)] * 4
        return in_vmem(fold_planes_kernel, outs, ak, ag, bk, bg, name="fold_planes")
    outs = [jax.ShapeDtypeStruct((-(-quarters // 2), rows, 2 * lanes), BF16)] * min(quarters, 2)
    return in_vmem(fold_last_kernel, outs, ak, ag, bk, bg, name="fold_last")


def fold_quarters_kernel(keep, got, *outs):
    for z in range(keep.shape[0]):
        out = outs[len(outs) - 1 - z]
        out[...] = plus(keep[z], got[z])


def fold_quarters(keep, got):
    count, rows, lanes = keep.shape
    outs = [jax.ShapeDtypeStruct((rows, lanes), BF16)] * count
    return in_vmem(fold_quarters_kernel, outs, keep, got, name="fold_quarters")


def over_cube(value, bit):
    count = lax.axis_size("cube")
    return lax.ppermute(value, "cube", [(i, i ^ (1 << bit)) for i in range(count)])


def over_blk(value, bit):
    return lax.ppermute(value, "blk", [(i, i ^ (1 << bit)) for i in range(MEMBERS)])


def chosen_pairs(is_home, cube_flip, blk_flip):
    pairs = []
    for c in range(lax.axis_size("cube")):
        for b in range(MEMBERS):
            if ((c & 1) == (b >> 1)) == is_home:
                pairs.append((c * MEMBERS + b, (c ^ cube_flip) * MEMBERS + (b ^ blk_flip)))
    return pairs


def sent_between(value, is_home, cube_flip, blk_flip):
    return lax.ppermute(value, ("cube", "blk"), chosen_pairs(is_home, cube_flip, blk_flip))


def exchanged(parts):
    far = over_blk(parts[3], 0)
    near = over_blk(parts[1], 0)
    core = over_cube(parts[2], 0)
    return [parts[0], near, core, over_cube(far, 0)]


def cube_bits():
    return list(range(1, lax.axis_size("cube").bit_length() - 1))


def by_cube(bit):
    return functools.partial(over_cube, bit=bit)


def by_blk(bit):
    return functools.partial(over_blk, bit=bit)


def scattering(a_send, a_keep, b_send, b_keep):
    for low, high in zip(cube_bits(), cube_bits()[::-1]):
        a_got, b_got = yield [(a_send, by_cube(low)), (b_send, by_cube(high))]
        *folded, = fold_planes(a_keep, a_got, b_keep, b_got)
        if len(folded) <= 2:
            return folded
        a_send, a_keep, b_send, b_keep = folded


def spreading(shard):
    (got,) = yield [(shard, by_blk(1))]
    both = jnp.stack([shard, got])
    (got,) = yield [(both, by_blk(0))]
    both = jnp.concatenate([both, got])[None]
    lanes = both.shape[3] // 2
    a_part, b_part = both[..., :lanes], both[..., lanes:]
    for low, high in zip(cube_bits(), cube_bits()[::-1]):
        a_got, b_got = yield [(a_part, by_cube(high)), (b_part, by_cube(low))]
        if low == cube_bits()[-1]:
            break
        a_part, b_part = jnp.concatenate([a_part, a_got]), jnp.concatenate([b_part, b_got])
    (got,) = yield [(join_planes(a_part, a_got, b_part, b_got), by_cube(0))]
    return got


def summing(keep, send):
    (got,) = yield [(send, by_cube(0))]
    send, keep = yield from scattering(*fold_core(keep, got))
    (got,) = yield [(send, by_blk(0))]
    send, keep = fold_quarters(keep, got)
    (got,) = yield [(send, by_blk(1))]
    return (yield from spreading(plus(keep, got)))


def summing_columns(parts, vectors, extra):
    send, keep = yield from scattering(*parts)
    (got,) = yield [(send, by_blk(1))]
    return (yield from spreading(fold_in(keep, got, vectors, extra)))


def closing(own, parts, gain, grad_hidden):
    p0, p1, p23 = parts
    (got,) = yield [(p23, by_cube(0))]
    near_sum, own_sum = plus(p1, got[1]), plus(p0, got[0])
    (got,) = yield [(near_sum, by_blk(0))]
    grad_here, grad_low = close(own, [own_sum, got], gain, grad_hidden)
    (moved,) = yield [(grad_low, lambda v: sent_between(v, False, 1, 2))]
    return grad_here, moved


class Order:
    def __init__(self, token):
        self.token = token

    def __call__(self, values):
        values, self.token = lax.optimization_barrier((values, self.token))
        return values


class Running:
    def __init__(self, steps):
        self.steps = steps
        self.result = None
        self.ready = next(steps)

    def take(self, arrived):
        try:
            self.ready = self.steps.send(arrived)
        except StopIteration as stop:
            self.ready, self.result = [], stop.value

    def spread(self):
        return self.ready[0][0].ndim == 5


def send(order, *runs):
    values = order([[v for v, _ in run.ready] for run in runs])
    for run, given in zip(runs, values):
        run.values = given
        run.arrived = [move(v) for v, (_, move) in zip(given, run.ready)]


def take(order, *runs):
    arrived = order([run.arrived for run in runs])
    for run, got in zip(runs, arrived):
        run.take(got)


def take_all(order, run):
    take(order, run)
    while not run.spread():
        send(order, run)
        take(order, run)


def advance(order, *runs):
    take(order, *runs)
    ready = [run for run in runs if run.ready]
    if ready:
        send(order, *ready)


def member_columns(matrix, member, axis):
    return lax.dynamic_slice_in_dim(matrix, member * WIDTH, WIDTH, axis)


def body(
    inputs,
    cotangent,
    absent_groups,
    token_group,
    pre_gain,
    pre_shift,
    input_weight,
    input_bias,
    output_weight,
    output_bias,
    mid_gain,
    mid_shift,
    up_weight,
    up_bias,
    down_weight,
    down_bias,
):
    _, rows, model = inputs.shape
    hidden_units = up_weight.shape[1]
    cube, blk = lax.axis_index("cube"), lax.axis_index("blk")
    core = cube & 1
    pieces = lax.axis_size("cube") // 2
    where = jnp.stack([core, cube >> 1, blk]).astype(jnp.int32)
    at_home = core == (blk >> 1)
    member = 2 * core + (blk & 1)

    def moved(value):
        return jnp.where(at_home, value, sent_between(value, False, 1, 2))

    group_match = token_group[0][None, :] == jnp.arange(GROUPS, dtype=jnp.int32)[:, None]
    lacking = jnp.sum(jnp.where(group_match, absent_groups.reshape(GROUPS, 1), 0), axis=0)
    valid_here = (1 - lacking).astype(BF16)
    carried = jnp.concatenate(
        [inputs[0], jnp.broadcast_to(jnp.pad(valid_here, (0, model - rows)), (16, model))]
    )
    arriving = sent_between(carried, False, 1, 2)
    near_home = sent_between(carried, True, 0, 1)

    in_columns = jnp.concatenate(
        [member_columns(input_weight[:, s * model : (s + 1) * model], member, 1) for s in range(3)],
        axis=1,
    )
    bias_columns = member_columns(input_bias, member, 1)
    bias_columns = jnp.concatenate([bias_columns[0], jnp.zeros((WIDTH,), F32), bias_columns[1]])
    out_rows = jnp.stack([member_columns(output_weight, member ^ e, 0) for e in range(MEMBERS)])
    prepared = (in_columns, in_columns.T, bias_columns, bias_columns[:, None], out_rows)
    prepared, arriving = lax.optimization_barrier((prepared, arriving))
    in_columns, in_columns_turned, bias_columns, bias_turned, out_rows = prepared

    own = jnp.where(at_home, carried, arriving)
    near = jnp.where(at_home, near_home, sent_between(arriving, False, 0, 1))
    x_blocks = [own, near, over_cube(own, 0), over_cube(near, 0)]

    normed_low, qa, ka, va, kt, vt = project(
        x_blocks, rows, pre_gain, pre_shift, in_columns, in_columns_turned, bias_columns, bias_turned
    )
    qa, cot_here = lax.optimization_barrier((qa, cotangent[0]))
    cot_own = moved(cot_here)
    attended_own, turned, logs = attend(qa, ka, vt)
    attended = exchanged(attended_own)
    (
        layer_here,
        down_send,
        down_keep,
        rest_send,
        rest_keep,
        grad_up_bias,
        grad_hidden,
        *grad_attended,
        middle_vectors,
    ) = middle(
        where,
        pieces,
        own,
        attended,
        out_rows,
        output_bias,
        mid_gain,
        mid_shift,
        cot_own,
        down_bias,
        up_weight,
        up_bias,
        down_weight,
    )
    blocks = hidden_units // model
    order = Order(where)
    down, rest = Running(summing(down_keep, down_send)), Running(summing(rest_keep, rest_send))
    send(order, down)
    far, near_part = over_blk(grad_attended[3], 0), over_blk(grad_attended[1], 0)
    send(order, rest)
    advance(order, down)
    far, near_part = order((far, near_part))
    core_parts = (over_cube(grad_attended[2], 0), over_cube(far, 0))
    advance(order, rest)
    grads_here = [grad_attended[0], near_part, *order(core_parts)]
    layer_moved = sent_between(order(layer_here), False, 1, 2)
    columns = []

    def back(head):
        grads = order(grads_here)
        columns.extend(order(attend_back(head, qa, ka, va, kt, turned, logs, grads)))

    back(0)
    advance(order, down)
    back(1)
    advance(order, down)
    advance(order, rest)
    layer_out = jnp.where(at_home, layer_here, order(layer_moved))
    back(2)
    advance(order, down)
    advance(order, rest)
    p0, p1, p23, *in_parts, biases = order(
        unproject(where, order(columns), normed_low, in_columns, pieces)
    )
    vectors, extra = [], 16
    in_run = Running(summing_columns(in_parts, vectors, extra))
    closing_run = Running(closing(own, (p0, p1, p23), pre_gain, grad_hidden))
    send(order, in_run)
    send(order, closing_run)
    advance(order, down)
    advance(order, rest)
    advance(order, down)
    advance(order, in_run)
    pre_sums = in_vmem(
        pre_sums_kernel, [jax.ShapeDtypeStruct((2, model), F32)], *x_blocks, p0, p1, p23, name="pre_sums"
    )
    vectors += [*order(pre_sums), middle_vectors, biases, grad_up_bias]
    advance(order, in_run)
    advance(order, rest)
    advance(order, down)
    advance(order, in_run)
    advance(order, rest)
    advance(order, down)
    advance(order, in_run)
    advance(order, rest)
    take_all(order, down)
    advance(order, in_run)
    advance(order, closing_run)
    advance(order, rest)
    send(order, down)
    advance(order, in_run)
    advance(order, closing_run)
    take(order, down)
    (grad_down_weight,) = order(placed(order.token, down.values[0], down.result, [(hidden_units, model)]))
    take_all(order, rest)
    send(order, rest)
    take(order, closing_run)
    grad_here, grad_moved = closing_run.result
    input_grad = order(jnp.where(at_home, grad_here, grad_moved.astype(F32)))
    take_all(order, in_run)
    send(order, in_run)
    take(order, rest, in_run)
    (
        grad_up_weight,
        grad_output_weight,
        grad_input_weight,
        grad_pre_gain,
        grad_pre_shift,
        grad_mid_gain,
        grad_mid_shift,
        grad_output_bias,
        grad_down_bias,
        grad_input_bias,
        grad_up_bias,
    ) = placed_last(
        order.token, rest.values[0], rest.result, in_run.values[0], in_run.result, extra, hidden_units
    )
    return (
        layer_out[None],
        input_grad[None],
        grad_pre_gain,
        grad_pre_shift,
        grad_input_weight,
        grad_input_bias,
        grad_output_weight,
        grad_output_bias,
        grad_mid_gain,
        grad_mid_shift,
        grad_up_weight,
        grad_up_bias,
        grad_down_weight,
        grad_down_bias,
    )


def solution(mesh):
    rows_spec = P("cube", "blk", None)
    return jax.shard_map(
        body,
        mesh=mesh,
        in_specs=(rows_spec, rows_spec, P("cube", None), P("cube", "blk")) + (P(),) * 12,
        out_specs=(rows_spec, rows_spec) + (P(),) * 12,
        check_vma=False,
    )
```

```python
import functools
import jax
import jax.numpy as jnp
from jax import lax
from jax.experimental import pallas as pl
from jax.experimental.pallas import tpu as pltpu
from jax.sharding import PartitionSpec as P

HEADS = 12
HD = 64
GROUPS = 12
MEMBERS = 4
LOCAL_HEADS = HEADS // MEMBERS
WIDTH = LOCAL_HEADS * HD
NEG_FILL = -32768.0
EPSILON = 1e-06
BF16 = jnp.bfloat16
F32 = jnp.float32
TILE = 256
LANES = 128
VMEM = pltpu.VMEM
HBM = pltpu.MemorySpace.HBM
QUICK = pl.CostEstimate(flops=1, bytes_accessed=1, transcendentals=0)
LONG = pl.CostEstimate(flops=20_000_000_000, bytes_accessed=60_000_000, transcendentals=0)


def dot(left, right):
    return jnp.dot(left, right, preferred_element_type=F32)


def dot_nt(left, right):
    return lax.dot_general(left, right, (((1,), (1,)), ((), ())), preferred_element_type=F32)


def dot_tn(left, right):
    return lax.dot_general(left, right, (((0,), (0,)), ((), ())), preferred_element_type=F32)


def params(limit=60 << 20, **more):
    return pltpu.CompilerParams(vmem_limit_bytes=limit, **more)


def whole(*shape):
    return pl.BlockSpec(shape, lambda *_: (0,) * len(shape))


def normalized(values):
    centered = values - jnp.mean(values, axis=-1, keepdims=True)
    inverse = lax.rsqrt(jnp.mean(centered * centered, axis=-1, keepdims=True) + EPSILON)
    return centered * inverse, inverse


def streamed(steps):
    for ins, _, _ in steps:
        for copy in ins:
            copy.start()
    for ins, compute, outs in steps:
        for copy in ins:
            copy.wait()
        compute()
        for copy in outs:
            copy.start()
    for _, _, outs in steps:
        for copy in outs:
            copy.wait()


def mask_column(last, rows):
    return last[rows - packed_rows(rows) :, :rows].astype(F32).T[:, :1]


def rows_of(first, last, rows):
    top = first.shape[0]
    return jnp.concatenate([first[...], last[: rows - top, :]]).astype(F32)


def packing(rows):
    top = packed_rows(rows)
    return [(0, top, 0), (top, rows - top, WIDTH)]


def packed_rows(rows):
    return -(-rows // 32) * 16


def project_kernel(*refs):
    xs, (gain, shift, w, wt, bias, bias_col), refs = refs[:8], refs[8:14], refs[14:]
    results, held, (x_held, w_held, sem_in, sem_out) = refs[:6], refs[6:12], refs[12:]
    normed, qa, ka, va, kt, vt = held
    rows = normed.shape[0] // MEMBERS
    total = MEMBERS * rows
    padded = qa.shape[2]
    low_w = pltpu.make_async_copy(w, w_held.at[0], sem_in.at[MEMBERS, 0])
    steps = []
    for d in range(MEMBERS):
        here = pl.ds(d * rows, rows)

        def compute(d=d, here=here):
            part = x_held.at[d]

            for half, (at, size, _) in enumerate(packing(rows)):
                unit, _ = normalized(part[half, :size, :].astype(F32))
                normed[pl.ds(d * rows + at, size), :] = (unit * gain[...][None] + shift[...][None]).astype(BF16)
            natural = dot(normed[here, :], w_held[0, :, WIDTH:]) + bias[...][None, WIDTH:]
            lane = lax.broadcasted_iota(jnp.int32, (rows, HD), 1)
            low_mask = NEG_FILL * (1.0 - mask_column(part.at[1], rows))
            key_tail = jnp.where(lane == 0, low_mask, jnp.where(lane < 4, 1.0, 0.0)).astype(BF16)
            value_tail = jnp.where(lane < 3, 1.0, 0.0).astype(BF16)
            for h in range(LOCAL_HEADS):
                at = h * HD
                ka[h, here, :HD] = natural[:, at : at + HD].astype(BF16)
                ka[h, here, HD:] = key_tail
                va[h, here, :HD] = natural[:, WIDTH + at : WIDTH + at + HD].astype(BF16)
                va[h, here, HD:] = value_tail

        ins = [pltpu.make_async_copy(xs[2 * d + i], x_held.at[d, i], sem_in.at[d, i]) for i in range(2)]
        ins += [low_w] if d == 0 else []
        outs = [pltpu.make_async_copy(normed.at[here], results[0].at[here], sem_out.at[d, 0])]
        for i, at in enumerate((2, 3)):
            outs.append(
                pltpu.make_async_copy(held[at].at[:, here], results[at].at[:, here], sem_out.at[d, i + 1])
            )
        steps.append((ins, compute, outs))

    def turn():
        turned = dot_nt(wt[...], normed[...]) + bias_col[...]
        row = lax.broadcasted_iota(jnp.int32, (HD, padded), 0)
        query_tail = jnp.where(row == 0, 1.0, 0.0).astype(BF16)
        for h in range(LOCAL_HEADS):
            at = h * HD
            qa[h, :HD, :total] = (turned[at : at + HD] * HD ** (-0.5)).astype(BF16)
            qa[h, :HD, total:] = jnp.zeros((HD, padded - total), BF16)
            qa[h, HD:, :] = query_tail
            kt[h] = turned[WIDTH + at : WIDTH + at + HD].astype(BF16)
            vt[h] = turned[2 * WIDTH + at : 2 * WIDTH + at + HD].astype(BF16)

    outs = [
        pltpu.make_async_copy(held[at], results[at], sem_out.at[MEMBERS, i])
        for i, at in enumerate((1, 4, 5))
    ]
    steps.append(([], turn, outs))
    streamed(steps)


def prepare_kernel(w, bias, turned, bias_col):
    turned[...] = w[...].T
    bias_col[...] = jnp.broadcast_to(bias[...][None], (8, bias.shape[0])).T[:, :1]


def prepare(w, bias):
    model, width = w.shape
    outs = [jax.ShapeDtypeStruct((width, model), BF16), jax.ShapeDtypeStruct((width, 1), F32)]
    return in_vmem(prepare_kernel, outs, w, bias, name="prepare")


def project(x_blocks, rows, gain, shift, w, wt, bias, bias_col):
    model = x_blocks[0].shape[1]
    total = MEMBERS * rows
    padded = -(-total // TILE) * TILE
    n = LOCAL_HEADS
    outs = [
        jax.ShapeDtypeStruct((total, model), BF16),
        jax.ShapeDtypeStruct((n, 2 * HD, padded), BF16),
        jax.ShapeDtypeStruct((n, total, 2 * HD), BF16),
        jax.ShapeDtypeStruct((n, total, 2 * HD), BF16),
        jax.ShapeDtypeStruct((n, HD, total), BF16),
        jax.ShapeDtypeStruct((n, HD, total), BF16),
    ]
    anywhere, near = pl.BlockSpec(memory_space=pl.ANY), pl.BlockSpec(memory_space=VMEM)
    return pl.pallas_call(
        project_kernel,
        out_shape=outs,
        in_specs=[anywhere] * 8 + [near] * 2 + [anywhere] + [near] * 3,
        out_specs=[anywhere] * len(outs),
        scratch_shapes=[VMEM(o.shape, o.dtype) for o in outs]
        + [
            VMEM((MEMBERS, 2, *x_blocks[0].shape), BF16),
            VMEM((1, *w.shape), BF16),
            pltpu.SemaphoreType.DMA((MEMBERS + 1, 2)),
            pltpu.SemaphoreType.DMA((MEMBERS + 1, 3)),
        ],
        compiler_params=params(),
        cost_estimate=LONG,
        name="project",
    )(*x_blocks, gain, shift, w, wt, bias, bias_col)


def forward_kernel(qa, ka, vt, l0, l1, l2, l3, turned, logs, held, even, odd, top_even, top_odd):
    head = pl.program_id(0)
    rows = ka.shape[1] // MEMBERS
    tiles = qa.shape[2] // TILE

    def scored(i, out, top):
        here = pl.ds(pl.multiple_of(i * TILE, TILE), TILE)
        scores = dot(ka[0], qa[0, :, here])
        out[...] = scores
        top[...] = jnp.max(scores, axis=0, keepdims=True)

    def mixed_of(i, scores, top):
        here = pl.ds(pl.multiple_of(i * TILE, TILE), TILE)
        peak = top[...]
        weights = jnp.exp(scores[...] - peak)
        sums = jnp.sum(weights, axis=0, keepdims=True)
        mixed = dot(vt[0], weights.astype(BF16)) * (1.0 / sums)
        turned[0, :, here] = mixed
        logs[0, :, here] = peak + jnp.log(sums)
        held[here, :] = mixed.T.astype(BF16)

    scored(0, even, top_even)

    def pair(i, carry):
        scored(2 * i + 1, odd, top_odd)
        mixed_of(2 * i, even, top_even)
        scored(jnp.minimum(2 * i + 2, tiles - 1), even, top_even)
        mixed_of(2 * i + 1, odd, top_odd)
        return carry

    lax.fori_loop(0, tiles // 2, pair, 0)
    if tiles % 2:
        mixed_of(tiles - 1, even, top_even)
    for h in range(LOCAL_HEADS):

        @pl.when(head == h)
        def _(h=h):
            for d, low in enumerate((l0, l1, l2, l3)):
                for rows_at, size, lane in packing(rows):
                    at = d * rows + rows_at
                    low[:size, lane + h * HD : lane + (h + 1) * HD] = held[at : at + size, :]


def attend(qa, ka, vt):
    n, total, _ = ka.shape
    padded = qa.shape[2]
    rows = total // MEMBERS
    per_head = lambda *shape: pl.BlockSpec((1,) + shape, lambda h: (h, 0, 0))
    *low, turned, logs = pl.pallas_call(
        forward_kernel,
        grid=(n,),
        out_shape=[jax.ShapeDtypeStruct((packed_rows(rows), 2 * WIDTH), BF16)] * MEMBERS
        + [
            jax.ShapeDtypeStruct((n, HD, padded), F32),
            jax.ShapeDtypeStruct((n, 1, padded), F32),
        ],
        in_specs=[per_head(2 * HD, padded), per_head(total, 2 * HD), per_head(HD, total)],
        out_specs=[whole(packed_rows(rows), 2 * WIDTH)] * MEMBERS + [per_head(HD, padded), per_head(1, padded)],
        scratch_shapes=[VMEM((padded, HD), BF16), VMEM((total, TILE), F32), VMEM((total, TILE), F32)]
        + [VMEM((1, TILE), F32)] * 2,
        compiler_params=params(),
        cost_estimate=LONG,
        name="attend",
    )(qa, ka, vt)
    return low, turned, logs


def three_parts(row):
    high = row.astype(BF16).astype(F32)
    rest = row - high
    middle = rest.astype(BF16).astype(F32)
    return high, middle, rest - middle


def backward_kernel(
    head, qa, ka, va, kt, turned, logs, g0, g1, g2, g3, out_q, out_k, out_v, held_g, sum_k, sum_v, s0, s1, d0, d1
):
    total = ka.shape[1]
    rows = total // MEMBERS
    padded = qa.shape[2]
    tiles = padded // TILE
    for d, part in enumerate((g0, g1, g2, g3)):
        for rows_at, size, lane in packing(rows):
            at = d * rows + rows_at
            held_g[at : at + size, :] = part[:size, lane + head * HD : lane + (head + 1) * HD]
    held_g[total:, :] = jnp.zeros((padded - total, HD), BF16)
    sum_k[...] = jnp.zeros_like(sum_k)
    sum_v[...] = jnp.zeros_like(sum_v)
    row = lax.broadcasted_iota(jnp.int32, (HD, TILE), 0)

    def scored(i, probs_out, grads_out):
        here = pl.ds(pl.multiple_of(i * TILE, TILE), TILE)
        grad_turned = held_g[here, :].astype(F32).T
        delta = jnp.sum(grad_turned * turned[0, :, here], axis=0, keepdims=True)
        high, middle, least = three_parts(-logs[0, :, here])
        tail = jnp.where(row == 0, 1.0, jnp.where(row == 1, high, jnp.where(row == 2, middle, jnp.where(row == 3, least, 0.0))))
        query = jnp.concatenate([qa[0, :HD, here], tail.astype(BF16)], axis=0)
        probs_out[...] = dot(ka[0], query)
        high, middle, least = three_parts(-delta)
        tail = jnp.where(row == 0, high, jnp.where(row == 1, middle, jnp.where(row == 2, least, 0.0)))
        grad_tail = jnp.concatenate([grad_turned, tail], axis=0).astype(BF16)
        grads_out[...] = dot(va[0], grad_tail)

    def some(i, width, probs_in, grads_in):
        here = pl.ds(pl.multiple_of(i * TILE, TILE), TILE)
        probs = jnp.exp(probs_in[...])
        grad_scores = (probs * grads_in[...]).astype(BF16)
        grad_turned = held_g[here, :].astype(F32).T.astype(BF16)
        sum_v[...] += dot_nt(grad_turned, probs.astype(BF16))
        sum_k[...] += dot_nt(qa[0, :HD, here], grad_scores)
        query_grad = dot(kt[0], grad_scores) * HD ** (-0.5)
        out_q[pl.ds(pl.multiple_of(i * TILE, TILE), width), :] = query_grad.T.astype(BF16)[:width]

    def pair(i, carry):
        scored(2 * i + 1, s1, d1)
        some(2 * i, TILE, s0, d0)
        scored(2 * i + 2, s0, d0)
        some(2 * i + 1, TILE, s1, d1)
        return carry

    least = total - (tiles - 1) * TILE
    scored(0, s0, d0)
    lax.fori_loop(0, (tiles - 1) // 2, pair, 0)
    if tiles % 2 == 0:
        scored(tiles - 1, s1, d1)
        some(tiles - 2, TILE, s0, d0)
        some(tiles - 1, least, s1, d1)
    else:
        some(tiles - 1, least, s0, d0)
    out_k[...] = sum_k[...].T.astype(BF16)
    out_v[...] = sum_v[...].T.astype(BF16)


def attend_back(head, qa, ka, va, kt, turned, logs, grads):
    n, total, _ = ka.shape
    padded = qa.shape[2]
    per_head = lambda *shape: pl.BlockSpec((1,) + shape, lambda i: (head, 0, 0))
    return pl.pallas_call(
        functools.partial(backward_kernel, head),
        grid=(1,),
        out_shape=[jax.ShapeDtypeStruct((total, HD), BF16)] * 3,
        in_specs=[
            per_head(2 * HD, padded),
            per_head(total, 2 * HD),
            per_head(total, 2 * HD),
            per_head(HD, total),
            per_head(HD, padded),
            per_head(1, padded),
        ]
        + [whole(*grads[0].shape)] * MEMBERS,
        out_specs=[whole(total, HD)] * 3,
        scratch_shapes=[
            VMEM((padded, HD), BF16),
            VMEM((HD, total), F32),
            VMEM((HD, total), F32),
        ]
        + [VMEM((total, TILE), F32)] * 4,
        compiler_params=params(),
        cost_estimate=LONG,
        name="attend_back",
    )(qa, ka, va, kt, turned, logs, *grads)


def unproject_kernel(where, *refs):
    columns, normed, w = refs[:9], refs[9], refs[10]
    n0, n1, n23, a_send, a_keep, b_send, b_keep, sums = refs[11:19]
    held, held_normed, held_n, joint, grad, sem_in, sem_out = refs[19:]
    rows = n0.shape[0]
    here = [pl.ds(d * rows, rows) for d in range(MEMBERS)]
    steps = []
    for s in range(3):
        for h in range(LOCAL_HEADS):
            at = s * WIDTH + h * HD
            slot = 3 * h + s

            def put(at=at, slot=slot):
                joint[:, at : at + HD] = held[slot]

            steps.append(([pltpu.make_async_copy(columns[slot], held.at[slot], sem_in.at[slot])], put, []))
    for d in (2, 3, 1, 0):

        def back(d=d):
            held_n[d] = dot_nt(joint[here[d], :], w[...]).astype(BF16)

        place = (n0, n1, n23.at[0], n23.at[1])[d]
        ins = [pltpu.make_async_copy(normed, held_normed, sem_in.at[9])] if d == 0 else []
        steps.append((ins, back, [pltpu.make_async_copy(held_n.at[d], place, sem_out.at[d])]))

    def weights():
        whole_grad = dot_tn(joint[...], held_normed[...])
        count, each, model = grad.shape
        for i in range(count):
            grad[i] = whole_grad[i * each : (i + 1) * each]
        pieces = count // 2
        for r in range(pieces):
            for p in range(2):
                part = grad[(r ^ where[1]) * 2 + (p ^ (where[2] // 2))].astype(BF16)
                out = (a_keep, a_send)[r % 2]
                out[r // 2, p] = part[:, : model // 2]
                out = (b_keep, b_send)[2 * r // pieces]
                out[r % (pieces // 2), p] = part[:, model // 2 :]
        total = jnp.sum(joint[...].astype(F32), axis=0, keepdims=True)
        sums[...] = jnp.zeros_like(sums)
        for m in range(MEMBERS):

            @pl.when(2 * where[0] + where[2] % 2 == m)
            def _(m=m):
                sums[0:1, m * WIDTH : (m + 1) * WIDTH] = total[:, :WIDTH]
                sums[1:2, m * WIDTH : (m + 1) * WIDTH] = total[:, 2 * WIDTH :]

    steps.append(([], weights, []))
    streamed(steps)


def unproject(where, columns, normed, w, pieces):
    total, model = normed.shape
    rows = total // MEMBERS
    width = 3 * WIDTH
    each = width // pieces // 2
    shaped = jax.ShapeDtypeStruct
    outs = [shaped((rows, model), BF16)] * 2 + [shaped((2, rows, model), BF16)]
    outs += [shaped((pieces // 2, 2, each, model // 2), BF16)] * 4 + [shaped((2, model), F32)]
    anywhere, near = pl.BlockSpec(memory_space=pl.ANY), pl.BlockSpec(memory_space=VMEM)
    return pl.pallas_call(
        unproject_kernel,
        out_shape=outs,
        in_specs=[pl.BlockSpec(memory_space=pltpu.SMEM)] + [anywhere] * 10 + [near],
        out_specs=[anywhere] * 3 + [near] * 5,
        scratch_shapes=[
            VMEM((9, total, HD), BF16),
            VMEM((total, model), BF16),
            VMEM((MEMBERS, rows, model), BF16),
            VMEM((total, width), BF16),
            VMEM((2 * pieces, each, model), F32),
            pltpu.SemaphoreType.DMA((10,)),
            pltpu.SemaphoreType.DMA((MEMBERS,)),
        ],
        compiler_params=params(),
        cost_estimate=LONG,
        name="unproject",
    )(where, *columns, normed, w)


def pre_sums_kernel(*refs):
    xs, (n0, n1, n23, out) = refs[:8], refs[8:]
    rows = n0.shape[0]
    out[...] = jnp.zeros_like(out)
    for d, given in enumerate((n0, n1, n23.at[0], n23.at[1])):
        for (at, size, _), x in zip(packing(rows), xs[2 * d : 2 * d + 2]):
            unit, _ = normalized(x[:size, :].astype(F32))
            grad = given[at : at + size, :].astype(F32)
            out[0:1, :] += jnp.sum(grad * unit, axis=0, keepdims=True)
            out[1:2, :] += jnp.sum(grad, axis=0, keepdims=True)


def close_kernel(first, last, p0, p1, gain, hidden, grad, low):
    rows = hidden.shape[0]
    unit, inverse = normalized(rows_of(first, last, rows))
    given = p0[...].astype(F32) + p1[...].astype(F32)
    scaled = given * gain[...][None]
    inner = scaled - jnp.mean(scaled, axis=-1, keepdims=True)
    inner = inner - unit * jnp.mean(scaled * unit, axis=-1, keepdims=True)
    total = hidden[...] + inverse * inner
    grad[...] = total
    low[...] = total.astype(BF16)


def close(x, parts, gain, hidden):
    rows, model = hidden.shape
    shaped = jax.ShapeDtypeStruct
    return pl.pallas_call(
        close_kernel,
        out_shape=[shaped((rows, model), F32), shaped((rows, model), BF16)],
        in_specs=[pl.BlockSpec(memory_space=VMEM)] * 6,
        out_specs=[pl.BlockSpec(memory_space=VMEM)] * 2,
        compiler_params=params(),
        cost_estimate=LONG,
        name="close",
    )(*x, *parts, gain, hidden)


def middle_kernel(
    side, first, final, a0, a1, a2, a3, wo, out_bias, gain, shift, cot, down_bias, up, up_bias, down,
    layer, down_send, down_keep, rest_send, rest_keep, grad_up_bias, grad_hidden, g0, g1, g2, g3, vectors,
    hidden, normed, grad_down, total_out, total_grad, valid,
):
    step = pl.program_id(0)
    last = pl.num_programs(0) - 1
    half = pl.num_programs(0) // 2
    rows, model = cot.shape
    pieces = down_keep.shape[0]
    each = half * model // pieces
    share = model // each

    @pl.when(step == 0)
    def _():
        valid[...] = mask_column(final, rows)
        value = rows_of(first, final, rows) + out_bias[...][None]
        cuts = packing(rows)
        value += jnp.concatenate(
            [
                sum(dot(part[:size, lane : lane + WIDTH], wo[e]) for e, part in enumerate((a0, a1, a2, a3)))
                for _, size, lane in cuts
            ]
        )
        hidden[...] = value
        unit, _ = normalized(value)
        normed[...] = (unit * gain[...][None] + shift[...][None]).astype(BF16)
        low = (valid[...] * cot[...].astype(F32)).astype(BF16)
        grad_down[...] = low
        vectors[3:4, :] = jnp.sum(low.astype(F32), axis=0, keepdims=True)
        total_out[...] = value + down_bias[...][None]
        total_grad[...] = jnp.zeros_like(total_grad)

    gate = dot(normed[...], up[...]) + up_bias[0]
    below = 0.5 * (1.0 + lax.erf(gate * (0.5**0.5)))
    active = (gate * below).astype(BF16)
    slope = below + gate * (jnp.exp(-0.5 * gate * gate) * (0.5 / jnp.pi) ** 0.5)
    low = grad_down[...]
    grad_gate = (dot_nt(low, down[...]) * slope).astype(BF16)
    total_out[...] += dot(active, down[...])
    total_grad[...] += dot_nt(grad_gate, up[...])
    grad_up_bias[0] = jnp.sum(grad_gate.astype(F32), axis=0, keepdims=True)
    of_down = dot_tn(active, low).astype(BF16)
    of_up = dot_tn(normed[...], grad_gate).astype(BF16)
    few = each // MEMBERS
    for i in range(2 * half):

        @pl.when(step == i)
        def _(i=i):
            down_held, rest_held = (down_send, rest_send) if i < half else (down_keep, rest_keep)
            for j in range(share):
                piece = ((i % half) * share + j) ^ side[1]
                for z in range(MEMBERS):
                    at = j * each + z * few
                    down_held[piece, z ^ side[2]] = of_down[at : at + few]
                    rest_held[piece, z ^ side[2], :few, :] = of_up[at : at + few]

    @pl.when(step == last)
    def _():
        unit, inverse = normalized(hidden[...])
        layer[...] = (valid[...] * total_out[...]).astype(BF16)
        grad = total_grad[...]
        vectors[0:1, :] = jnp.sum(grad * unit, axis=0, keepdims=True)
        vectors[1:2, :] = jnp.sum(grad, axis=0, keepdims=True)
        scaled = grad * gain[...][None]
        inner = scaled - jnp.mean(scaled, axis=-1, keepdims=True)
        inner = inner - unit * jnp.mean(scaled * unit, axis=-1, keepdims=True)
        grad = grad_down[...].astype(F32) + inverse * inner
        grad_hidden[...] = grad
        branch = grad.astype(BF16)
        vectors[2:3, :] = jnp.sum(branch.astype(F32), axis=0, keepdims=True)
        parts = (a0, a1, a2, a3)
        count = pieces // 2
        some = WIDTH // count // MEMBERS
        for e, given in enumerate((g0, g1, g2, g3)):
            back = dot_nt(branch, wo[e]).astype(BF16)
            given[...] = jnp.zeros_like(given)
            for at, size, lane in packing(rows):
                given[:size, lane : lane + WIDTH] = back[at : at + size]
            held = rest_keep if e < 2 else rest_send
            place = ((side[2] % 2) ^ (e & 1)) * count
            of_out = sum(
                dot_tn(parts[e][:size, lane : lane + WIDTH], branch[at : at + size])
                for at, size, lane in packing(rows)
            ).astype(BF16)
            for j in range(count):
                for z in range(MEMBERS):
                    at = (j * MEMBERS + z) * some
                    held[(place + j) ^ side[1], z ^ side[2], few:, :] = of_out[at : at + some]


def middle(where, pieces, x, attended, wo, out_bias, gain, shift, cot, down_bias, up, up_bias, down):
    rows, model = cot.shape
    blocks = up.shape[1] // model
    half = blocks // 2

    def block_of(i, side):
        return lax.rem(i, half) + half * jnp.where(i < half, 1 - side[0], side[0])

    whole_s = lambda *shape: pl.BlockSpec(shape, lambda i, side: (0,) * len(shape))
    each = half * model // pieces // MEMBERS
    held = (pieces, MEMBERS, each, model)
    rest = (pieces, MEMBERS, each + 2 * WIDTH // pieces // MEMBERS, model)
    shaped = jax.ShapeDtypeStruct
    outs = [
        (shaped((rows, model), BF16), whole_s(rows, model)),
        (shaped(held, BF16), whole_s(*held)),
        (shaped(held, BF16), whole_s(*held)),
        (shaped(rest, BF16), whole_s(*rest)),
        (shaped(rest, BF16), whole_s(*rest)),
        (shaped((blocks, 1, model), F32), pl.BlockSpec((1, 1, model), lambda i, side: (block_of(i, side), 0, 0))),
        (shaped((rows, model), F32), whole_s(rows, model)),
    ]
    outs += [(shaped(attended[0].shape, BF16), whole_s(*attended[0].shape))] * MEMBERS
    outs += [(shaped((4, model), F32), whole_s(4, model))]
    return pl.pallas_call(
        middle_kernel,
        out_shape=[o[0] for o in outs],
        grid_spec=pltpu.PrefetchScalarGridSpec(
            num_scalar_prefetch=1,
            grid=(blocks,),
            in_specs=[whole_s(*x[0].shape)] * 2
            + [whole_s(*attended[0].shape)] * MEMBERS
            + [whole_s(MEMBERS, WIDTH, model)]
            + [whole_s(model)] * 3
            + [whole_s(rows, model), whole_s(model)]
            + [
                pl.BlockSpec((model, model), lambda i, side: (0, block_of(i, side))),
                pl.BlockSpec((1, 1, model), lambda i, side: (block_of(i, side), 0, 0)),
                pl.BlockSpec((model, model), lambda i, side: (block_of(i, side), 0)),
            ],
            out_specs=[o[1] for o in outs],
            scratch_shapes=[
                VMEM((rows, model), F32),
                VMEM((rows, model), BF16),
                VMEM((rows, model), BF16),
                VMEM((rows, model), F32),
                VMEM((rows, model), F32),
                VMEM((rows, 1), F32),
            ],
        ),
        compiler_params=params(),
        cost_estimate=LONG,
        name="middle",
    )(
        where,
        *x, *attended, wo, out_bias, gain, shift, cot, down_bias,
        up, up_bias.reshape(blocks, 1, model), down,
    )


def reversed_bits(index, count):
    bits = count.bit_length() - 1
    total = 0
    for bit in range(bits):
        total = total | (((index >> bit) & 1) << (bits - 1 - bit))
    return total


def place_steps(where, other, parts, cuts, outs, held_in, held, sem_in, sem_out):
    _, pieces, _, _, lanes = parts.shape
    model = 2 * lanes
    half = where[0] ^ other
    steps = []
    for r in range(pieces):
        piece = r ^ where[1]
        ins = [
            pltpu.make_async_copy(parts.at[i, at], held_in.at[other, r, i], sem_in.at[other, r, i])
            for i, at in enumerate((reversed_bits(r, pieces), r))
        ]

        def compute(r=r):
            for z in range(MEMBERS):
                given = reversed_bits(z ^ where[2], MEMBERS)
                for i in range(2):
                    for out, (start, size) in zip(held, cuts):
                        value = held_in[other, r, i, given, start : start + size, :]
                        out[other, r, z * size : (z + 1) * size, i * lanes : (i + 1) * lanes] = value.astype(F32)

        places = []
        for out, (_, size) in zip(outs, cuts):
            rows = size * MEMBERS
            if out.shape[1] == model:
                places.append(out.at[pl.ds((half * pieces + piece) * rows, rows)])
            else:
                share = model // rows
                column = half * (out.shape[1] // model // 2) + piece // share
                places.append(
                    out.at[
                        pl.ds(lax.rem(piece, share) * rows, rows),
                        pl.ds(pl.multiple_of(column * model, model), model),
                    ]
                )
        sends = [
            pltpu.make_async_copy(given.at[other, r], place, sem_out.at[other, r, i])
            for i, (given, place) in enumerate(zip(held, places))
        ]
        steps.append((ins, compute, sends))
    return steps


def cuts_of(parts, shapes):
    _, pieces, _, rows, lanes = parts.shape
    sizes = [shape[0] * shape[1] // (2 * lanes) // 2 // pieces // MEMBERS for shape in shapes]
    return [(sum(sizes[:i]), size) for i, size in enumerate(sizes)]


def place_scratch(parts, cuts):
    _, pieces, _, rows, lanes = parts.shape
    scratch = [VMEM((2, pieces, 2, MEMBERS, rows, lanes), BF16)]
    scratch += [VMEM((2, pieces, MEMBERS * size, 2 * lanes), F32) for _, size in cuts]
    return scratch + [
        pltpu.SemaphoreType.DMA((2, pieces, 2)),
        pltpu.SemaphoreType.DMA((2, pieces, len(cuts))),
    ]


def place_kernel(cuts, where, own, got, *refs):
    count = len(cuts)
    outs, held_in, held, sems = refs[:count], refs[count], refs[count + 1 : -2], refs[-2:]
    streamed(
        place_steps(where, 0, own, cuts, outs, held_in, held, *sems)
        + place_steps(where, 1, got, cuts, outs, held_in, held, *sems)
    )


def placed(where, own, got, shapes):
    cuts = cuts_of(own, shapes)
    anywhere = pl.BlockSpec(memory_space=pl.ANY)
    return pl.pallas_call(
        functools.partial(place_kernel, cuts),
        out_shape=[jax.ShapeDtypeStruct(shape, F32) for shape in shapes],
        in_specs=[pl.BlockSpec(memory_space=pltpu.SMEM)] + [anywhere] * 2,
        out_specs=[anywhere] * len(cuts),
        scratch_shapes=place_scratch(own, cuts),
        compiler_params=params(),
        cost_estimate=LONG,
        name="placed",
    )(where, own, got)


def place_last_kernel(cuts, where, own, got, in_own, in_got, *refs):
    count = len(cuts)
    outs, (out, *vectors), scratch = refs[:count], refs[count : count + 9], refs[count + 9 :]
    held_in, held, sems = scratch[0], scratch[1 : 1 + count], scratch[1 + count : 3 + count]
    in_held, columns, out_held, sem_in, sem_out = scratch[3 + count :]
    steps = place_steps(where, 0, own, cuts, outs, held_in, held, *sems)
    steps += place_steps(where, 1, got, cuts, outs, held_in, held, *sems)
    _, pieces, _, _, lanes = in_own.shape
    model = 2 * lanes
    each = columns.shape[2]
    totals = []

    def gather(other):
        total = 0.0
        for piece in range(pieces):
            for side in range(MEMBERS):
                r, z = piece ^ where[1], side ^ where[2]
                at = reversed_bits(z, MEMBERS)
                both = (in_held[other, 0, reversed_bits(r, pieces), at], in_held[other, 1, r, at])
                both = jnp.concatenate([v.astype(F32) for v in both], axis=1)
                columns[2 * other + side % 2, piece * 2 + side // 2] = both[:each]
                total = total + both[each:]
        totals.append(total)

    def turn(other, s):
        for m in range(2):
            given = columns[2 * other + m].reshape(3 * WIDTH, model)[s * WIDTH : (s + 1) * WIDTH]
            out_held[other, s, :, m * WIDTH : (m + 1) * WIDTH] = given.T

    for other, given in enumerate((in_own, in_got)):
        copy = pltpu.make_async_copy(given, in_held.at[other], sem_in.at[other])
        steps.append(([copy], functools.partial(gather, other), []))
        for s in range(3):
            at = s * model + (where[0] ^ other) * lanes
            place = out.at[:, pl.ds(pl.multiple_of(at, lanes), lanes)]
            copy = pltpu.make_async_copy(out_held.at[other, s], place, sem_out.at[other, s])
            steps.append(([], functools.partial(turn, other, s), [copy]))
    streamed(steps)
    total = totals[0] + totals[1]
    for i in range(6):
        vectors[i][...] = total[i]
    vectors[6][...] = total[6:8]
    for i in range(vectors[7].shape[0] // model):
        vectors[7][i * model : (i + 1) * model] = total[8 + i]


def placed_last(where, own, got, in_own, in_got, extra, hidden_units):
    _, pieces, _, rows, lanes = in_own.shape
    model = 2 * lanes
    shapes = [(model, hidden_units), (model, model)]
    cuts = cuts_of(own, shapes)
    vectors = [(model,)] * 6 + [(2, model), (hidden_units,)]
    anywhere, near = pl.BlockSpec(memory_space=pl.ANY), pl.BlockSpec(memory_space=VMEM)
    return pl.pallas_call(
        functools.partial(place_last_kernel, cuts),
        out_shape=[jax.ShapeDtypeStruct(shape, F32) for shape in shapes + [(model, 3 * model)] + vectors],
        in_specs=[pl.BlockSpec(memory_space=pltpu.SMEM)] + [anywhere] * 4,
        out_specs=[anywhere] * 3 + [near] * 8,
        scratch_shapes=place_scratch(own, cuts)
        + [
            VMEM((2, *in_own.shape), BF16),
            VMEM((MEMBERS, 2 * pieces, rows - extra, model), F32),
            VMEM((2, 3, model, lanes), F32),
            pltpu.SemaphoreType.DMA((2,)),
            pltpu.SemaphoreType.DMA((2, 3)),
        ],
        compiler_params=params(),
        cost_estimate=LONG,
        name="placed_last",
    )(where, own, got, in_own, in_got)


def plus(first, second):
    return (first.astype(F32) + second.astype(F32)).astype(BF16)


def fold_core_kernel(keep, got, a_send, a_keep, b_send, b_keep, held, held_out, sem_in, sem_out):
    pieces, _, _, lanes = keep.shape
    steps = []
    for p in range(pieces):
        ins = [
            pltpu.make_async_copy(keep.at[p], held.at[p], sem_in.at[p, 0]),
        ]

        def compute(p=p):
            total = plus(held[p], got[p])
            held_out[p, 0] = total[:, :, : lanes // 2]
            held_out[p, 1] = total[:, :, lanes // 2 :]

        first = (a_keep, a_send)[p % 2].at[p // 2]
        second = (b_keep, b_send)[2 * p // pieces].at[p % (pieces // 2)]
        outs = [
            pltpu.make_async_copy(held_out.at[p, i], place, sem_out.at[p, i])
            for i, place in enumerate((first, second))
        ]
        steps.append((ins, compute, outs))
    streamed(steps)


def fold_core(keep, got):
    pieces, quarters, rows, lanes = keep.shape
    half = (quarters, rows, lanes // 2)
    return pl.pallas_call(
        fold_core_kernel,
        out_shape=[jax.ShapeDtypeStruct((pieces // 2, *half), BF16)] * 4,
        in_specs=[pl.BlockSpec(memory_space=HBM), pl.BlockSpec(memory_space=VMEM)],
        out_specs=[pl.BlockSpec(memory_space=HBM)] * 4,
        scratch_shapes=[
            VMEM(keep.shape, BF16),
            VMEM((pieces, 2, *half), BF16),
            pltpu.SemaphoreType.DMA((pieces, 2)),
            pltpu.SemaphoreType.DMA((pieces, 2)),
        ],
        compiler_params=params(),
        cost_estimate=QUICK,
        name="fold_core",
    )(keep, got)


def fold_core_quarters_kernel(keep, got, send, kept, held, held_got, held_out, sem_in, sem_out):
    pieces, quarters = keep.shape[:2]
    steps = []
    for p in range(pieces):
        ins = [
            pltpu.make_async_copy(keep.at[p], held.at[p], sem_in.at[p, 0]),
            pltpu.make_async_copy(got.at[p], held_got.at[p], sem_in.at[p, 1]),
        ]

        def compute(p=p):
            for z in range(quarters):
                held_out[p, z % 2, z // 2] = plus(held[p, z], held_got[p, z])

        outs = [
            pltpu.make_async_copy(held_out.at[p, i], place.at[p], sem_out.at[p, i])
            for i, place in enumerate((kept, send))
        ]
        steps.append((ins, compute, outs))
    streamed(steps)


def fold_core_quarters(keep, got):
    pieces, quarters, rows, lanes = keep.shape
    half = (quarters // 2, rows, lanes)
    return pl.pallas_call(
        fold_core_quarters_kernel,
        out_shape=[jax.ShapeDtypeStruct((pieces, *half), BF16)] * 2,
        in_specs=[pl.BlockSpec(memory_space=pl.ANY)] * 2,
        out_specs=[pl.BlockSpec(memory_space=pl.ANY)] * 2,
        scratch_shapes=[
            VMEM(keep.shape, BF16),
            VMEM(keep.shape, BF16),
            VMEM((pieces, 2, *half), BF16),
            pltpu.SemaphoreType.DMA((pieces, 2)),
            pltpu.SemaphoreType.DMA((pieces, 2)),
        ],
        compiler_params=params(),
        cost_estimate=QUICK,
        name="fold_core_quarters",
    )(keep, got)


def fold_halves_kernel(keep, got, send, kept):
    for p in range(keep.shape[0]):
        kept[p] = plus(keep[p, 0], got[p, 0])
        send[p] = plus(keep[p, 1], got[p, 1])


def fold_halves(keep, got):
    pieces, _, rows, lanes = keep.shape
    outs = [jax.ShapeDtypeStruct((pieces, rows, lanes), BF16)] * 2
    return in_vmem(fold_halves_kernel, outs, keep, got, name="fold_halves")


def fold_pieces_kernel(keep, got, a_send, a_keep, b_send, b_keep):
    pieces, _, model = keep.shape
    for r in range(pieces):
        total = plus(keep[r], got[r])
        out = (a_keep, a_send)[r % 2]
        out[r // 2, 0] = total[:, : model // 2]
        out = (b_keep, b_send)[2 * r // pieces]
        out[r % (pieces // 2), 0] = total[:, model // 2 :]


def fold_pieces(keep, got):
    pieces, rows, model = keep.shape
    outs = [jax.ShapeDtypeStruct((pieces // 2, 1, rows, model // 2), BF16)] * 4
    return in_vmem(fold_pieces_kernel, outs, keep, got, name="fold_pieces")


def join_planes_kernel(ak, ag, bk, bg, out):
    count = ak.shape[0]
    for r in range(count):
        out[0, r], out[0, count + r] = ak[r], ag[r]
        out[1, r], out[1, count + r] = bk[r], bg[r]


def join_planes(ak, ag, bk, bg):
    count, *rest = ak.shape
    outs = [jax.ShapeDtypeStruct((2, 2 * count, *rest), BF16)]
    return in_vmem(join_planes_kernel, outs, ak, ag, bk, bg, name="join_planes")[0]


def fold_in_kernel(keep, got, pre, mid, biases, up_bias, out):
    rows = keep.shape[1]
    out[:rows, :] = plus(keep[0], got[0])
    vectors = [pre[...], mid[...], biases[...]] + [up_bias[i] for i in range(up_bias.shape[0])]
    count = sum(v.shape[0] for v in vectors)
    filled = vectors + [jnp.zeros((out.shape[0] - rows - count, out.shape[1]), F32)]
    out[rows:, :] = jnp.concatenate(filled).astype(BF16)


def fold_in(keep, got, vectors, extra):
    _, rows, lanes = keep.shape
    outs = [jax.ShapeDtypeStruct((rows + extra, lanes), BF16)]
    return in_vmem(fold_in_kernel, outs, keep, got, *vectors, name="fold_in")[0]


def in_vmem(kernel, outs, *values, name):
    return pl.pallas_call(
        kernel,
        out_shape=outs,
        in_specs=[pl.BlockSpec(memory_space=VMEM)] * len(values),
        out_specs=[pl.BlockSpec(memory_space=VMEM)] * len(outs),
        compiler_params=params(),
        cost_estimate=QUICK,
        name=name,
    )(*values)


def fold_planes_kernel(ak, ag, bk, bg, a_send, a_keep, b_send, b_keep):
    count = ak.shape[0]
    for r in range(count):
        out = (a_keep, a_send)[r % 2]
        out[r // 2] = plus(ak[r], ag[r])
        out = (b_keep, b_send)[2 * r // count]
        out[r % (count // 2)] = plus(bk[r], bg[r])


def fold_last_kernel(ak, ag, bk, bg, send, keep=None):
    quarters = ak.shape[1]
    lanes = ak.shape[3]
    keep = send if keep is None else keep
    for z in range(quarters):
        out = (keep, send)[z % 2]
        out[z // 2, :, :lanes] = plus(ak[0, z], ag[0, z])
        out[z // 2, :, lanes:] = plus(bk[0, z], bg[0, z])


def fold_planes(ak, ag, bk, bg):
    count, quarters, rows, lanes = ak.shape
    if count > 1:
        outs = [jax.ShapeDtypeStruct((count // 2, quarters, rows, lanes), BF16)] * 4
        return in_vmem(fold_planes_kernel, outs, ak, ag, bk, bg, name="fold_planes")
    outs = [jax.ShapeDtypeStruct((-(-quarters // 2), rows, 2 * lanes), BF16)] * min(quarters, 2)
    return in_vmem(fold_last_kernel, outs, ak, ag, bk, bg, name="fold_last")


def fold_quarters_kernel(keep, got, *outs):
    for z in range(keep.shape[0]):
        out = outs[len(outs) - 1 - z]
        out[...] = plus(keep[z], got[z])


def fold_quarters(keep, got):
    count, rows, lanes = keep.shape
    outs = [jax.ShapeDtypeStruct((rows, lanes), BF16)] * count
    return in_vmem(fold_quarters_kernel, outs, keep, got, name="fold_quarters")


def over_cube(value, bit):
    count = lax.axis_size("cube")
    return lax.ppermute(value, "cube", [(i, i ^ (1 << bit)) for i in range(count)])


def over_blk(value, bit):
    return lax.ppermute(value, "blk", [(i, i ^ (1 << bit)) for i in range(MEMBERS)])


def chosen_pairs(is_home, cube_flip, blk_flip):
    pairs = []
    for c in range(lax.axis_size("cube")):
        for b in range(MEMBERS):
            if ((c & 1) == (b >> 1)) == is_home:
                pairs.append((c * MEMBERS + b, (c ^ cube_flip) * MEMBERS + (b ^ blk_flip)))
    return pairs


def sent_between(value, is_home, cube_flip, blk_flip):
    return lax.ppermute(value, ("cube", "blk"), chosen_pairs(is_home, cube_flip, blk_flip))


def exchanged(parts):
    far = over_blk(parts[3], 0)
    near = over_blk(parts[1], 0)
    core = over_cube(parts[2], 0)
    return [parts[0], near, core, over_cube(far, 0)]


def cube_bits():
    return list(range(1, lax.axis_size("cube").bit_length() - 1))


def by_cube(bit):
    return functools.partial(over_cube, bit=bit)


def by_blk(bit):
    return functools.partial(over_blk, bit=bit)


def scattering(a_send, a_keep, b_send, b_keep):
    for low, high in zip(cube_bits(), cube_bits()[::-1]):
        a_got, b_got = yield [(a_send, by_cube(low)), (b_send, by_cube(high))]
        *folded, = fold_planes(a_keep, a_got, b_keep, b_got)
        if len(folded) <= 2:
            return folded
        a_send, a_keep, b_send, b_keep = folded


def spreading(shard):
    (got,) = yield [(shard, by_blk(1))]
    both = jnp.stack([shard, got])
    (got,) = yield [(both, by_blk(0))]
    both = jnp.concatenate([both, got])[None]
    lanes = both.shape[3] // 2
    a_part, b_part = both[..., :lanes], both[..., lanes:]
    for low, high in zip(cube_bits(), cube_bits()[::-1]):
        a_got, b_got = yield [(a_part, by_cube(high)), (b_part, by_cube(low))]
        if low == cube_bits()[-1]:
            break
        a_part, b_part = jnp.concatenate([a_part, a_got]), jnp.concatenate([b_part, b_got])
    (got,) = yield [(join_planes(a_part, a_got, b_part, b_got), by_cube(0))]
    return got


def summing(keep, send):
    (got,) = yield [(send, by_cube(0))]
    send, keep = yield from scattering(*fold_core(keep, got))
    (got,) = yield [(send, by_blk(0))]
    send, keep = fold_quarters(keep, got)
    (got,) = yield [(send, by_blk(1))]
    return (yield from spreading(plus(keep, got)))


def summing_columns(parts, vectors, extra):
    send, keep = yield from scattering(*parts)
    (got,) = yield [(send, by_blk(1))]
    return (yield from spreading(fold_in(keep, got, vectors, extra)))


def closing(own, parts, gain, grad_hidden):
    p0, p1, p23 = parts
    (got,) = yield [(p23, by_cube(0))]
    near_sum, own_sum = plus(p1, got[1]), plus(p0, got[0])
    (got,) = yield [(near_sum, by_blk(0))]
    grad_here, grad_low = close(own, [own_sum, got], gain, grad_hidden)
    (moved,) = yield [(grad_low, lambda v: sent_between(v, False, 1, 2))]
    return grad_here, moved


class Order:
    def __init__(self, token):
        self.token = token

    def __call__(self, values):
        values, self.token = lax.optimization_barrier((values, self.token))
        return values


class Running:
    def __init__(self, steps):
        self.steps = steps
        self.result = None
        self.ready = next(steps)

    def take(self, arrived):
        try:
            self.ready = self.steps.send(arrived)
        except StopIteration as stop:
            self.ready, self.result = [], stop.value

    def spread(self):
        return self.ready[0][0].ndim == 5


def send(order, *runs):
    values = order([[v for v, _ in run.ready] for run in runs])
    for run, given in zip(runs, values):
        run.values = given
        run.arrived = [move(v) for v, (_, move) in zip(given, run.ready)]


def take(order, *runs):
    arrived = order([run.arrived for run in runs])
    for run, got in zip(runs, arrived):
        run.take(got)


def take_all(order, run):
    take(order, run)
    while not run.spread():
        send(order, run)
        take(order, run)


def advance(order, *runs):
    take(order, *runs)
    ready = [run for run in runs if run.ready]
    if ready:
        send(order, *ready)


def member_columns(matrix, member, axis):
    return lax.dynamic_slice_in_dim(matrix, member * WIDTH, WIDTH, axis)


def body(
    inputs,
    cotangent,
    absent_groups,
    token_group,
    pre_gain,
    pre_shift,
    input_weight,
    input_bias,
    output_weight,
    output_bias,
    mid_gain,
    mid_shift,
    up_weight,
    up_bias,
    down_weight,
    down_bias,
):
    _, rows, model = inputs.shape
    hidden_units = up_weight.shape[1]
    cube, blk = lax.axis_index("cube"), lax.axis_index("blk")
    core = cube & 1
    pieces = lax.axis_size("cube") // 2
    where = jnp.stack([core, cube >> 1, blk]).astype(jnp.int32)
    at_home = core == (blk >> 1)
    member = 2 * core + (blk & 1)

    def moved(value):
        return jnp.where(at_home, value, sent_between(value, False, 1, 2))

    group_match = token_group[0][None, :] == jnp.arange(GROUPS, dtype=jnp.int32)[:, None]
    lacking = jnp.sum(jnp.where(group_match, absent_groups.reshape(GROUPS, 1), 0), axis=0)
    valid_here = (1 - lacking).astype(BF16)
    top = packed_rows(rows)
    mask_rows = jnp.broadcast_to(jnp.pad(valid_here, (0, model - rows)), (2 * top - rows, model))
    carried = [inputs[0, :top], jnp.concatenate([inputs[0, top:], mask_rows])]
    arriving = [sent_between(part, False, 1, 2) for part in carried]
    near_home = [sent_between(part, True, 0, 1) for part in carried]

    in_columns = jnp.concatenate(
        [member_columns(input_weight[:, s * model : (s + 1) * model], member, 1) for s in range(3)],
        axis=1,
    )
    bias_columns = member_columns(input_bias, member, 1)
    bias_columns = jnp.concatenate([bias_columns[0], jnp.zeros((WIDTH,), F32), bias_columns[1]])
    out_rows = jnp.stack([member_columns(output_weight, member ^ e, 0) for e in range(MEMBERS)])
    prepared = (in_columns, *prepare(in_columns, bias_columns), bias_columns, out_rows)
    prepared, arriving[1] = lax.optimization_barrier((prepared, arriving[1]))
    in_columns, in_columns_turned, bias_turned, bias_columns, out_rows = prepared

    own, near = [], []
    for given, moved_in, from_home in zip(carried, arriving, near_home):
        own.append(jnp.where(at_home, given, moved_in))
        near.append(jnp.where(at_home, from_home, sent_between(moved_in, False, 0, 1)))
    x_blocks = [*own, *near]
    x_blocks += [over_cube(part, 0) for part in own] + [over_cube(part, 0) for part in near]

    normed_low, qa, ka, va, kt, vt = project(
        x_blocks, rows, pre_gain, pre_shift, in_columns, in_columns_turned, bias_columns, bias_turned
    )
    qa, cot_here = lax.optimization_barrier((qa, cotangent[0]))
    cot_own = moved(cot_here)
    attended_own, turned, logs = attend(qa, ka, vt)
    attended = exchanged(attended_own)
    (
        layer_here,
        down_send,
        down_keep,
        rest_send,
        rest_keep,
        grad_up_bias,
        grad_hidden,
        *grad_attended,
        middle_vectors,
    ) = middle(
        where,
        pieces,
        own,
        attended,
        out_rows,
        output_bias,
        mid_gain,
        mid_shift,
        cot_own,
        down_bias,
        up_weight,
        up_bias,
        down_weight,
    )
    blocks = hidden_units // model
    order = Order(where)
    down, rest = Running(summing(down_keep, down_send)), Running(summing(rest_keep, rest_send))
    send(order, down)
    far, near_part = over_blk(grad_attended[3], 0), over_blk(grad_attended[1], 0)
    send(order, rest)
    advance(order, down)
    far, near_part = order((far, near_part))
    core_parts = (over_cube(grad_attended[2], 0), over_cube(far, 0))
    advance(order, rest)
    grads_here = [grad_attended[0], near_part, *order(core_parts)]
    layer_moved = sent_between(order(layer_here), False, 1, 2)
    columns = []

    def back(head):
        grads = order(grads_here)
        columns.extend(order(attend_back(head, qa, ka, va, kt, turned, logs, grads)))

    back(0)
    advance(order, down)
    back(1)
    advance(order, down)
    advance(order, rest)
    layer_out = jnp.where(at_home, layer_here, order(layer_moved))
    back(2)
    advance(order, down)
    advance(order, rest)
    p0, p1, p23, *in_parts, biases = order(
        unproject(where, order(columns), normed_low, in_columns, pieces)
    )
    vectors, extra = [], 16
    in_run = Running(summing_columns(in_parts, vectors, extra))
    closing_run = Running(closing(own, (p0, p1, p23), pre_gain, grad_hidden))
    send(order, in_run)
    send(order, closing_run)
    advance(order, down)
    advance(order, rest)
    advance(order, down)
    advance(order, in_run)
    pre_sums = in_vmem(
        pre_sums_kernel, [jax.ShapeDtypeStruct((2, model), F32)], *x_blocks, p0, p1, p23, name="pre_sums"
    )
    vectors += [*order(pre_sums), middle_vectors, biases, grad_up_bias]
    advance(order, in_run)
    advance(order, rest)
    advance(order, down)
    advance(order, in_run)
    advance(order, rest)
    advance(order, down)
    advance(order, in_run)
    advance(order, rest)
    take_all(order, down)
    advance(order, in_run)
    advance(order, closing_run)
    advance(order, rest)
    send(order, down)
    advance(order, in_run)
    advance(order, closing_run)
    take(order, down)
    take_all(order, rest)
    send(order, rest)
    (grad_down_weight,) = order(placed(order.token, down.values[0], down.result, [(hidden_units, model)]))
    take(order, closing_run)
    grad_here, grad_moved = closing_run.result
    input_grad = order(jnp.where(at_home, grad_here, grad_moved.astype(F32)))
    take_all(order, in_run)
    send(order, in_run)
    take(order, rest, in_run)
    (
        grad_up_weight,
        grad_output_weight,
        grad_input_weight,
        grad_pre_gain,
        grad_pre_shift,
        grad_mid_gain,
        grad_mid_shift,
        grad_output_bias,
        grad_down_bias,
        grad_input_bias,
        grad_up_bias,
    ) = placed_last(
        order.token, rest.values[0], rest.result, in_run.values[0], in_run.result, extra, hidden_units
    )
    return (
        layer_out[None],
        input_grad[None],
        grad_pre_gain,
        grad_pre_shift,
        grad_input_weight,
        grad_input_bias,
        grad_output_weight,
        grad_output_bias,
        grad_mid_gain,
        grad_mid_shift,
        grad_up_weight,
        grad_up_bias,
        grad_down_weight,
        grad_down_bias,
    )


def solution(mesh):
    rows_spec = P("cube", "blk", None)
    return jax.shard_map(
        body,
        mesh=mesh,
        in_specs=(rows_spec, rows_spec, P("cube", None), P("cube", "blk")) + (P(),) * 12,
        out_specs=(rows_spec, rows_spec) + (P(),) * 12,
        check_vma=False,
    )
```

```python
import functools
import jax
import jax.numpy as jnp
from jax import lax
from jax.experimental import pallas as pl
from jax.experimental.pallas import tpu as pltpu
from jax.sharding import PartitionSpec as P

HEADS = 12
HD = 64
GROUPS = 12
MEMBERS = 4
LOCAL_HEADS = HEADS // MEMBERS
WIDTH = LOCAL_HEADS * HD
NEG_FILL = -32768.0
EPSILON = 1e-06
BF16 = jnp.bfloat16
F32 = jnp.float32
TILE = 256
LANES = 128
VMEM = pltpu.VMEM
HBM = pltpu.MemorySpace.HBM
QUICK = pl.CostEstimate(flops=1_000_000_000, bytes_accessed=3_000_000, transcendentals=0)
LONG = pl.CostEstimate(flops=60_000_000_000, bytes_accessed=180_000_000, transcendentals=0)


def dot(left, right):
    return jnp.dot(left, right, preferred_element_type=F32)


def dot_nt(left, right):
    return lax.dot_general(left, right, (((1,), (1,)), ((), ())), preferred_element_type=F32)


def dot_tn(left, right):
    return lax.dot_general(left, right, (((0,), (0,)), ((), ())), preferred_element_type=F32)


def params(limit=60 << 20, **more):
    return pltpu.CompilerParams(vmem_limit_bytes=limit, **more)


def whole(*shape):
    return pl.BlockSpec(shape, lambda *_: (0,) * len(shape))


def normalized(values):
    centered = values - jnp.mean(values, axis=-1, keepdims=True)
    inverse = lax.rsqrt(jnp.mean(centered * centered, axis=-1, keepdims=True) + EPSILON)
    return centered * inverse, inverse


def streamed(steps):
    for ins, _, _ in steps:
        for copy in ins:
            copy.start()
    for ins, compute, outs in steps:
        for copy in ins:
            copy.wait()
        compute()
        for copy in outs:
            copy.start()
    for _, _, outs in steps:
        for copy in outs:
            copy.wait()


def mask_column(last, rows):
    return last[rows - packed_rows(rows) :, :rows].astype(F32).T[:, :1]


def rows_of(first, last, rows):
    top = first.shape[0]
    return jnp.concatenate([first[...], last[: rows - top, :]]).astype(F32)


def packing(rows):
    top = packed_rows(rows)
    return [(0, top, 0), (top, rows - top, WIDTH)]


def packed_rows(rows):
    return -(-rows // 32) * 16


def project_kernel(*refs):
    xs, (gain, shift, w, wt, bias, bias_col), refs = refs[:8], refs[8:14], refs[14:]
    results, held, (x_held, w_held, sem_in, sem_out) = refs[:6], refs[6:12], refs[12:]
    normed, qa, ka, va, kt, vt = held
    rows = normed.shape[0] // MEMBERS
    total = MEMBERS * rows
    padded = qa.shape[2]
    low_w = pltpu.make_async_copy(w, w_held.at[0], sem_in.at[MEMBERS, 0])
    steps = []
    for d in range(MEMBERS):
        here = pl.ds(d * rows, rows)

        def compute(d=d, here=here):
            part = x_held.at[d]

            for half, (at, size, _) in enumerate(packing(rows)):
                unit, _ = normalized(part[half, :size, :].astype(F32))
                normed[pl.ds(d * rows + at, size), :] = (unit * gain[...][None] + shift[...][None]).astype(BF16)
            natural = dot(normed[here, :], w_held[0, :, WIDTH:]) + bias[...][None, WIDTH:]
            lane = lax.broadcasted_iota(jnp.int32, (rows, HD), 1)
            low_mask = NEG_FILL * (1.0 - mask_column(part.at[1], rows))
            key_tail = jnp.where(lane == 0, low_mask, jnp.where(lane < 4, 1.0, 0.0)).astype(BF16)
            value_tail = jnp.where(lane < 3, 1.0, 0.0).astype(BF16)
            for h in range(LOCAL_HEADS):
                at = h * HD
                ka[h, here, :HD] = natural[:, at : at + HD].astype(BF16)
                ka[h, here, HD:] = key_tail
                va[h, here, :HD] = natural[:, WIDTH + at : WIDTH + at + HD].astype(BF16)
                va[h, here, HD:] = value_tail

        ins = [pltpu.make_async_copy(xs[2 * d + i], x_held.at[d, i], sem_in.at[d, i]) for i in range(2)]
        ins += [low_w] if d == 0 else []
        outs = [pltpu.make_async_copy(normed.at[here], results[0].at[here], sem_out.at[d, 0])]
        for i, at in enumerate((2, 3)):
            outs.append(
                pltpu.make_async_copy(held[at].at[:, here], results[at].at[:, here], sem_out.at[d, i + 1])
            )
        steps.append((ins, compute, outs))

    def turn():
        turned = dot_nt(wt[...], normed[...]) + bias_col[...]
        row = lax.broadcasted_iota(jnp.int32, (HD, padded), 0)
        query_tail = jnp.where(row == 0, 1.0, 0.0).astype(BF16)
        for h in range(LOCAL_HEADS):
            at = h * HD
            qa[h, :HD, :total] = (turned[at : at + HD] * HD ** (-0.5)).astype(BF16)
            qa[h, :HD, total:] = jnp.zeros((HD, padded - total), BF16)
            qa[h, HD:, :] = query_tail
            kt[h] = turned[WIDTH + at : WIDTH + at + HD].astype(BF16)
            vt[h] = turned[2 * WIDTH + at : 2 * WIDTH + at + HD].astype(BF16)

    outs = [
        pltpu.make_async_copy(held[at], results[at], sem_out.at[MEMBERS, i])
        for i, at in enumerate((1, 4, 5))
    ]
    steps.append(([], turn, outs))
    streamed(steps)


def prepare_kernel(w, bias, turned, bias_col):
    turned[...] = w[...].T
    bias_col[...] = jnp.broadcast_to(bias[...][None], (8, bias.shape[0])).T[:, :1]


def prepare(w, bias):
    model, width = w.shape
    outs = [jax.ShapeDtypeStruct((width, model), BF16), jax.ShapeDtypeStruct((width, 1), F32)]
    return in_vmem(prepare_kernel, outs, w, bias, name="prepare")


def project(x_blocks, rows, gain, shift, w, wt, bias, bias_col):
    model = x_blocks[0].shape[1]
    total = MEMBERS * rows
    padded = -(-total // TILE) * TILE
    n = LOCAL_HEADS
    outs = [
        jax.ShapeDtypeStruct((total, model), BF16),
        jax.ShapeDtypeStruct((n, 2 * HD, padded), BF16),
        jax.ShapeDtypeStruct((n, total, 2 * HD), BF16),
        jax.ShapeDtypeStruct((n, total, 2 * HD), BF16),
        jax.ShapeDtypeStruct((n, HD, total), BF16),
        jax.ShapeDtypeStruct((n, HD, total), BF16),
    ]
    anywhere, near = pl.BlockSpec(memory_space=pl.ANY), pl.BlockSpec(memory_space=VMEM)
    return pl.pallas_call(
        project_kernel,
        out_shape=outs,
        in_specs=[anywhere] * 8 + [near] * 2 + [anywhere] + [near] * 3,
        out_specs=[anywhere] * len(outs),
        scratch_shapes=[VMEM(o.shape, o.dtype) for o in outs]
        + [
            VMEM((MEMBERS, 2, *x_blocks[0].shape), BF16),
            VMEM((1, *w.shape), BF16),
            pltpu.SemaphoreType.DMA((MEMBERS + 1, 2)),
            pltpu.SemaphoreType.DMA((MEMBERS + 1, 3)),
        ],
        compiler_params=params(),
        cost_estimate=LONG,
        name="project",
    )(*x_blocks, gain, shift, w, wt, bias, bias_col)


def forward_kernel(qa, ka, vt, l0, l1, l2, l3, turned, logs, held, even, odd, top_even, top_odd):
    head = pl.program_id(0)
    rows = ka.shape[1] // MEMBERS
    tiles = qa.shape[2] // TILE

    def scored(i, out, top):
        here = pl.ds(pl.multiple_of(i * TILE, TILE), TILE)
        scores = dot(ka[0], qa[0, :, here])
        out[...] = scores
        top[...] = jnp.max(scores, axis=0, keepdims=True)

    def mixed_of(i, scores, top):
        here = pl.ds(pl.multiple_of(i * TILE, TILE), TILE)
        peak = top[...]
        weights = jnp.exp(scores[...] - peak)
        sums = jnp.sum(weights, axis=0, keepdims=True)
        mixed = dot(vt[0], weights.astype(BF16)) * (1.0 / sums)
        turned[0, :, here] = mixed
        logs[0, :, here] = peak + jnp.log(sums)
        held[here, :] = mixed.T.astype(BF16)

    scored(0, even, top_even)

    def pair(i, carry):
        scored(2 * i + 1, odd, top_odd)
        mixed_of(2 * i, even, top_even)
        scored(jnp.minimum(2 * i + 2, tiles - 1), even, top_even)
        mixed_of(2 * i + 1, odd, top_odd)
        return carry

    lax.fori_loop(0, tiles // 2, pair, 0)
    if tiles % 2:
        mixed_of(tiles - 1, even, top_even)
    for h in range(LOCAL_HEADS):

        @pl.when(head == h)
        def _(h=h):
            for d, low in enumerate((l0, l1, l2, l3)):
                for rows_at, size, lane in packing(rows):
                    at = d * rows + rows_at
                    low[:size, lane + h * HD : lane + (h + 1) * HD] = held[at : at + size, :]


def attend(qa, ka, vt):
    n, total, _ = ka.shape
    padded = qa.shape[2]
    rows = total // MEMBERS
    per_head = lambda *shape: pl.BlockSpec((1,) + shape, lambda h: (h, 0, 0))
    *low, turned, logs = pl.pallas_call(
        forward_kernel,
        grid=(n,),
        out_shape=[jax.ShapeDtypeStruct((packed_rows(rows), 2 * WIDTH), BF16)] * MEMBERS
        + [
            jax.ShapeDtypeStruct((n, HD, padded), F32),
            jax.ShapeDtypeStruct((n, 1, padded), F32),
        ],
        in_specs=[per_head(2 * HD, padded), per_head(total, 2 * HD), per_head(HD, total)],
        out_specs=[whole(packed_rows(rows), 2 * WIDTH)] * MEMBERS + [per_head(HD, padded), per_head(1, padded)],
        scratch_shapes=[VMEM((padded, HD), BF16), VMEM((total, TILE), F32), VMEM((total, TILE), F32)]
        + [VMEM((1, TILE), F32)] * 2,
        compiler_params=params(),
        cost_estimate=LONG,
        name="attend",
    )(qa, ka, vt)
    return low, turned, logs


def three_parts(row):
    high = row.astype(BF16).astype(F32)
    rest = row - high
    middle = rest.astype(BF16).astype(F32)
    return high, middle, rest - middle


def backward_kernel(
    head, qa, ka, va, kt, turned, logs, g0, g1, g2, g3, out_q, out_k, out_v, held_g, sum_k, sum_v, s0, s1, d0, d1
):
    total = ka.shape[1]
    rows = total // MEMBERS
    padded = qa.shape[2]
    tiles = padded // TILE
    for d, part in enumerate((g0, g1, g2, g3)):
        for rows_at, size, lane in packing(rows):
            at = d * rows + rows_at
            held_g[at : at + size, :] = part[:size, lane + head * HD : lane + (head + 1) * HD]
    held_g[total:, :] = jnp.zeros((padded - total, HD), BF16)
    sum_k[...] = jnp.zeros_like(sum_k)
    sum_v[...] = jnp.zeros_like(sum_v)
    row = lax.broadcasted_iota(jnp.int32, (HD, TILE), 0)

    def scored(i, probs_out, grads_out):
        here = pl.ds(pl.multiple_of(i * TILE, TILE), TILE)
        grad_turned = held_g[here, :].astype(F32).T
        delta = jnp.sum(grad_turned * turned[0, :, here], axis=0, keepdims=True)
        high, middle, least = three_parts(-logs[0, :, here])
        tail = jnp.where(row == 0, 1.0, jnp.where(row == 1, high, jnp.where(row == 2, middle, jnp.where(row == 3, least, 0.0))))
        query = jnp.concatenate([qa[0, :HD, here], tail.astype(BF16)], axis=0)
        probs_out[...] = dot(ka[0], query)
        high, middle, least = three_parts(-delta)
        tail = jnp.where(row == 0, high, jnp.where(row == 1, middle, jnp.where(row == 2, least, 0.0)))
        grad_tail = jnp.concatenate([grad_turned, tail], axis=0).astype(BF16)
        grads_out[...] = dot(va[0], grad_tail)

    def some(i, width, probs_in, grads_in):
        here = pl.ds(pl.multiple_of(i * TILE, TILE), TILE)
        probs = jnp.exp(probs_in[...])
        grad_scores = (probs * grads_in[...]).astype(BF16)
        grad_turned = held_g[here, :].astype(F32).T.astype(BF16)
        sum_v[...] += dot_nt(grad_turned, probs.astype(BF16))
        sum_k[...] += dot_nt(qa[0, :HD, here], grad_scores)
        query_grad = dot(kt[0], grad_scores) * HD ** (-0.5)
        out_q[pl.ds(pl.multiple_of(i * TILE, TILE), width), :] = query_grad.T.astype(BF16)[:width]

    def pair(i, carry):
        scored(2 * i + 1, s1, d1)
        some(2 * i, TILE, s0, d0)
        scored(2 * i + 2, s0, d0)
        some(2 * i + 1, TILE, s1, d1)
        return carry

    least = total - (tiles - 1) * TILE
    scored(0, s0, d0)
    lax.fori_loop(0, (tiles - 1) // 2, pair, 0)
    if tiles % 2 == 0:
        scored(tiles - 1, s1, d1)
        some(tiles - 2, TILE, s0, d0)
        some(tiles - 1, least, s1, d1)
    else:
        some(tiles - 1, least, s0, d0)
    out_k[...] = sum_k[...].T.astype(BF16)
    out_v[...] = sum_v[...].T.astype(BF16)


def attend_back(head, qa, ka, va, kt, turned, logs, grads):
    n, total, _ = ka.shape
    padded = qa.shape[2]
    per_head = lambda *shape: pl.BlockSpec((1,) + shape, lambda i: (head, 0, 0))
    return pl.pallas_call(
        functools.partial(backward_kernel, head),
        grid=(1,),
        out_shape=[jax.ShapeDtypeStruct((total, HD), BF16)] * 3,
        in_specs=[
            per_head(2 * HD, padded),
            per_head(total, 2 * HD),
            per_head(total, 2 * HD),
            per_head(HD, total),
            per_head(HD, padded),
            per_head(1, padded),
        ]
        + [whole(*grads[0].shape)] * MEMBERS,
        out_specs=[whole(total, HD)] * 3,
        scratch_shapes=[
            VMEM((padded, HD), BF16),
            VMEM((HD, total), F32),
            VMEM((HD, total), F32),
        ]
        + [VMEM((total, TILE), F32)] * 4,
        compiler_params=params(),
        cost_estimate=LONG,
        name="attend_back",
    )(qa, ka, va, kt, turned, logs, *grads)


def unproject_kernel(where, *refs):
    columns, normed, w = refs[:9], refs[9], refs[10]
    n0, n1, n23, a_send, a_keep, b_send, b_keep, sums = refs[11:19]
    held, held_normed, held_n, joint, grad, sem_in, sem_out = refs[19:]
    rows = n0.shape[0]
    here = [pl.ds(d * rows, rows) for d in range(MEMBERS)]
    steps = []
    for s in range(3):
        for h in range(LOCAL_HEADS):
            at = s * WIDTH + h * HD
            slot = 3 * h + s

            def put(at=at, slot=slot):
                joint[:, at : at + HD] = held[slot]

            steps.append(([pltpu.make_async_copy(columns[slot], held.at[slot], sem_in.at[slot])], put, []))
    for d in (2, 3, 1, 0):

        def back(d=d):
            held_n[d] = dot_nt(joint[here[d], :], w[...]).astype(BF16)

        place = (n0, n1, n23.at[0], n23.at[1])[d]
        ins = [pltpu.make_async_copy(normed, held_normed, sem_in.at[9])] if d == 0 else []
        steps.append((ins, back, [pltpu.make_async_copy(held_n.at[d], place, sem_out.at[d])]))

    def weights():
        whole_grad = dot_tn(joint[...], held_normed[...])
        count, each, model = grad.shape
        for i in range(count):
            grad[i] = whole_grad[i * each : (i + 1) * each]
        pieces = count // 2
        for r in range(pieces):
            for p in range(2):
                part = grad[(r ^ where[1]) * 2 + (p ^ (where[2] // 2))].astype(BF16)
                out = (a_keep, a_send)[r % 2]
                out[r // 2, p] = part[:, : model // 2]
                out = (b_keep, b_send)[2 * r // pieces]
                out[r % (pieces // 2), p] = part[:, model // 2 :]
        total = jnp.sum(joint[...].astype(F32), axis=0, keepdims=True)
        sums[...] = jnp.zeros_like(sums)
        for m in range(MEMBERS):

            @pl.when(2 * where[0] + where[2] % 2 == m)
            def _(m=m):
                sums[0:1, m * WIDTH : (m + 1) * WIDTH] = total[:, :WIDTH]
                sums[1:2, m * WIDTH : (m + 1) * WIDTH] = total[:, 2 * WIDTH :]

    steps.append(([], weights, []))
    streamed(steps)


def unproject(where, columns, normed, w, pieces):
    total, model = normed.shape
    rows = total // MEMBERS
    width = 3 * WIDTH
    each = width // pieces // 2
    shaped = jax.ShapeDtypeStruct
    outs = [shaped((rows, model), BF16)] * 2 + [shaped((2, rows, model), BF16)]
    outs += [shaped((pieces // 2, 2, each, model // 2), BF16)] * 4 + [shaped((2, model), F32)]
    anywhere, near = pl.BlockSpec(memory_space=pl.ANY), pl.BlockSpec(memory_space=VMEM)
    return pl.pallas_call(
        unproject_kernel,
        out_shape=outs,
        in_specs=[pl.BlockSpec(memory_space=pltpu.SMEM)] + [anywhere] * 10 + [near],
        out_specs=[anywhere] * 3 + [near] * 5,
        scratch_shapes=[
            VMEM((9, total, HD), BF16),
            VMEM((total, model), BF16),
            VMEM((MEMBERS, rows, model), BF16),
            VMEM((total, width), BF16),
            VMEM((2 * pieces, each, model), F32),
            pltpu.SemaphoreType.DMA((10,)),
            pltpu.SemaphoreType.DMA((MEMBERS,)),
        ],
        compiler_params=params(),
        cost_estimate=LONG,
        name="unproject",
    )(where, *columns, normed, w)


def pre_sums_kernel(*refs):
    xs, (n0, n1, n23, out) = refs[:8], refs[8:]
    rows = n0.shape[0]
    out[...] = jnp.zeros_like(out)
    for d, given in enumerate((n0, n1, n23.at[0], n23.at[1])):
        for (at, size, _), x in zip(packing(rows), xs[2 * d : 2 * d + 2]):
            unit, _ = normalized(x[:size, :].astype(F32))
            grad = given[at : at + size, :].astype(F32)
            out[0:1, :] += jnp.sum(grad * unit, axis=0, keepdims=True)
            out[1:2, :] += jnp.sum(grad, axis=0, keepdims=True)


def close_kernel(first, last, p0, p1, gain, hidden, grad, low):
    rows = hidden.shape[0]
    unit, inverse = normalized(rows_of(first, last, rows))
    given = p0[...].astype(F32) + p1[...].astype(F32)
    scaled = given * gain[...][None]
    inner = scaled - jnp.mean(scaled, axis=-1, keepdims=True)
    inner = inner - unit * jnp.mean(scaled * unit, axis=-1, keepdims=True)
    total = hidden[...] + inverse * inner
    grad[...] = total
    low[...] = total.astype(BF16)


def close(x, parts, gain, hidden):
    rows, model = hidden.shape
    shaped = jax.ShapeDtypeStruct
    return pl.pallas_call(
        close_kernel,
        out_shape=[shaped((rows, model), F32), shaped((rows, model), BF16)],
        in_specs=[pl.BlockSpec(memory_space=VMEM)] * 6,
        out_specs=[pl.BlockSpec(memory_space=VMEM)] * 2,
        compiler_params=params(),
        cost_estimate=LONG,
        name="close",
    )(*x, *parts, gain, hidden)


def middle_kernel(
    side, first, final, a0, a1, a2, a3, wo, out_bias, gain, shift, cot, down_bias, up, up_bias, down,
    layer, down_send, down_keep, rest_send, rest_keep, grad_up_bias, grad_hidden, g0, g1, g2, g3, vectors,
    hidden, normed, grad_down, total_out, total_grad, valid,
):
    step = pl.program_id(0)
    last = pl.num_programs(0) - 1
    half = pl.num_programs(0) // 2
    rows, model = cot.shape
    pieces = down_keep.shape[0]
    each = half * model // pieces
    share = model // each

    @pl.when(step == 0)
    def _():
        valid[...] = mask_column(final, rows)
        value = rows_of(first, final, rows) + out_bias[...][None]
        cuts = packing(rows)
        value += jnp.concatenate(
            [
                sum(dot(part[:size, lane : lane + WIDTH], wo[e]) for e, part in enumerate((a0, a1, a2, a3)))
                for _, size, lane in cuts
            ]
        )
        hidden[...] = value
        unit, _ = normalized(value)
        normed[...] = (unit * gain[...][None] + shift[...][None]).astype(BF16)
        low = (valid[...] * cot[...].astype(F32)).astype(BF16)
        grad_down[...] = low
        vectors[3:4, :] = jnp.sum(low.astype(F32), axis=0, keepdims=True)
        total_out[...] = value + down_bias[...][None]
        total_grad[...] = jnp.zeros_like(total_grad)

    gate = dot(normed[...], up[...]) + up_bias[0]
    below = 0.5 * (1.0 + lax.erf(gate * (0.5**0.5)))
    active = (gate * below).astype(BF16)
    slope = below + gate * (jnp.exp(-0.5 * gate * gate) * (0.5 / jnp.pi) ** 0.5)
    low = grad_down[...]
    grad_gate = (dot_nt(low, down[...]) * slope).astype(BF16)
    total_out[...] += dot(active, down[...])
    total_grad[...] += dot_nt(grad_gate, up[...])
    grad_up_bias[0] = jnp.sum(grad_gate.astype(F32), axis=0, keepdims=True)
    of_down = dot_tn(active, low).astype(BF16)
    of_up = dot_tn(normed[...], grad_gate).astype(BF16)
    few = each // MEMBERS
    for i in range(2 * half):

        @pl.when(step == i)
        def _(i=i):
            down_held, rest_held = (down_send, rest_send) if i < half else (down_keep, rest_keep)
            for j in range(share):
                piece = ((i % half) * share + j) ^ side[1]
                for z in range(MEMBERS):
                    at = j * each + z * few
                    down_held[piece, z ^ side[2]] = of_down[at : at + few]
                    rest_held[piece, z ^ side[2], :few, :] = of_up[at : at + few]

    @pl.when(step == last)
    def _():
        unit, inverse = normalized(hidden[...])
        layer[...] = (valid[...] * total_out[...]).astype(BF16)
        grad = total_grad[...]
        vectors[0:1, :] = jnp.sum(grad * unit, axis=0, keepdims=True)
        vectors[1:2, :] = jnp.sum(grad, axis=0, keepdims=True)
        scaled = grad * gain[...][None]
        inner = scaled - jnp.mean(scaled, axis=-1, keepdims=True)
        inner = inner - unit * jnp.mean(scaled * unit, axis=-1, keepdims=True)
        grad = grad_down[...].astype(F32) + inverse * inner
        grad_hidden[...] = grad
        branch = grad.astype(BF16)
        vectors[2:3, :] = jnp.sum(branch.astype(F32), axis=0, keepdims=True)
        parts = (a0, a1, a2, a3)
        count = pieces // 2
        some = WIDTH // count // MEMBERS
        for e, given in enumerate((g0, g1, g2, g3)):
            back = dot_nt(branch, wo[e]).astype(BF16)
            given[...] = jnp.zeros_like(given)
            for at, size, lane in packing(rows):
                given[:size, lane : lane + WIDTH] = back[at : at + size]
            held = rest_keep if e < 2 else rest_send
            place = ((side[2] % 2) ^ (e & 1)) * count
            of_out = sum(
                dot_tn(parts[e][:size, lane : lane + WIDTH], branch[at : at + size])
                for at, size, lane in packing(rows)
            ).astype(BF16)
            for j in range(count):
                for z in range(MEMBERS):
                    at = (j * MEMBERS + z) * some
                    held[(place + j) ^ side[1], z ^ side[2], few:, :] = of_out[at : at + some]


def middle(where, pieces, x, attended, wo, out_bias, gain, shift, cot, down_bias, up, up_bias, down):
    rows, model = cot.shape
    blocks = up.shape[1] // model
    half = blocks // 2

    def block_of(i, side):
        return lax.rem(i, half) + half * jnp.where(i < half, 1 - side[0], side[0])

    whole_s = lambda *shape: pl.BlockSpec(shape, lambda i, side: (0,) * len(shape))
    each = half * model // pieces // MEMBERS
    held = (pieces, MEMBERS, each, model)
    rest = (pieces, MEMBERS, each + 2 * WIDTH // pieces // MEMBERS, model)
    shaped = jax.ShapeDtypeStruct
    outs = [
        (shaped((rows, model), BF16), whole_s(rows, model)),
        (shaped(held, BF16), whole_s(*held)),
        (shaped(held, BF16), whole_s(*held)),
        (shaped(rest, BF16), whole_s(*rest)),
        (shaped(rest, BF16), whole_s(*rest)),
        (shaped((blocks, 1, model), F32), pl.BlockSpec((1, 1, model), lambda i, side: (block_of(i, side), 0, 0))),
        (shaped((rows, model), F32), whole_s(rows, model)),
    ]
    outs += [(shaped(attended[0].shape, BF16), whole_s(*attended[0].shape))] * MEMBERS
    outs += [(shaped((4, model), F32), whole_s(4, model))]
    return pl.pallas_call(
        middle_kernel,
        out_shape=[o[0] for o in outs],
        grid_spec=pltpu.PrefetchScalarGridSpec(
            num_scalar_prefetch=1,
            grid=(blocks,),
            in_specs=[whole_s(*x[0].shape)] * 2
            + [whole_s(*attended[0].shape)] * MEMBERS
            + [whole_s(MEMBERS, WIDTH, model)]
            + [whole_s(model)] * 3
            + [whole_s(rows, model), whole_s(model)]
            + [
                pl.BlockSpec((model, model), lambda i, side: (0, block_of(i, side))),
                pl.BlockSpec((1, 1, model), lambda i, side: (block_of(i, side), 0, 0)),
                pl.BlockSpec((model, model), lambda i, side: (block_of(i, side), 0)),
            ],
            out_specs=[o[1] for o in outs],
            scratch_shapes=[
                VMEM((rows, model), F32),
                VMEM((rows, model), BF16),
                VMEM((rows, model), BF16),
                VMEM((rows, model), F32),
                VMEM((rows, model), F32),
                VMEM((rows, 1), F32),
            ],
        ),
        compiler_params=params(),
        cost_estimate=LONG,
        name="middle",
    )(
        where,
        *x, *attended, wo, out_bias, gain, shift, cot, down_bias,
        up, up_bias.reshape(blocks, 1, model), down,
    )


def reversed_bits(index, count):
    bits = count.bit_length() - 1
    total = 0
    for bit in range(bits):
        total = total | (((index >> bit) & 1) << (bits - 1 - bit))
    return total


def place_steps(where, other, parts, cuts, outs, held_in, held, sem_in, sem_out):
    _, pieces, _, _, lanes = parts.shape
    model = 2 * lanes
    half = where[0] ^ other
    steps = []
    for r in range(pieces):
        piece = r ^ where[1]
        ins = [
            pltpu.make_async_copy(parts.at[i, at], held_in.at[other, r, i], sem_in.at[other, r, i])
            for i, at in enumerate((reversed_bits(r, pieces), r))
        ]

        def compute(r=r):
            for z in range(MEMBERS):
                given = reversed_bits(z ^ where[2], MEMBERS)
                for i in range(2):
                    for out, (start, size) in zip(held, cuts):
                        value = held_in[other, r, i, given, start : start + size, :]
                        out[other, r, z * size : (z + 1) * size, i * lanes : (i + 1) * lanes] = value.astype(F32)

        places = []
        for out, (_, size) in zip(outs, cuts):
            rows = size * MEMBERS
            if out.shape[1] == model:
                places.append(out.at[pl.ds((half * pieces + piece) * rows, rows)])
            else:
                share = model // rows
                column = half * (out.shape[1] // model // 2) + piece // share
                places.append(
                    out.at[
                        pl.ds(lax.rem(piece, share) * rows, rows),
                        pl.ds(pl.multiple_of(column * model, model), model),
                    ]
                )
        sends = [
            pltpu.make_async_copy(given.at[other, r], place, sem_out.at[other, r, i])
            for i, (given, place) in enumerate(zip(held, places))
        ]
        steps.append((ins, compute, sends))
    return steps


def cuts_of(parts, shapes):
    _, pieces, _, rows, lanes = parts.shape
    sizes = [shape[0] * shape[1] // (2 * lanes) // 2 // pieces // MEMBERS for shape in shapes]
    return [(sum(sizes[:i]), size) for i, size in enumerate(sizes)]


def place_scratch(parts, cuts):
    _, pieces, _, rows, lanes = parts.shape
    scratch = [VMEM((2, pieces, 2, MEMBERS, rows, lanes), BF16)]
    scratch += [VMEM((2, pieces, MEMBERS * size, 2 * lanes), F32) for _, size in cuts]
    return scratch + [
        pltpu.SemaphoreType.DMA((2, pieces, 2)),
        pltpu.SemaphoreType.DMA((2, pieces, len(cuts))),
    ]


def place_kernel(cuts, where, own, got, *refs):
    count = len(cuts)
    outs, held_in, held, sems = refs[:count], refs[count], refs[count + 1 : -2], refs[-2:]
    streamed(
        place_steps(where, 0, own, cuts, outs, held_in, held, *sems)
        + place_steps(where, 1, got, cuts, outs, held_in, held, *sems)
    )


def placed(where, own, got, shapes):
    cuts = cuts_of(own, shapes)
    anywhere = pl.BlockSpec(memory_space=pl.ANY)
    return pl.pallas_call(
        functools.partial(place_kernel, cuts),
        out_shape=[jax.ShapeDtypeStruct(shape, F32) for shape in shapes],
        in_specs=[pl.BlockSpec(memory_space=pltpu.SMEM)] + [anywhere] * 2,
        out_specs=[anywhere] * len(cuts),
        scratch_shapes=place_scratch(own, cuts),
        compiler_params=params(),
        cost_estimate=LONG,
        name="placed",
    )(where, own, got)


def place_in_kernel(where, own, got, out, *refs):
    vectors, (columns, out_held, sem_out) = refs[:8], refs[8:]
    _, pieces, _, _, lanes = own.shape
    model = 2 * lanes
    each = columns.shape[2]
    totals = []

    def gather(other, parts):
        total = 0.0
        for piece in range(pieces):
            for side in range(MEMBERS):
                r, z = piece ^ where[1], side ^ where[2]
                at = reversed_bits(z, MEMBERS)
                both = (parts[0, reversed_bits(r, pieces), at], parts[1, r, at])
                both = jnp.concatenate([v.astype(F32) for v in both], axis=1)
                columns[2 * other + side % 2, piece * 2 + side // 2] = both[:each]
                total = total + both[each:]
        totals.append(total)

    def turn(other, s):
        for m in range(2):
            given = columns[2 * other + m].reshape(3 * WIDTH, model)[s * WIDTH : (s + 1) * WIDTH]
            out_held[other, s, :, m * WIDTH : (m + 1) * WIDTH] = given.T

    steps = []
    for other, parts in enumerate((own, got)):
        steps.append(([], functools.partial(gather, other, parts), []))
        for s in range(3):
            at = s * model + (where[0] ^ other) * lanes
            place = out.at[:, pl.ds(pl.multiple_of(at, lanes), lanes)]
            copy = pltpu.make_async_copy(out_held.at[other, s], place, sem_out.at[other, s])
            steps.append(([], functools.partial(turn, other, s), [copy]))
    streamed(steps)
    total = totals[0] + totals[1]
    for i in range(6):
        vectors[i][...] = total[i]
    vectors[6][...] = total[6:8]
    for i in range(vectors[7].shape[0] // model):
        vectors[7][i * model : (i + 1) * model] = total[8 + i]


def placed_in(where, own, got, extra, hidden_units):
    _, pieces, _, rows, lanes = own.shape
    model = 2 * lanes
    vectors = [(model,)] * 6 + [(2, model), (hidden_units,)]
    anywhere, near = pl.BlockSpec(memory_space=pl.ANY), pl.BlockSpec(memory_space=VMEM)
    return pl.pallas_call(
        place_in_kernel,
        out_shape=[jax.ShapeDtypeStruct(shape, F32) for shape in [(model, 3 * model)] + vectors],
        in_specs=[pl.BlockSpec(memory_space=pltpu.SMEM)] + [near] * 2,
        out_specs=[anywhere] + [near] * 8,
        scratch_shapes=[
            VMEM((MEMBERS, 2 * pieces, rows - extra, model), F32),
            VMEM((2, 3, model, lanes), F32),
            pltpu.SemaphoreType.DMA((2, 3)),
        ],
        compiler_params=params(),
        cost_estimate=LONG,
        name="placed_in",
    )(where, own, got)


def plus(first, second):
    return (first.astype(F32) + second.astype(F32)).astype(BF16)


def fold_core_kernel(keep, got, a_send, a_keep, b_send, b_keep, held, held_out, sem_in, sem_out):
    pieces, _, _, lanes = keep.shape
    steps = []
    for p in range(pieces):
        ins = [
            pltpu.make_async_copy(keep.at[p], held.at[p], sem_in.at[p, 0]),
        ]

        def compute(p=p):
            total = plus(held[p], got[p])
            held_out[p, 0] = total[:, :, : lanes // 2]
            held_out[p, 1] = total[:, :, lanes // 2 :]

        first = (a_keep, a_send)[p % 2].at[p // 2]
        second = (b_keep, b_send)[2 * p // pieces].at[p % (pieces // 2)]
        outs = [
            pltpu.make_async_copy(held_out.at[p, i], place, sem_out.at[p, i])
            for i, place in enumerate((first, second))
        ]
        steps.append((ins, compute, outs))
    streamed(steps)


def fold_core(keep, got):
    pieces, quarters, rows, lanes = keep.shape
    half = (quarters, rows, lanes // 2)
    return pl.pallas_call(
        fold_core_kernel,
        out_shape=[jax.ShapeDtypeStruct((pieces // 2, *half), BF16)] * 4,
        in_specs=[pl.BlockSpec(memory_space=HBM), pl.BlockSpec(memory_space=VMEM)],
        out_specs=[pl.BlockSpec(memory_space=HBM)] * 4,
        scratch_shapes=[
            VMEM(keep.shape, BF16),
            VMEM((pieces, 2, *half), BF16),
            pltpu.SemaphoreType.DMA((pieces, 2)),
            pltpu.SemaphoreType.DMA((pieces, 2)),
        ],
        compiler_params=params(),
        cost_estimate=QUICK,
        name="fold_core",
    )(keep, got)


def fold_core_quarters_kernel(keep, got, send, kept, held, held_got, held_out, sem_in, sem_out):
    pieces, quarters = keep.shape[:2]
    steps = []
    for p in range(pieces):
        ins = [
            pltpu.make_async_copy(keep.at[p], held.at[p], sem_in.at[p, 0]),
            pltpu.make_async_copy(got.at[p], held_got.at[p], sem_in.at[p, 1]),
        ]

        def compute(p=p):
            for z in range(quarters):
                held_out[p, z % 2, z // 2] = plus(held[p, z], held_got[p, z])

        outs = [
            pltpu.make_async_copy(held_out.at[p, i], place.at[p], sem_out.at[p, i])
            for i, place in enumerate((kept, send))
        ]
        steps.append((ins, compute, outs))
    streamed(steps)


def fold_core_quarters(keep, got):
    pieces, quarters, rows, lanes = keep.shape
    half = (quarters // 2, rows, lanes)
    return pl.pallas_call(
        fold_core_quarters_kernel,
        out_shape=[jax.ShapeDtypeStruct((pieces, *half), BF16)] * 2,
        in_specs=[pl.BlockSpec(memory_space=pl.ANY)] * 2,
        out_specs=[pl.BlockSpec(memory_space=pl.ANY)] * 2,
        scratch_shapes=[
            VMEM(keep.shape, BF16),
            VMEM(keep.shape, BF16),
            VMEM((pieces, 2, *half), BF16),
            pltpu.SemaphoreType.DMA((pieces, 2)),
            pltpu.SemaphoreType.DMA((pieces, 2)),
        ],
        compiler_params=params(),
        cost_estimate=QUICK,
        name="fold_core_quarters",
    )(keep, got)


def fold_halves_kernel(keep, got, send, kept):
    for p in range(keep.shape[0]):
        kept[p] = plus(keep[p, 0], got[p, 0])
        send[p] = plus(keep[p, 1], got[p, 1])


def fold_halves(keep, got):
    pieces, _, rows, lanes = keep.shape
    outs = [jax.ShapeDtypeStruct((pieces, rows, lanes), BF16)] * 2
    return in_vmem(fold_halves_kernel, outs, keep, got, name="fold_halves")


def fold_pieces_kernel(keep, got, a_send, a_keep, b_send, b_keep):
    pieces, _, model = keep.shape
    for r in range(pieces):
        total = plus(keep[r], got[r])
        out = (a_keep, a_send)[r % 2]
        out[r // 2, 0] = total[:, : model // 2]
        out = (b_keep, b_send)[2 * r // pieces]
        out[r % (pieces // 2), 0] = total[:, model // 2 :]


def fold_pieces(keep, got):
    pieces, rows, model = keep.shape
    outs = [jax.ShapeDtypeStruct((pieces // 2, 1, rows, model // 2), BF16)] * 4
    return in_vmem(fold_pieces_kernel, outs, keep, got, name="fold_pieces")


def join_planes_kernel(ak, ag, bk, bg, out):
    count = ak.shape[0]
    for r in range(count):
        out[0, r], out[0, count + r] = ak[r], ag[r]
        out[1, r], out[1, count + r] = bk[r], bg[r]


def join_planes(ak, ag, bk, bg):
    count, *rest = ak.shape
    outs = [jax.ShapeDtypeStruct((2, 2 * count, *rest), BF16)]
    return in_vmem(join_planes_kernel, outs, ak, ag, bk, bg, name="join_planes")[0]


def fold_in_kernel(keep, got, pre, mid, biases, up_bias, out):
    rows = keep.shape[1]
    out[:rows, :] = plus(keep[0], got[0])
    vectors = [pre[...], mid[...], biases[...]] + [up_bias[i] for i in range(up_bias.shape[0])]
    count = sum(v.shape[0] for v in vectors)
    filled = vectors + [jnp.zeros((out.shape[0] - rows - count, out.shape[1]), F32)]
    out[rows:, :] = jnp.concatenate(filled).astype(BF16)


def fold_in(keep, got, vectors, extra):
    _, rows, lanes = keep.shape
    outs = [jax.ShapeDtypeStruct((rows + extra, lanes), BF16)]
    return in_vmem(fold_in_kernel, outs, keep, got, *vectors, name="fold_in")[0]


def in_vmem(kernel, outs, *values, name):
    return pl.pallas_call(
        kernel,
        out_shape=outs,
        in_specs=[pl.BlockSpec(memory_space=VMEM)] * len(values),
        out_specs=[pl.BlockSpec(memory_space=VMEM)] * len(outs),
        compiler_params=params(),
        cost_estimate=QUICK,
        name=name,
    )(*values)


def fold_planes_kernel(ak, ag, bk, bg, a_send, a_keep, b_send, b_keep):
    count = ak.shape[0]
    for r in range(count):
        out = (a_keep, a_send)[r % 2]
        out[r // 2] = plus(ak[r], ag[r])
        out = (b_keep, b_send)[2 * r // count]
        out[r % (count // 2)] = plus(bk[r], bg[r])


def fold_last_kernel(ak, ag, bk, bg, send, keep=None):
    quarters = ak.shape[1]
    lanes = ak.shape[3]
    keep = send if keep is None else keep
    for z in range(quarters):
        out = (keep, send)[z % 2]
        out[z // 2, :, :lanes] = plus(ak[0, z], ag[0, z])
        out[z // 2, :, lanes:] = plus(bk[0, z], bg[0, z])


def fold_planes(ak, ag, bk, bg):
    count, quarters, rows, lanes = ak.shape
    if count > 1:
        outs = [jax.ShapeDtypeStruct((count // 2, quarters, rows, lanes), BF16)] * 4
        return in_vmem(fold_planes_kernel, outs, ak, ag, bk, bg, name="fold_planes")
    outs = [jax.ShapeDtypeStruct((-(-quarters // 2), rows, 2 * lanes), BF16)] * min(quarters, 2)
    return in_vmem(fold_last_kernel, outs, ak, ag, bk, bg, name="fold_last")


def fold_quarters_kernel(keep, got, *outs):
    for z in range(keep.shape[0]):
        out = outs[len(outs) - 1 - z]
        out[...] = plus(keep[z], got[z])


def fold_quarters(keep, got):
    count, rows, lanes = keep.shape
    outs = [jax.ShapeDtypeStruct((rows, lanes), BF16)] * count
    return in_vmem(fold_quarters_kernel, outs, keep, got, name="fold_quarters")


def over_cube(value, bit):
    count = lax.axis_size("cube")
    return lax.ppermute(value, "cube", [(i, i ^ (1 << bit)) for i in range(count)])


def over_blk(value, bit):
    return lax.ppermute(value, "blk", [(i, i ^ (1 << bit)) for i in range(MEMBERS)])


def chosen_pairs(is_home, cube_flip, blk_flip):
    pairs = []
    for c in range(lax.axis_size("cube")):
        for b in range(MEMBERS):
            if ((c & 1) == (b >> 1)) == is_home:
                pairs.append((c * MEMBERS + b, (c ^ cube_flip) * MEMBERS + (b ^ blk_flip)))
    return pairs


def sent_between(value, is_home, cube_flip, blk_flip):
    return lax.ppermute(value, ("cube", "blk"), chosen_pairs(is_home, cube_flip, blk_flip))


def exchanged(parts):
    far = over_blk(parts[3], 0)
    near = over_blk(parts[1], 0)
    core = over_cube(parts[2], 0)
    return [parts[0], near, core, over_cube(far, 0)]


def cube_bits():
    return list(range(1, lax.axis_size("cube").bit_length() - 1))


def by_cube(bit):
    return functools.partial(over_cube, bit=bit)


def by_blk(bit):
    return functools.partial(over_blk, bit=bit)


def scattering(a_send, a_keep, b_send, b_keep):
    for low, high in zip(cube_bits(), cube_bits()[::-1]):
        a_got, b_got = yield [(a_send, by_cube(low)), (b_send, by_cube(high))]
        *folded, = fold_planes(a_keep, a_got, b_keep, b_got)
        if len(folded) <= 2:
            return folded
        a_send, a_keep, b_send, b_keep = folded


def spreading(shard):
    (got,) = yield [(shard, by_blk(1))]
    both = jnp.stack([shard, got])
    (got,) = yield [(both, by_blk(0))]
    both = jnp.concatenate([both, got])[None]
    lanes = both.shape[3] // 2
    a_part, b_part = both[..., :lanes], both[..., lanes:]
    for low, high in zip(cube_bits(), cube_bits()[::-1]):
        a_got, b_got = yield [(a_part, by_cube(high)), (b_part, by_cube(low))]
        if low == cube_bits()[-1]:
            break
        a_part, b_part = jnp.concatenate([a_part, a_got]), jnp.concatenate([b_part, b_got])
    (got,) = yield [(join_planes(a_part, a_got, b_part, b_got), by_cube(0))]
    return got


def summing(keep, send):
    (got,) = yield [(send, by_cube(0))]
    send, keep = yield from scattering(*fold_core(keep, got))
    (got,) = yield [(send, by_blk(0))]
    send, keep = fold_quarters(keep, got)
    (got,) = yield [(send, by_blk(1))]
    return (yield from spreading(plus(keep, got)))


def summing_columns(parts, vectors, extra):
    send, keep = yield from scattering(*parts)
    (got,) = yield [(send, by_blk(1))]
    return (yield from spreading(fold_in(keep, got, vectors, extra)))


def closing(own, parts, gain, grad_hidden):
    p0, p1, p23 = parts
    (got,) = yield [(p23, by_cube(0))]
    near_sum, own_sum = plus(p1, got[1]), plus(p0, got[0])
    (got,) = yield [(near_sum, by_blk(0))]
    grad_here, grad_low = close(own, [own_sum, got], gain, grad_hidden)
    (moved,) = yield [(grad_low, lambda v: sent_between(v, False, 1, 2))]
    return grad_here, moved


class Order:
    def __init__(self, token):
        self.token = token

    def __call__(self, values):
        values, self.token = lax.optimization_barrier((values, self.token))
        return values


class Running:
    def __init__(self, steps):
        self.steps = steps
        self.result = None
        self.ready = next(steps)

    def take(self, arrived):
        try:
            self.ready = self.steps.send(arrived)
        except StopIteration as stop:
            self.ready, self.result = [], stop.value

    def spread(self):
        return self.ready[0][0].ndim == 5


def send(order, *runs):
    values = order([[v for v, _ in run.ready] for run in runs])
    for run, given in zip(runs, values):
        run.values = given
        run.arrived = [move(v) for v, (_, move) in zip(given, run.ready)]


def take(order, *runs):
    arrived = order([run.arrived for run in runs])
    for run, got in zip(runs, arrived):
        run.take(got)


def take_all(order, run):
    take(order, run)
    while not run.spread():
        send(order, run)
        take(order, run)


def advance(order, *runs):
    take(order, *runs)
    ready = [run for run in runs if run.ready]
    if ready:
        send(order, *ready)


def member_columns(matrix, member, axis):
    return lax.dynamic_slice_in_dim(matrix, member * WIDTH, WIDTH, axis)


def body(
    inputs,
    cotangent,
    absent_groups,
    token_group,
    pre_gain,
    pre_shift,
    input_weight,
    input_bias,
    output_weight,
    output_bias,
    mid_gain,
    mid_shift,
    up_weight,
    up_bias,
    down_weight,
    down_bias,
):
    _, rows, model = inputs.shape
    hidden_units = up_weight.shape[1]
    cube, blk = lax.axis_index("cube"), lax.axis_index("blk")
    core = cube & 1
    pieces = lax.axis_size("cube") // 2
    where = jnp.stack([core, cube >> 1, blk]).astype(jnp.int32)
    at_home = core == (blk >> 1)
    member = 2 * core + (blk & 1)

    def moved(value):
        return jnp.where(at_home, value, sent_between(value, False, 1, 2))

    group_match = token_group[0][None, :] == jnp.arange(GROUPS, dtype=jnp.int32)[:, None]
    lacking = jnp.sum(jnp.where(group_match, absent_groups.reshape(GROUPS, 1), 0), axis=0)
    valid_here = (1 - lacking).astype(BF16)
    top = packed_rows(rows)
    mask_rows = jnp.broadcast_to(jnp.pad(valid_here, (0, model - rows)), (2 * top - rows, model))
    carried = [inputs[0, :top], jnp.concatenate([inputs[0, top:], mask_rows])]
    arriving = [sent_between(part, False, 1, 2) for part in carried]
    near_home = [sent_between(part, True, 0, 1) for part in carried]

    in_columns = jnp.concatenate(
        [member_columns(input_weight[:, s * model : (s + 1) * model], member, 1) for s in range(3)],
        axis=1,
    )
    bias_columns = member_columns(input_bias, member, 1)
    bias_columns = jnp.concatenate([bias_columns[0], jnp.zeros((WIDTH,), F32), bias_columns[1]])
    out_rows = jnp.stack([member_columns(output_weight, member ^ e, 0) for e in range(MEMBERS)])
    prepared = (in_columns, *prepare(in_columns, bias_columns), bias_columns, out_rows)
    prepared, arriving[1] = lax.optimization_barrier((prepared, arriving[1]))
    in_columns, in_columns_turned, bias_turned, bias_columns, out_rows = prepared

    own, near = [], []
    for given, moved_in, from_home in zip(carried, arriving, near_home):
        own.append(jnp.where(at_home, given, moved_in))
        near.append(jnp.where(at_home, from_home, sent_between(moved_in, False, 0, 1)))
    x_blocks = [*own, *near]
    x_blocks += [over_cube(part, 0) for part in own] + [over_cube(part, 0) for part in near]

    normed_low, qa, ka, va, kt, vt = project(
        x_blocks, rows, pre_gain, pre_shift, in_columns, in_columns_turned, bias_columns, bias_turned
    )
    qa, cot_here = lax.optimization_barrier((qa, cotangent[0]))
    cot_own = moved(cot_here)
    attended_own, turned, logs = attend(qa, ka, vt)
    attended = exchanged(attended_own)
    (
        layer_here,
        down_send,
        down_keep,
        rest_send,
        rest_keep,
        grad_up_bias,
        grad_hidden,
        *grad_attended,
        middle_vectors,
    ) = middle(
        where,
        pieces,
        own,
        attended,
        out_rows,
        output_bias,
        mid_gain,
        mid_shift,
        cot_own,
        down_bias,
        up_weight,
        up_bias,
        down_weight,
    )
    blocks = hidden_units // model
    order = Order(where)
    down, rest = Running(summing(down_keep, down_send)), Running(summing(rest_keep, rest_send))
    send(order, down)
    far, near_part = over_blk(grad_attended[3], 0), over_blk(grad_attended[1], 0)
    send(order, rest)
    advance(order, down)
    far, near_part = order((far, near_part))
    core_parts = (over_cube(grad_attended[2], 0), over_cube(far, 0))
    advance(order, rest)
    grads_here = [grad_attended[0], near_part, *order(core_parts)]
    layer_moved = sent_between(order(layer_here), False, 1, 2)
    columns = []

    def back(head):
        grads = order(grads_here)
        columns.extend(order(attend_back(head, qa, ka, va, kt, turned, logs, grads)))

    back(0)
    advance(order, down)
    back(1)
    advance(order, down)
    advance(order, rest)
    layer_out = jnp.where(at_home, layer_here, order(layer_moved))
    back(2)
    advance(order, down)
    advance(order, rest)
    p0, p1, p23, *in_parts, biases = order(
        unproject(where, order(columns), normed_low, in_columns, pieces)
    )
    vectors, extra = [], 16
    in_run = Running(summing_columns(in_parts, vectors, extra))
    closing_run = Running(closing(own, (p0, p1, p23), pre_gain, grad_hidden))
    send(order, in_run)
    send(order, closing_run)
    advance(order, down)
    advance(order, rest)
    advance(order, down)
    advance(order, in_run)
    pre_sums = in_vmem(
        pre_sums_kernel, [jax.ShapeDtypeStruct((2, model), F32)], *x_blocks, p0, p1, p23, name="pre_sums"
    )
    vectors += [*order(pre_sums), middle_vectors, biases, grad_up_bias]
    advance(order, in_run)
    advance(order, rest)
    advance(order, down)
    advance(order, in_run)
    advance(order, rest)
    advance(order, down)
    advance(order, in_run)
    advance(order, rest)
    take_all(order, down)
    advance(order, in_run)
    advance(order, closing_run)
    advance(order, rest)
    send(order, down)
    advance(order, in_run)
    advance(order, closing_run)
    take(order, down)
    take_all(order, rest)
    send(order, rest)
    (grad_down_weight,) = order(placed(order.token, down.values[0], down.result, [(hidden_units, model)]))
    take_all(order, in_run)
    send(order, in_run)
    take(order, closing_run)
    grad_here, grad_moved = closing_run.result
    input_grad = order(jnp.where(at_home, grad_here, grad_moved.astype(F32)))
    take(order, rest)
    shapes = [(model, hidden_units), (model, model)]
    grad_up_weight, grad_output_weight = order(placed(order.token, rest.values[0], rest.result, shapes))
    take(order, in_run)
    (
        grad_input_weight,
        grad_pre_gain,
        grad_pre_shift,
        grad_mid_gain,
        grad_mid_shift,
        grad_output_bias,
        grad_down_bias,
        grad_input_bias,
        grad_up_bias,
    ) = placed_in(order.token, in_run.values[0], in_run.result, extra, hidden_units)
    return (
        layer_out[None],
        input_grad[None],
        grad_pre_gain,
        grad_pre_shift,
        grad_input_weight,
        grad_input_bias,
        grad_output_weight,
        grad_output_bias,
        grad_mid_gain,
        grad_mid_shift,
        grad_up_weight,
        grad_up_bias,
        grad_down_weight,
        grad_down_bias,
    )


def solution(mesh):
    rows_spec = P("cube", "blk", None)
    return jax.shard_map(
        body,
        mesh=mesh,
        in_specs=(rows_spec, rows_spec, P("cube", None), P("cube", "blk")) + (P(),) * 12,
        out_specs=(rows_spec, rows_spec) + (P(),) * 12,
        check_vma=False,
    )
```

```python
import functools
import jax
import jax.numpy as jnp
from jax import lax
from jax.experimental import pallas as pl
from jax.experimental.pallas import tpu as pltpu
from jax.sharding import PartitionSpec as P

HEADS = 12
HD = 64
GROUPS = 12
MEMBERS = 4
LOCAL_HEADS = HEADS // MEMBERS
WIDTH = LOCAL_HEADS * HD
NEG_FILL = -32768.0
EPSILON = 1e-06
BF16 = jnp.bfloat16
F32 = jnp.float32
TILE = 256
LANES = 128
VMEM = pltpu.VMEM
HBM = pltpu.MemorySpace.HBM
QUICK = pl.CostEstimate(flops=1_000_000_000, bytes_accessed=3_000_000, transcendentals=0)
LONG = pl.CostEstimate(flops=60_000_000_000, bytes_accessed=180_000_000, transcendentals=0)


def dot(left, right):
    return jnp.dot(left, right, preferred_element_type=F32)


def dot_nt(left, right):
    return lax.dot_general(left, right, (((1,), (1,)), ((), ())), preferred_element_type=F32)


def dot_tn(left, right):
    return lax.dot_general(left, right, (((0,), (0,)), ((), ())), preferred_element_type=F32)


def params(limit=60 << 20, **more):
    return pltpu.CompilerParams(vmem_limit_bytes=limit, **more)


def whole(*shape):
    return pl.BlockSpec(shape, lambda *_: (0,) * len(shape))


def normalized(values):
    centered = values - jnp.mean(values, axis=-1, keepdims=True)
    inverse = lax.rsqrt(jnp.mean(centered * centered, axis=-1, keepdims=True) + EPSILON)
    return centered * inverse, inverse


def streamed(steps):
    for ins, _, _ in steps:
        for copy in ins:
            copy.start()
    for ins, compute, outs in steps:
        for copy in ins:
            copy.wait()
        compute()
        for copy in outs:
            copy.start()
    for _, _, outs in steps:
        for copy in outs:
            copy.wait()


def mask_column(last, rows):
    return last[rows - packed_rows(rows) :, :rows].astype(F32).T[:, :1]


def rows_of(first, last, rows):
    top = first.shape[0]
    return jnp.concatenate([first[...], last[: rows - top, :]]).astype(F32)


def packing(rows):
    top = packed_rows(rows)
    return [(0, top, 0), (top, rows - top, WIDTH)]


def packed_rows(rows):
    return -(-rows // 32) * 16


def project_kernel(*refs):
    xs, (gain, shift, w, wt, bias, bias_col), refs = refs[:8], refs[8:14], refs[14:]
    results, held, (x_held, w_held, sem_in, sem_out) = refs[:6], refs[6:12], refs[12:]
    normed, qa, ka, va, kt, vt = held
    rows = normed.shape[0] // MEMBERS
    total = MEMBERS * rows
    padded = qa.shape[2]
    low_w = pltpu.make_async_copy(w, w_held.at[0], sem_in.at[MEMBERS, 0])
    steps = []
    for d in range(MEMBERS):
        here = pl.ds(d * rows, rows)

        def compute(d=d, here=here):
            part = x_held.at[d]

            for half, (at, size, _) in enumerate(packing(rows)):
                unit, _ = normalized(part[half, :size, :].astype(F32))
                normed[pl.ds(d * rows + at, size), :] = (unit * gain[...][None] + shift[...][None]).astype(BF16)
            natural = dot(normed[here, :], w_held[0, :, WIDTH:]) + bias[...][None, WIDTH:]
            lane = lax.broadcasted_iota(jnp.int32, (rows, HD), 1)
            low_mask = NEG_FILL * (1.0 - mask_column(part.at[1], rows))
            key_tail = jnp.where(lane == 0, low_mask, jnp.where(lane < 4, 1.0, 0.0)).astype(BF16)
            value_tail = jnp.where(lane < 3, 1.0, 0.0).astype(BF16)
            for h in range(LOCAL_HEADS):
                at = h * HD
                ka[h, here, :HD] = natural[:, at : at + HD].astype(BF16)
                ka[h, here, HD:] = key_tail
                va[h, here, :HD] = natural[:, WIDTH + at : WIDTH + at + HD].astype(BF16)
                va[h, here, HD:] = value_tail

        ins = [pltpu.make_async_copy(xs[2 * d + i], x_held.at[d, i], sem_in.at[d, i]) for i in range(2)]
        ins += [low_w] if d == 0 else []
        outs = [pltpu.make_async_copy(normed.at[here], results[0].at[here], sem_out.at[d, 0])]
        for i, at in enumerate((2, 3)):
            outs.append(
                pltpu.make_async_copy(held[at].at[:, here], results[at].at[:, here], sem_out.at[d, i + 1])
            )
        steps.append((ins, compute, outs))

    def turn():
        turned = dot_nt(wt[...], normed[...]) + bias_col[...]
        row = lax.broadcasted_iota(jnp.int32, (HD, padded), 0)
        query_tail = jnp.where(row == 0, 1.0, 0.0).astype(BF16)
        for h in range(LOCAL_HEADS):
            at = h * HD
            qa[h, :HD, :total] = (turned[at : at + HD] * HD ** (-0.5)).astype(BF16)
            qa[h, :HD, total:] = jnp.zeros((HD, padded - total), BF16)
            qa[h, HD:, :] = query_tail
            kt[h] = turned[WIDTH + at : WIDTH + at + HD].astype(BF16)
            vt[h] = turned[2 * WIDTH + at : 2 * WIDTH + at + HD].astype(BF16)

    outs = [
        pltpu.make_async_copy(held[at], results[at], sem_out.at[MEMBERS, i])
        for i, at in enumerate((1, 4, 5))
    ]
    steps.append(([], turn, outs))
    streamed(steps)


def prepare_kernel(w, bias, turned, bias_col):
    turned[...] = w[...].T
    bias_col[...] = jnp.broadcast_to(bias[...][None], (8, bias.shape[0])).T[:, :1]


def prepare(w, bias):
    model, width = w.shape
    outs = [jax.ShapeDtypeStruct((width, model), BF16), jax.ShapeDtypeStruct((width, 1), F32)]
    return in_vmem(prepare_kernel, outs, w, bias, name="prepare")


def project(x_blocks, rows, gain, shift, w, wt, bias, bias_col):
    model = x_blocks[0].shape[1]
    total = MEMBERS * rows
    padded = -(-total // TILE) * TILE
    n = LOCAL_HEADS
    outs = [
        jax.ShapeDtypeStruct((total, model), BF16),
        jax.ShapeDtypeStruct((n, 2 * HD, padded), BF16),
        jax.ShapeDtypeStruct((n, total, 2 * HD), BF16),
        jax.ShapeDtypeStruct((n, total, 2 * HD), BF16),
        jax.ShapeDtypeStruct((n, HD, total), BF16),
        jax.ShapeDtypeStruct((n, HD, total), BF16),
    ]
    anywhere, near = pl.BlockSpec(memory_space=pl.ANY), pl.BlockSpec(memory_space=VMEM)
    return pl.pallas_call(
        project_kernel,
        out_shape=outs,
        in_specs=[anywhere] * 8 + [near] * 2 + [anywhere] + [near] * 3,
        out_specs=[anywhere] * len(outs),
        scratch_shapes=[VMEM(o.shape, o.dtype) for o in outs]
        + [
            VMEM((MEMBERS, 2, *x_blocks[0].shape), BF16),
            VMEM((1, *w.shape), BF16),
            pltpu.SemaphoreType.DMA((MEMBERS + 1, 2)),
            pltpu.SemaphoreType.DMA((MEMBERS + 1, 3)),
        ],
        compiler_params=params(),
        cost_estimate=LONG,
        name="project",
    )(*x_blocks, gain, shift, w, wt, bias, bias_col)


def forward_kernel(qa, ka, vt, l0, l1, l2, l3, turned, logs, held, even, odd, top_even, top_odd):
    head = pl.program_id(0)
    rows = ka.shape[1] // MEMBERS
    tiles = qa.shape[2] // TILE

    def scored(i, out, top):
        here = pl.ds(pl.multiple_of(i * TILE, TILE), TILE)
        scores = dot(ka[0], qa[0, :, here])
        out[...] = scores
        top[...] = jnp.max(scores, axis=0, keepdims=True)

    def mixed_of(i, scores, top):
        here = pl.ds(pl.multiple_of(i * TILE, TILE), TILE)
        peak = top[...]
        weights = jnp.exp(scores[...] - peak)
        sums = jnp.sum(weights, axis=0, keepdims=True)
        mixed = dot(vt[0], weights.astype(BF16)) * (1.0 / sums)
        turned[0, :, here] = mixed
        logs[0, :, here] = peak + jnp.log(sums)
        held[here, :] = mixed.T.astype(BF16)

    scored(0, even, top_even)

    def pair(i, carry):
        scored(2 * i + 1, odd, top_odd)
        mixed_of(2 * i, even, top_even)
        scored(jnp.minimum(2 * i + 2, tiles - 1), even, top_even)
        mixed_of(2 * i + 1, odd, top_odd)
        return carry

    lax.fori_loop(0, tiles // 2, pair, 0)
    if tiles % 2:
        mixed_of(tiles - 1, even, top_even)
    for h in range(LOCAL_HEADS):

        @pl.when(head == h)
        def _(h=h):
            for d, low in enumerate((l0, l1, l2, l3)):
                for rows_at, size, lane in packing(rows):
                    at = d * rows + rows_at
                    low[:size, lane + h * HD : lane + (h + 1) * HD] = held[at : at + size, :]


def attend(qa, ka, vt):
    n, total, _ = ka.shape
    padded = qa.shape[2]
    rows = total // MEMBERS
    per_head = lambda *shape: pl.BlockSpec((1,) + shape, lambda h: (h, 0, 0))
    *low, turned, logs = pl.pallas_call(
        forward_kernel,
        grid=(n,),
        out_shape=[jax.ShapeDtypeStruct((packed_rows(rows), 2 * WIDTH), BF16)] * MEMBERS
        + [
            jax.ShapeDtypeStruct((n, HD, padded), F32),
            jax.ShapeDtypeStruct((n, 1, padded), F32),
        ],
        in_specs=[per_head(2 * HD, padded), per_head(total, 2 * HD), per_head(HD, total)],
        out_specs=[whole(packed_rows(rows), 2 * WIDTH)] * MEMBERS + [per_head(HD, padded), per_head(1, padded)],
        scratch_shapes=[VMEM((padded, HD), BF16), VMEM((total, TILE), F32), VMEM((total, TILE), F32)]
        + [VMEM((1, TILE), F32)] * 2,
        compiler_params=params(),
        cost_estimate=LONG,
        name="attend",
    )(qa, ka, vt)
    return low, turned, logs


def three_parts(row):
    high = row.astype(BF16).astype(F32)
    rest = row - high
    middle = rest.astype(BF16).astype(F32)
    return high, middle, rest - middle


def backward_kernel(
    head, qa, ka, va, kt, turned, logs, g0, g1, g2, g3, out_q, out_k, out_v, held_g, sum_k, sum_v, s0, s1, d0, d1
):
    total = ka.shape[1]
    rows = total // MEMBERS
    padded = qa.shape[2]
    tiles = padded // TILE
    for d, part in enumerate((g0, g1, g2, g3)):
        for rows_at, size, lane in packing(rows):
            at = d * rows + rows_at
            held_g[at : at + size, :] = part[:size, lane + head * HD : lane + (head + 1) * HD]
    held_g[total:, :] = jnp.zeros((padded - total, HD), BF16)
    sum_k[...] = jnp.zeros_like(sum_k)
    sum_v[...] = jnp.zeros_like(sum_v)
    row = lax.broadcasted_iota(jnp.int32, (HD, TILE), 0)

    def scored(i, probs_out, grads_out):
        here = pl.ds(pl.multiple_of(i * TILE, TILE), TILE)
        grad_turned = held_g[here, :].astype(F32).T
        delta = jnp.sum(grad_turned * turned[0, :, here], axis=0, keepdims=True)
        high, middle, least = three_parts(-logs[0, :, here])
        tail = jnp.where(row == 0, 1.0, jnp.where(row == 1, high, jnp.where(row == 2, middle, jnp.where(row == 3, least, 0.0))))
        query = jnp.concatenate([qa[0, :HD, here], tail.astype(BF16)], axis=0)
        probs_out[...] = dot(ka[0], query)
        high, middle, least = three_parts(-delta)
        tail = jnp.where(row == 0, high, jnp.where(row == 1, middle, jnp.where(row == 2, least, 0.0)))
        grad_tail = jnp.concatenate([grad_turned, tail], axis=0).astype(BF16)
        grads_out[...] = dot(va[0], grad_tail)

    def some(i, width, probs_in, grads_in):
        here = pl.ds(pl.multiple_of(i * TILE, TILE), TILE)
        probs = jnp.exp(probs_in[...])
        grad_scores = (probs * grads_in[...]).astype(BF16)
        grad_turned = held_g[here, :].astype(F32).T.astype(BF16)
        sum_v[...] += dot_nt(grad_turned, probs.astype(BF16))
        sum_k[...] += dot_nt(qa[0, :HD, here], grad_scores)
        query_grad = dot(kt[0], grad_scores) * HD ** (-0.5)
        out_q[pl.ds(pl.multiple_of(i * TILE, TILE), width), :] = query_grad.T.astype(BF16)[:width]

    def pair(i, carry):
        scored(2 * i + 1, s1, d1)
        some(2 * i, TILE, s0, d0)
        scored(2 * i + 2, s0, d0)
        some(2 * i + 1, TILE, s1, d1)
        return carry

    least = total - (tiles - 1) * TILE
    scored(0, s0, d0)
    lax.fori_loop(0, (tiles - 1) // 2, pair, 0)
    if tiles % 2 == 0:
        scored(tiles - 1, s1, d1)
        some(tiles - 2, TILE, s0, d0)
        some(tiles - 1, least, s1, d1)
    else:
        some(tiles - 1, least, s0, d0)
    out_k[...] = sum_k[...].T.astype(BF16)
    out_v[...] = sum_v[...].T.astype(BF16)


def attend_back(head, qa, ka, va, kt, turned, logs, grads):
    n, total, _ = ka.shape
    padded = qa.shape[2]
    per_head = lambda *shape: pl.BlockSpec((1,) + shape, lambda i: (head, 0, 0))
    return pl.pallas_call(
        functools.partial(backward_kernel, head),
        grid=(1,),
        out_shape=[jax.ShapeDtypeStruct((total, HD), BF16)] * 3,
        in_specs=[
            per_head(2 * HD, padded),
            per_head(total, 2 * HD),
            per_head(total, 2 * HD),
            per_head(HD, total),
            per_head(HD, padded),
            per_head(1, padded),
        ]
        + [whole(*grads[0].shape)] * MEMBERS,
        out_specs=[whole(total, HD)] * 3,
        scratch_shapes=[
            VMEM((padded, HD), BF16),
            VMEM((HD, total), F32),
            VMEM((HD, total), F32),
        ]
        + [VMEM((total, TILE), F32)] * 4,
        compiler_params=params(),
        cost_estimate=LONG,
        name="attend_back",
    )(qa, ka, va, kt, turned, logs, *grads)


def unproject_kernel(where, *refs):
    columns, normed, w = refs[:9], refs[9], refs[10]
    n0, n1, n23, a_send, a_keep, b_send, b_keep, sums = refs[11:19]
    held, held_normed, held_n, joint, grad, sem_in, sem_out = refs[19:]
    rows = n0.shape[0]
    here = [pl.ds(d * rows, rows) for d in range(MEMBERS)]
    steps = []
    for s in range(3):
        for h in range(LOCAL_HEADS):
            at = s * WIDTH + h * HD
            slot = 3 * h + s

            def put(at=at, slot=slot):
                joint[:, at : at + HD] = held[slot]

            steps.append(([pltpu.make_async_copy(columns[slot], held.at[slot], sem_in.at[slot])], put, []))
    for d in (2, 3, 1, 0):

        def back(d=d):
            held_n[d] = dot_nt(joint[here[d], :], w[...]).astype(BF16)

        place = (n0, n1, n23.at[0], n23.at[1])[d]
        ins = [pltpu.make_async_copy(normed, held_normed, sem_in.at[9])] if d == 0 else []
        steps.append((ins, back, [pltpu.make_async_copy(held_n.at[d], place, sem_out.at[d])]))

    def weights():
        whole_grad = dot_tn(joint[...], held_normed[...])
        count, each, model = grad.shape
        for i in range(count):
            grad[i] = whole_grad[i * each : (i + 1) * each]
        pieces = count // 2
        for r in range(pieces):
            for p in range(2):
                part = grad[(r ^ where[1]) * 2 + (p ^ (where[2] // 2))].astype(BF16)
                out = (a_keep, a_send)[r % 2]
                out[r // 2, p] = part[:, : model // 2]
                out = (b_keep, b_send)[2 * r // pieces]
                out[r % (pieces // 2), p] = part[:, model // 2 :]
        total = jnp.sum(joint[...].astype(F32), axis=0, keepdims=True)
        sums[...] = jnp.zeros_like(sums)
        for m in range(MEMBERS):

            @pl.when(2 * where[0] + where[2] % 2 == m)
            def _(m=m):
                sums[0:1, m * WIDTH : (m + 1) * WIDTH] = total[:, :WIDTH]
                sums[1:2, m * WIDTH : (m + 1) * WIDTH] = total[:, 2 * WIDTH :]

    steps.append(([], weights, []))
    streamed(steps)


def unproject(where, columns, normed, w, pieces):
    total, model = normed.shape
    rows = total // MEMBERS
    width = 3 * WIDTH
    each = width // pieces // 2
    shaped = jax.ShapeDtypeStruct
    outs = [shaped((rows, model), BF16)] * 2 + [shaped((2, rows, model), BF16)]
    outs += [shaped((pieces // 2, 2, each, model // 2), BF16)] * 4 + [shaped((2, model), F32)]
    anywhere, near = pl.BlockSpec(memory_space=pl.ANY), pl.BlockSpec(memory_space=VMEM)
    return pl.pallas_call(
        unproject_kernel,
        out_shape=outs,
        in_specs=[pl.BlockSpec(memory_space=pltpu.SMEM)] + [anywhere] * 10 + [near],
        out_specs=[anywhere] * 3 + [near] * 5,
        scratch_shapes=[
            VMEM((9, total, HD), BF16),
            VMEM((total, model), BF16),
            VMEM((MEMBERS, rows, model), BF16),
            VMEM((total, width), BF16),
            VMEM((2 * pieces, each, model), F32),
            pltpu.SemaphoreType.DMA((10,)),
            pltpu.SemaphoreType.DMA((MEMBERS,)),
        ],
        compiler_params=params(),
        cost_estimate=LONG,
        name="unproject",
    )(where, *columns, normed, w)


def pre_sums_kernel(*refs):
    xs, (n0, n1, n23, out) = refs[:8], refs[8:]
    rows = n0.shape[0]
    out[...] = jnp.zeros_like(out)
    for d, given in enumerate((n0, n1, n23.at[0], n23.at[1])):
        for (at, size, _), x in zip(packing(rows), xs[2 * d : 2 * d + 2]):
            unit, _ = normalized(x[:size, :].astype(F32))
            grad = given[at : at + size, :].astype(F32)
            out[0:1, :] += jnp.sum(grad * unit, axis=0, keepdims=True)
            out[1:2, :] += jnp.sum(grad, axis=0, keepdims=True)


def close_kernel(first, last, p0, p1, gain, hidden, grad, low):
    rows = hidden.shape[0]
    unit, inverse = normalized(rows_of(first, last, rows))
    given = p0[...].astype(F32) + p1[...].astype(F32)
    scaled = given * gain[...][None]
    inner = scaled - jnp.mean(scaled, axis=-1, keepdims=True)
    inner = inner - unit * jnp.mean(scaled * unit, axis=-1, keepdims=True)
    total = hidden[...] + inverse * inner
    grad[...] = total
    low[...] = total.astype(BF16)


def close(x, parts, gain, hidden):
    rows, model = hidden.shape
    shaped = jax.ShapeDtypeStruct
    return pl.pallas_call(
        close_kernel,
        out_shape=[shaped((rows, model), F32), shaped((rows, model), BF16)],
        in_specs=[pl.BlockSpec(memory_space=VMEM)] * 6,
        out_specs=[pl.BlockSpec(memory_space=VMEM)] * 2,
        compiler_params=params(),
        cost_estimate=LONG,
        name="close",
    )(*x, *parts, gain, hidden)


def middle_kernel(
    side, first, final, a0, a1, a2, a3, wo, out_bias, gain, shift, cot, down_bias, up, up_bias, down,
    layer, down_send, down_keep, rest_send, rest_keep, grad_up_bias, grad_hidden, g0, g1, g2, g3, vectors,
    hidden, normed, grad_down, total_out, total_grad, valid,
):
    step = pl.program_id(0)
    last = pl.num_programs(0) - 1
    half = pl.num_programs(0) // 2
    rows, model = cot.shape
    pieces = down_keep.shape[0]
    each = half * model // pieces
    share = model // each

    @pl.when(step == 0)
    def _():
        valid[...] = mask_column(final, rows)
        value = rows_of(first, final, rows) + out_bias[...][None]
        cuts = packing(rows)
        value += jnp.concatenate(
            [
                sum(dot(part[:size, lane : lane + WIDTH], wo[e]) for e, part in enumerate((a0, a1, a2, a3)))
                for _, size, lane in cuts
            ]
        )
        hidden[...] = value
        unit, _ = normalized(value)
        normed[...] = (unit * gain[...][None] + shift[...][None]).astype(BF16)
        low = (valid[...] * cot[...].astype(F32)).astype(BF16)
        grad_down[...] = low
        vectors[3:4, :] = jnp.sum(low.astype(F32), axis=0, keepdims=True)
        total_out[...] = value + down_bias[...][None]
        total_grad[...] = jnp.zeros_like(total_grad)

    gate = dot(normed[...], up[...]) + up_bias[0]
    below = 0.5 * (1.0 + lax.erf(gate * (0.5**0.5)))
    active = (gate * below).astype(BF16)
    slope = below + gate * (jnp.exp(-0.5 * gate * gate) * (0.5 / jnp.pi) ** 0.5)
    low = grad_down[...]
    grad_gate = (dot_nt(low, down[...]) * slope).astype(BF16)
    total_out[...] += dot(active, down[...])
    total_grad[...] += dot_nt(grad_gate, up[...])
    grad_up_bias[0] = jnp.sum(grad_gate.astype(F32), axis=0, keepdims=True)
    of_down = dot_tn(active, low).astype(BF16)
    of_up = dot_tn(normed[...], grad_gate).astype(BF16)
    few = each // MEMBERS
    for i in range(2 * half):

        @pl.when(step == i)
        def _(i=i):
            down_held, rest_held = (down_send, rest_send) if i < half else (down_keep, rest_keep)
            for j in range(share):
                piece = ((i % half) * share + j) ^ side[1]
                for z in range(MEMBERS):
                    at = j * each + z * few
                    down_held[piece, z ^ side[2]] = of_down[at : at + few]
                    rest_held[piece, z ^ side[2], :few, :] = of_up[at : at + few]

    @pl.when(step == last)
    def _():
        unit, inverse = normalized(hidden[...])
        layer[...] = (valid[...] * total_out[...]).astype(BF16)
        grad = total_grad[...]
        vectors[0:1, :] = jnp.sum(grad * unit, axis=0, keepdims=True)
        vectors[1:2, :] = jnp.sum(grad, axis=0, keepdims=True)
        scaled = grad * gain[...][None]
        inner = scaled - jnp.mean(scaled, axis=-1, keepdims=True)
        inner = inner - unit * jnp.mean(scaled * unit, axis=-1, keepdims=True)
        grad = grad_down[...].astype(F32) + inverse * inner
        grad_hidden[...] = grad
        branch = grad.astype(BF16)
        vectors[2:3, :] = jnp.sum(branch.astype(F32), axis=0, keepdims=True)
        parts = (a0, a1, a2, a3)
        count = pieces // 2
        some = WIDTH // count // MEMBERS
        for e, given in enumerate((g0, g1, g2, g3)):
            back = dot_nt(branch, wo[e]).astype(BF16)
            given[...] = jnp.zeros_like(given)
            for at, size, lane in packing(rows):
                given[:size, lane : lane + WIDTH] = back[at : at + size]
            held = rest_keep if e < 2 else rest_send
            place = ((side[2] % 2) ^ (e & 1)) * count
            of_out = sum(
                dot_tn(parts[e][:size, lane : lane + WIDTH], branch[at : at + size])
                for at, size, lane in packing(rows)
            ).astype(BF16)
            for j in range(count):
                for z in range(MEMBERS):
                    at = (j * MEMBERS + z) * some
                    held[(place + j) ^ side[1], z ^ side[2], few:, :] = of_out[at : at + some]


def middle(where, pieces, x, attended, wo, out_bias, gain, shift, cot, down_bias, up, up_bias, down):
    rows, model = cot.shape
    blocks = up.shape[1] // model
    half = blocks // 2

    def block_of(i, side):
        return lax.rem(i, half) + half * jnp.where(i < half, 1 - side[0], side[0])

    whole_s = lambda *shape: pl.BlockSpec(shape, lambda i, side: (0,) * len(shape))
    each = half * model // pieces // MEMBERS
    held = (pieces, MEMBERS, each, model)
    rest = (pieces, MEMBERS, each + 2 * WIDTH // pieces // MEMBERS, model)
    shaped = jax.ShapeDtypeStruct
    outs = [
        (shaped((rows, model), BF16), whole_s(rows, model)),
        (shaped(held, BF16), whole_s(*held)),
        (shaped(held, BF16), whole_s(*held)),
        (shaped(rest, BF16), whole_s(*rest)),
        (shaped(rest, BF16), whole_s(*rest)),
        (shaped((blocks, 1, model), F32), pl.BlockSpec((1, 1, model), lambda i, side: (block_of(i, side), 0, 0))),
        (shaped((rows, model), F32), whole_s(rows, model)),
    ]
    outs += [(shaped(attended[0].shape, BF16), whole_s(*attended[0].shape))] * MEMBERS
    outs += [(shaped((4, model), F32), whole_s(4, model))]
    return pl.pallas_call(
        middle_kernel,
        out_shape=[o[0] for o in outs],
        grid_spec=pltpu.PrefetchScalarGridSpec(
            num_scalar_prefetch=1,
            grid=(blocks,),
            in_specs=[whole_s(*x[0].shape)] * 2
            + [whole_s(*attended[0].shape)] * MEMBERS
            + [whole_s(MEMBERS, WIDTH, model)]
            + [whole_s(model)] * 3
            + [whole_s(rows, model), whole_s(model)]
            + [
                pl.BlockSpec((model, model), lambda i, side: (0, block_of(i, side))),
                pl.BlockSpec((1, 1, model), lambda i, side: (block_of(i, side), 0, 0)),
                pl.BlockSpec((model, model), lambda i, side: (block_of(i, side), 0)),
            ],
            out_specs=[o[1] for o in outs],
            scratch_shapes=[
                VMEM((rows, model), F32),
                VMEM((rows, model), BF16),
                VMEM((rows, model), BF16),
                VMEM((rows, model), F32),
                VMEM((rows, model), F32),
                VMEM((rows, 1), F32),
            ],
        ),
        compiler_params=params(),
        cost_estimate=LONG,
        name="middle",
    )(
        where,
        *x, *attended, wo, out_bias, gain, shift, cot, down_bias,
        up, up_bias.reshape(blocks, 1, model), down,
    )


def reversed_bits(index, count):
    bits = count.bit_length() - 1
    total = 0
    for bit in range(bits):
        total = total | (((index >> bit) & 1) << (bits - 1 - bit))
    return total


def place_steps(where, other, parts, cuts, outs, held_in, held, sem_in, sem_out):
    _, pieces, _, _, lanes = parts.shape
    model = 2 * lanes
    half = where[0] ^ other
    steps = []
    for r in range(pieces):
        piece = r ^ where[1]
        ins = [
            pltpu.make_async_copy(parts.at[i, at], held_in.at[other, r, i], sem_in.at[other, r, i])
            for i, at in enumerate((reversed_bits(r, pieces), r))
        ]

        def compute(r=r):
            for z in range(MEMBERS):
                given = reversed_bits(z ^ where[2], MEMBERS)
                for i in range(2):
                    for out, (start, size) in zip(held, cuts):
                        value = held_in[other, r, i, given, start : start + size, :]
                        out[other, r, z * size : (z + 1) * size, i * lanes : (i + 1) * lanes] = value.astype(F32)

        places = []
        for out, (_, size) in zip(outs, cuts):
            rows = size * MEMBERS
            if out.shape[1] == model:
                places.append(out.at[pl.ds((half * pieces + piece) * rows, rows)])
            else:
                share = model // rows
                column = half * (out.shape[1] // model // 2) + piece // share
                places.append(
                    out.at[
                        pl.ds(lax.rem(piece, share) * rows, rows),
                        pl.ds(pl.multiple_of(column * model, model), model),
                    ]
                )
        sends = [
            pltpu.make_async_copy(given.at[other, r], place, sem_out.at[other, r, i])
            for i, (given, place) in enumerate(zip(held, places))
        ]
        steps.append((ins, compute, sends))
    return steps


def cuts_of(parts, shapes):
    _, pieces, _, rows, lanes = parts.shape
    sizes = [shape[0] * shape[1] // (2 * lanes) // 2 // pieces // MEMBERS for shape in shapes]
    return [(sum(sizes[:i]), size) for i, size in enumerate(sizes)]


def place_scratch(parts, cuts):
    _, pieces, _, rows, lanes = parts.shape
    scratch = [VMEM((2, pieces, 2, MEMBERS, rows, lanes), BF16)]
    scratch += [VMEM((2, pieces, MEMBERS * size, 2 * lanes), F32) for _, size in cuts]
    return scratch + [
        pltpu.SemaphoreType.DMA((2, pieces, 2)),
        pltpu.SemaphoreType.DMA((2, pieces, len(cuts))),
    ]


def place_kernel(cuts, where, own, got, *refs):
    count = len(cuts)
    outs, held_in, held, sems = refs[:count], refs[count], refs[count + 1 : -2], refs[-2:]
    streamed(
        place_steps(where, 0, own, cuts, outs, held_in, held, *sems)
        + place_steps(where, 1, got, cuts, outs, held_in, held, *sems)
    )


def placed(where, own, got, shapes):
    cuts = cuts_of(own, shapes)
    anywhere = pl.BlockSpec(memory_space=pl.ANY)
    return pl.pallas_call(
        functools.partial(place_kernel, cuts),
        out_shape=[jax.ShapeDtypeStruct(shape, F32) for shape in shapes],
        in_specs=[pl.BlockSpec(memory_space=pltpu.SMEM)] + [anywhere] * 2,
        out_specs=[anywhere] * len(cuts),
        scratch_shapes=place_scratch(own, cuts),
        compiler_params=params(),
        cost_estimate=LONG,
        name="placed",
    )(where, own, got)


def place_in_kernel(where, own, got, out, *refs):
    vectors, (columns, out_held, sem_out) = refs[:8], refs[8:]
    _, pieces, _, _, lanes = own.shape
    model = 2 * lanes
    each = columns.shape[2]
    totals = []

    def gather(other, parts):
        total = 0.0
        for piece in range(pieces):
            for side in range(MEMBERS):
                r, z = piece ^ where[1], side ^ where[2]
                at = reversed_bits(z, MEMBERS)
                both = (parts[0, reversed_bits(r, pieces), at], parts[1, r, at])
                both = jnp.concatenate([v.astype(F32) for v in both], axis=1)
                columns[2 * other + side % 2, piece * 2 + side // 2] = both[:each]
                total = total + both[each:]
        totals.append(total)

    def turn(other, s):
        for m in range(2):
            given = columns[2 * other + m].reshape(3 * WIDTH, model)[s * WIDTH : (s + 1) * WIDTH]
            out_held[other, s, :, m * WIDTH : (m + 1) * WIDTH] = given.T

    steps = []
    for other, parts in enumerate((own, got)):
        steps.append(([], functools.partial(gather, other, parts), []))
        for s in range(3):
            at = s * model + (where[0] ^ other) * lanes
            place = out.at[:, pl.ds(pl.multiple_of(at, lanes), lanes)]
            copy = pltpu.make_async_copy(out_held.at[other, s], place, sem_out.at[other, s])
            steps.append(([], functools.partial(turn, other, s), [copy]))
    streamed(steps)
    total = totals[0] + totals[1]
    for i in range(6):
        vectors[i][...] = total[i]
    vectors[6][...] = total[6:8]
    for i in range(vectors[7].shape[0] // model):
        vectors[7][i * model : (i + 1) * model] = total[8 + i]


def placed_in(where, own, got, extra, hidden_units):
    _, pieces, _, rows, lanes = own.shape
    model = 2 * lanes
    vectors = [(model,)] * 6 + [(2, model), (hidden_units,)]
    anywhere, near = pl.BlockSpec(memory_space=pl.ANY), pl.BlockSpec(memory_space=VMEM)
    return pl.pallas_call(
        place_in_kernel,
        out_shape=[jax.ShapeDtypeStruct(shape, F32) for shape in [(model, 3 * model)] + vectors],
        in_specs=[pl.BlockSpec(memory_space=pltpu.SMEM)] + [near] * 2,
        out_specs=[anywhere] + [near] * 8,
        scratch_shapes=[
            VMEM((MEMBERS, 2 * pieces, rows - extra, model), F32),
            VMEM((2, 3, model, lanes), F32),
            pltpu.SemaphoreType.DMA((2, 3)),
        ],
        compiler_params=params(),
        cost_estimate=LONG,
        name="placed_in",
    )(where, own, got)


def plus(first, second):
    return (first.astype(F32) + second.astype(F32)).astype(BF16)


def fold_core_kernel(keep, got, a_send, a_keep, b_send, b_keep, held, held_out, sem_in, sem_out):
    pieces, _, _, lanes = keep.shape
    steps = []
    for p in range(pieces):
        ins = [
            pltpu.make_async_copy(keep.at[p], held.at[p], sem_in.at[p, 0]),
        ]

        def compute(p=p):
            total = plus(held[p], got[p])
            held_out[p, 0] = total[:, :, : lanes // 2]
            held_out[p, 1] = total[:, :, lanes // 2 :]

        first = (a_keep, a_send)[p % 2].at[p // 2]
        second = (b_keep, b_send)[2 * p // pieces].at[p % (pieces // 2)]
        outs = [
            pltpu.make_async_copy(held_out.at[p, i], place, sem_out.at[p, i])
            for i, place in enumerate((first, second))
        ]
        steps.append((ins, compute, outs))
    streamed(steps)


def fold_core(keep, got):
    pieces, quarters, rows, lanes = keep.shape
    half = (quarters, rows, lanes // 2)
    return pl.pallas_call(
        fold_core_kernel,
        out_shape=[jax.ShapeDtypeStruct((pieces // 2, *half), BF16)] * 4,
        in_specs=[pl.BlockSpec(memory_space=HBM), pl.BlockSpec(memory_space=VMEM)],
        out_specs=[pl.BlockSpec(memory_space=HBM)] * 4,
        scratch_shapes=[
            VMEM(keep.shape, BF16),
            VMEM((pieces, 2, *half), BF16),
            pltpu.SemaphoreType.DMA((pieces, 2)),
            pltpu.SemaphoreType.DMA((pieces, 2)),
        ],
        compiler_params=params(),
        cost_estimate=QUICK,
        name="fold_core",
    )(keep, got)


def fold_core_quarters_kernel(keep, got, send, kept, held, held_got, held_out, sem_in, sem_out):
    pieces, quarters = keep.shape[:2]
    steps = []
    for p in range(pieces):
        ins = [
            pltpu.make_async_copy(keep.at[p], held.at[p], sem_in.at[p, 0]),
            pltpu.make_async_copy(got.at[p], held_got.at[p], sem_in.at[p, 1]),
        ]

        def compute(p=p):
            for z in range(quarters):
                held_out[p, z % 2, z // 2] = plus(held[p, z], held_got[p, z])

        outs = [
            pltpu.make_async_copy(held_out.at[p, i], place.at[p], sem_out.at[p, i])
            for i, place in enumerate((kept, send))
        ]
        steps.append((ins, compute, outs))
    streamed(steps)


def fold_core_quarters(keep, got):
    pieces, quarters, rows, lanes = keep.shape
    half = (quarters // 2, rows, lanes)
    return pl.pallas_call(
        fold_core_quarters_kernel,
        out_shape=[jax.ShapeDtypeStruct((pieces, *half), BF16)] * 2,
        in_specs=[pl.BlockSpec(memory_space=pl.ANY)] * 2,
        out_specs=[pl.BlockSpec(memory_space=pl.ANY)] * 2,
        scratch_shapes=[
            VMEM(keep.shape, BF16),
            VMEM(keep.shape, BF16),
            VMEM((pieces, 2, *half), BF16),
            pltpu.SemaphoreType.DMA((pieces, 2)),
            pltpu.SemaphoreType.DMA((pieces, 2)),
        ],
        compiler_params=params(),
        cost_estimate=QUICK,
        name="fold_core_quarters",
    )(keep, got)


def fold_halves_kernel(keep, got, send, kept):
    for p in range(keep.shape[0]):
        kept[p] = plus(keep[p, 0], got[p, 0])
        send[p] = plus(keep[p, 1], got[p, 1])


def fold_halves(keep, got):
    pieces, _, rows, lanes = keep.shape
    outs = [jax.ShapeDtypeStruct((pieces, rows, lanes), BF16)] * 2
    return in_vmem(fold_halves_kernel, outs, keep, got, name="fold_halves")


def fold_pieces_kernel(keep, got, a_send, a_keep, b_send, b_keep):
    pieces, _, model = keep.shape
    for r in range(pieces):
        total = plus(keep[r], got[r])
        out = (a_keep, a_send)[r % 2]
        out[r // 2, 0] = total[:, : model // 2]
        out = (b_keep, b_send)[2 * r // pieces]
        out[r % (pieces // 2), 0] = total[:, model // 2 :]


def fold_pieces(keep, got):
    pieces, rows, model = keep.shape
    outs = [jax.ShapeDtypeStruct((pieces // 2, 1, rows, model // 2), BF16)] * 4
    return in_vmem(fold_pieces_kernel, outs, keep, got, name="fold_pieces")


def join_planes_kernel(ak, ag, bk, bg, out):
    count = ak.shape[0]
    for r in range(count):
        out[0, r], out[0, count + r] = ak[r], ag[r]
        out[1, r], out[1, count + r] = bk[r], bg[r]


def join_planes(ak, ag, bk, bg):
    count, *rest = ak.shape
    outs = [jax.ShapeDtypeStruct((2, 2 * count, *rest), BF16)]
    return in_vmem(join_planes_kernel, outs, ak, ag, bk, bg, name="join_planes")[0]


def fold_in_kernel(keep, got, pre, mid, biases, up_bias, out):
    rows = keep.shape[1]
    out[:rows, :] = plus(keep[0], got[0])
    vectors = [pre[...], mid[...], biases[...]] + [up_bias[i] for i in range(up_bias.shape[0])]
    count = sum(v.shape[0] for v in vectors)
    filled = vectors + [jnp.zeros((out.shape[0] - rows - count, out.shape[1]), F32)]
    out[rows:, :] = jnp.concatenate(filled).astype(BF16)


def fold_in(keep, got, vectors, extra):
    _, rows, lanes = keep.shape
    outs = [jax.ShapeDtypeStruct((rows + extra, lanes), BF16)]
    return in_vmem(fold_in_kernel, outs, keep, got, *vectors, name="fold_in")[0]


def in_vmem(kernel, outs, *values, name):
    return pl.pallas_call(
        kernel,
        out_shape=outs,
        in_specs=[pl.BlockSpec(memory_space=VMEM)] * len(values),
        out_specs=[pl.BlockSpec(memory_space=VMEM)] * len(outs),
        compiler_params=params(),
        cost_estimate=QUICK,
        name=name,
    )(*values)


def fold_planes_kernel(ak, ag, bk, bg, a_send, a_keep, b_send, b_keep):
    count = ak.shape[0]
    for r in range(count):
        out = (a_keep, a_send)[r % 2]
        out[r // 2] = plus(ak[r], ag[r])
        out = (b_keep, b_send)[2 * r // count]
        out[r % (count // 2)] = plus(bk[r], bg[r])


def fold_last_kernel(ak, ag, bk, bg, send, keep=None):
    quarters = ak.shape[1]
    lanes = ak.shape[3]
    keep = send if keep is None else keep
    for z in range(quarters):
        out = (keep, send)[z % 2]
        out[z // 2, :, :lanes] = plus(ak[0, z], ag[0, z])
        out[z // 2, :, lanes:] = plus(bk[0, z], bg[0, z])


def fold_planes(ak, ag, bk, bg):
    count, quarters, rows, lanes = ak.shape
    if count > 1:
        outs = [jax.ShapeDtypeStruct((count // 2, quarters, rows, lanes), BF16)] * 4
        return in_vmem(fold_planes_kernel, outs, ak, ag, bk, bg, name="fold_planes")
    outs = [jax.ShapeDtypeStruct((-(-quarters // 2), rows, 2 * lanes), BF16)] * min(quarters, 2)
    return in_vmem(fold_last_kernel, outs, ak, ag, bk, bg, name="fold_last")


def fold_quarters_kernel(keep, got, *outs):
    for z in range(keep.shape[0]):
        out = outs[len(outs) - 1 - z]
        out[...] = plus(keep[z], got[z])


def fold_quarters(keep, got):
    count, rows, lanes = keep.shape
    outs = [jax.ShapeDtypeStruct((rows, lanes), BF16)] * count
    return in_vmem(fold_quarters_kernel, outs, keep, got, name="fold_quarters")


def over_cube(value, bit):
    count = lax.axis_size("cube")
    return lax.ppermute(value, "cube", [(i, i ^ (1 << bit)) for i in range(count)])


def over_blk(value, bit):
    return lax.ppermute(value, "blk", [(i, i ^ (1 << bit)) for i in range(MEMBERS)])


def chosen_pairs(is_home, cube_flip, blk_flip):
    pairs = []
    for c in range(lax.axis_size("cube")):
        for b in range(MEMBERS):
            if ((c & 1) == (b >> 1)) == is_home:
                pairs.append((c * MEMBERS + b, (c ^ cube_flip) * MEMBERS + (b ^ blk_flip)))
    return pairs


def sent_between(value, is_home, cube_flip, blk_flip):
    return lax.ppermute(value, ("cube", "blk"), chosen_pairs(is_home, cube_flip, blk_flip))


def exchanged(parts):
    far = over_blk(parts[3], 0)
    near = over_blk(parts[1], 0)
    core = over_cube(parts[2], 0)
    return [parts[0], near, core, over_cube(far, 0)]


def cube_bits():
    return list(range(1, lax.axis_size("cube").bit_length() - 1))


def by_cube(bit):
    return functools.partial(over_cube, bit=bit)


def by_blk(bit):
    return functools.partial(over_blk, bit=bit)


def scattering(a_send, a_keep, b_send, b_keep):
    for low, high in zip(cube_bits(), cube_bits()[::-1]):
        a_got, b_got = yield [(a_send, by_cube(low)), (b_send, by_cube(high))]
        *folded, = fold_planes(a_keep, a_got, b_keep, b_got)
        if len(folded) <= 2:
            return folded
        a_send, a_keep, b_send, b_keep = folded


def spreading(shard):
    (got,) = yield [(shard, by_blk(1))]
    both = jnp.stack([shard, got])
    (got,) = yield [(both, by_blk(0))]
    both = jnp.concatenate([both, got])[None]
    lanes = both.shape[3] // 2
    a_part, b_part = both[..., :lanes], both[..., lanes:]
    for low, high in zip(cube_bits(), cube_bits()[::-1]):
        a_got, b_got = yield [(a_part, by_cube(high)), (b_part, by_cube(low))]
        if low == cube_bits()[-1]:
            break
        a_part, b_part = jnp.concatenate([a_part, a_got]), jnp.concatenate([b_part, b_got])
    (got,) = yield [(join_planes(a_part, a_got, b_part, b_got), by_cube(0))]
    return got


def summing(keep, send):
    (got,) = yield [(send, by_cube(0))]
    send, keep = yield from scattering(*fold_core(keep, got))
    (got,) = yield [(send, by_blk(0))]
    send, keep = fold_quarters(keep, got)
    (got,) = yield [(send, by_blk(1))]
    return (yield from spreading(plus(keep, got)))


def summing_columns(parts, vectors, extra):
    send, keep = yield from scattering(*parts)
    (got,) = yield [(send, by_blk(1))]
    return (yield from spreading(fold_in(keep, got, vectors, extra)))


def closing(own, parts, gain, grad_hidden):
    p0, p1, p23 = parts
    (got,) = yield [(p23, by_cube(0))]
    near_sum, own_sum = plus(p1, got[1]), plus(p0, got[0])
    (got,) = yield [(near_sum, by_blk(0))]
    grad_here, grad_low = close(own, [own_sum, got], gain, grad_hidden)
    (moved,) = yield [(grad_low, lambda v: sent_between(v, False, 1, 2))]
    return grad_here, moved


class Order:
    def __init__(self, token):
        self.token = token

    def __call__(self, values):
        values, self.token = lax.optimization_barrier((values, self.token))
        return values


class Running:
    def __init__(self, steps):
        self.steps = steps
        self.result = None
        self.ready = next(steps)

    def take(self, arrived):
        try:
            self.ready = self.steps.send(arrived)
        except StopIteration as stop:
            self.ready, self.result = [], stop.value

    def spread(self):
        return self.ready[0][0].ndim == 5


def send(order, *runs):
    values = order([[v for v, _ in run.ready] for run in runs])
    for run, given in zip(runs, values):
        run.values = given
        run.arrived = [move(v) for v, (_, move) in zip(given, run.ready)]


def take(order, *runs):
    arrived = order([run.arrived for run in runs])
    for run, got in zip(runs, arrived):
        run.take(got)


def take_all(order, run):
    take(order, run)
    while not run.spread():
        send(order, run)
        take(order, run)


def advance(order, *runs):
    take(order, *runs)
    ready = [run for run in runs if run.ready]
    if ready:
        send(order, *ready)


def member_columns(matrix, member, axis):
    return lax.dynamic_slice_in_dim(matrix, member * WIDTH, WIDTH, axis)


def body(
    inputs,
    cotangent,
    absent_groups,
    token_group,
    pre_gain,
    pre_shift,
    input_weight,
    input_bias,
    output_weight,
    output_bias,
    mid_gain,
    mid_shift,
    up_weight,
    up_bias,
    down_weight,
    down_bias,
):
    _, rows, model = inputs.shape
    hidden_units = up_weight.shape[1]
    cube, blk = lax.axis_index("cube"), lax.axis_index("blk")
    core = cube & 1
    pieces = lax.axis_size("cube") // 2
    where = jnp.stack([core, cube >> 1, blk]).astype(jnp.int32)
    at_home = core == (blk >> 1)
    member = 2 * core + (blk & 1)

    def moved(value):
        return jnp.where(at_home, value, sent_between(value, False, 1, 2))

    group_match = token_group[0][None, :] == jnp.arange(GROUPS, dtype=jnp.int32)[:, None]
    lacking = jnp.sum(jnp.where(group_match, absent_groups.reshape(GROUPS, 1), 0), axis=0)
    valid_here = (1 - lacking).astype(BF16)
    top = packed_rows(rows)
    mask_rows = jnp.broadcast_to(jnp.pad(valid_here, (0, model - rows)), (2 * top - rows, model))
    carried = [inputs[0, :top], jnp.concatenate([inputs[0, top:], mask_rows])]
    arriving = [sent_between(part, False, 1, 2) for part in carried]
    near_home = [sent_between(part, True, 0, 1) for part in carried]

    in_columns = jnp.concatenate(
        [member_columns(input_weight[:, s * model : (s + 1) * model], member, 1) for s in range(3)],
        axis=1,
    )
    bias_columns = member_columns(input_bias, member, 1)
    bias_columns = jnp.concatenate([bias_columns[0], jnp.zeros((WIDTH,), F32), bias_columns[1]])
    out_rows = jnp.stack([member_columns(output_weight, member ^ e, 0) for e in range(MEMBERS)])
    prepared = (in_columns, *prepare(in_columns, bias_columns), bias_columns, out_rows)
    prepared, arriving[1] = lax.optimization_barrier((prepared, arriving[1]))
    in_columns, in_columns_turned, bias_turned, bias_columns, out_rows = prepared

    own, near = [], []
    for given, moved_in, from_home in zip(carried, arriving, near_home):
        own.append(jnp.where(at_home, given, moved_in))
        near.append(jnp.where(at_home, from_home, sent_between(moved_in, False, 0, 1)))
    x_blocks = [*own, *near]
    x_blocks += [over_cube(part, 0) for part in own] + [over_cube(part, 0) for part in near]

    normed_low, qa, ka, va, kt, vt = project(
        x_blocks, rows, pre_gain, pre_shift, in_columns, in_columns_turned, bias_columns, bias_turned
    )
    qa, cot_here = lax.optimization_barrier((qa, cotangent[0]))
    cot_own = moved(cot_here)
    attended_own, turned, logs = attend(qa, ka, vt)
    attended = exchanged(attended_own)
    (
        layer_here,
        down_send,
        down_keep,
        rest_send,
        rest_keep,
        grad_up_bias,
        grad_hidden,
        *grad_attended,
        middle_vectors,
    ) = middle(
        where,
        pieces,
        own,
        attended,
        out_rows,
        output_bias,
        mid_gain,
        mid_shift,
        cot_own,
        down_bias,
        up_weight,
        up_bias,
        down_weight,
    )
    blocks = hidden_units // model
    order = Order(where)
    down, rest = Running(summing(down_keep, down_send)), Running(summing(rest_keep, rest_send))
    send(order, down)
    far, near_part = over_blk(grad_attended[3], 0), over_blk(grad_attended[1], 0)
    send(order, rest)
    advance(order, down)
    far, near_part = order((far, near_part))
    core_parts = (over_cube(grad_attended[2], 0), over_cube(far, 0))
    advance(order, rest)
    grads_here = [grad_attended[0], near_part, *order(core_parts)]
    layer_moved = sent_between(order(layer_here), False, 1, 2)
    columns = []

    def back(head):
        grads = order(grads_here)
        columns.extend(order(attend_back(head, qa, ka, va, kt, turned, logs, grads)))

    back(0)
    advance(order, down)
    back(1)
    advance(order, down)
    advance(order, rest)
    layer_out = jnp.where(at_home, layer_here, order(layer_moved))
    back(2)
    advance(order, down)
    advance(order, rest)
    p0, p1, p23, *in_parts, biases = order(
        unproject(where, order(columns), normed_low, in_columns, pieces)
    )
    vectors, extra = [], 16
    in_run = Running(summing_columns(in_parts, vectors, extra))
    closing_run = Running(closing(own, (p0, p1, p23), pre_gain, grad_hidden))
    send(order, in_run)
    send(order, closing_run)
    advance(order, down)
    advance(order, rest)
    advance(order, down)
    advance(order, in_run)
    pre_sums = in_vmem(
        pre_sums_kernel, [jax.ShapeDtypeStruct((2, model), F32)], *x_blocks, p0, p1, p23, name="pre_sums"
    )
    vectors += [*order(pre_sums), middle_vectors, biases, grad_up_bias]
    advance(order, in_run)
    advance(order, rest)
    advance(order, down)
    advance(order, in_run)
    advance(order, rest)
    advance(order, down)
    advance(order, in_run)
    advance(order, rest)
    take_all(order, down)
    advance(order, in_run)
    advance(order, closing_run)
    advance(order, rest)
    advance(order, in_run)
    send(order, down)
    advance(order, closing_run)
    take(order, down)
    take_all(order, rest)
    send(order, rest)
    (grad_down_weight,) = order(placed(order.token, down.values[0], down.result, [(hidden_units, model)]))
    take_all(order, in_run)
    send(order, in_run)
    take(order, closing_run)
    grad_here, grad_moved = closing_run.result
    input_grad = order(jnp.where(at_home, grad_here, grad_moved.astype(F32)))
    take(order, rest)
    shapes = [(model, hidden_units), (model, model)]
    grad_up_weight, grad_output_weight = order(placed(order.token, rest.values[0], rest.result, shapes))
    take(order, in_run)
    (
        grad_input_weight,
        grad_pre_gain,
        grad_pre_shift,
        grad_mid_gain,
        grad_mid_shift,
        grad_output_bias,
        grad_down_bias,
        grad_input_bias,
        grad_up_bias,
    ) = placed_in(order.token, in_run.values[0], in_run.result, extra, hidden_units)
    return (
        layer_out[None],
        input_grad[None],
        grad_pre_gain,
        grad_pre_shift,
        grad_input_weight,
        grad_input_bias,
        grad_output_weight,
        grad_output_bias,
        grad_mid_gain,
        grad_mid_shift,
        grad_up_weight,
        grad_up_bias,
        grad_down_weight,
        grad_down_bias,
    )


def solution(mesh):
    rows_spec = P("cube", "blk", None)
    return jax.shard_map(
        body,
        mesh=mesh,
        in_specs=(rows_spec, rows_spec, P("cube", None), P("cube", "blk")) + (P(),) * 12,
        out_specs=(rows_spec, rows_spec) + (P(),) * 12,
        check_vma=False,
    )
```
